32 devices in a mesh: ctx: 8 (over z, x), head: 4 (over y, core).
Axes of the slice: x: 2, y: 2, z: 4, core: 2. Of those that a mesh axis runs over, the one named last changes fastest.
Arguments:
- queries: bfloat16 [4096, 2048], P('ctx', 'head'), may hold values from -6 to 6
- keys: bfloat16 [4096, 2048], P('ctx', 'head'), may hold values from -6 to 6
- values: bfloat16 [4096, 2048], P('ctx', 'head'), may hold values from -6 to 6
- out_grad: bfloat16 [4096, 2048], P('ctx', 'head'), may hold values from -6 to 6
- inputs: bfloat16 [4096, 4096], P('ctx', 'head'), may hold values from -6 to 6
- value_weight: bfloat16 [4096, 2048], P('ctx', 'head'), may hold values from -0.125 to 0.125
Outputs:
- query_grad: bfloat16 [4096, 2048], P('ctx', 'head')
- key_grad: bfloat16 [4096, 2048], P('ctx', 'head')
- input_grad: bfloat16 [4096, 4096], P('ctx', 'head')
- weight_grad: float32 [4096, 2048], P('ctx', 'head')
The draws below stay inside these ranges and needn't reach their ends.
All inputs are finite; a program needn't handle non-finite values.
Results may differ from the reference program's by a relative error of at most 0.0049.
Values may be sent and summed in bfloat16 or wider, within the bound.
No kernel may reach another device: no remote copies, remote signals or barrier semaphores. Data moves between devices by JAX's collectives and lax.ppermute only.
A program may use at most 128 MiB of HBM per device.

```python
import math
import jax
import jax.numpy as jnp
from jax import lax

D = 4096
HEADS = 16
DH = 128
TOK_DEV = 512
TOKENS = 4096
HD = 2048


def with_spikes(entries, stream_key, source, target, shards_of, factor):
    owner, partner = [(jnp.arange(entries.shape[position]) // (entries.shape[position] // shards_of)).reshape([-1 if axis == position else 1 for axis in range(entries.ndim)]) for position in (source, target)]
    chosen = jax.random.permutation(stream_key, shards_of)[partner]
    strong = (owner == chosen) | (owner == (partner + shards_of // 2) % shards_of)
    return jnp.where(strong, factor * entries, entries)


def block_scale(own_key, dims, pieces, low, high):
    loudness = 1.0
    for axis_at, parts in pieces:
        steps = jax.random.uniform(jax.random.fold_in(jax.random.fold_in(own_key, 6), axis_at), (parts,), jnp.float32, low / len(pieces), high / len(pieces))
        loudness = loudness * jnp.repeat(jnp.exp(steps), dims[axis_at] // parts).reshape((-1,) + (1,) * (len(dims) - 1 - axis_at))
    return loudness


def bell_draw(rng, shape, width, limit, cuts=(), dtype=jnp.bfloat16):
    factor_of = block_scale(rng, shape, cuts, -0.22, 0.18) if cuts else 1.0
    drawn = jax.random.normal(rng, shape, jnp.float32) * width * factor_of
    return jnp.minimum(jnp.maximum(drawn, -limit), limit).astype(dtype)


def noise_with(rng, shape, deviation, bound, shards, heavy, dtype=jnp.bfloat16):
    values = deviation * jax.random.normal(rng, shape, jnp.float32)
    if shards:
        values = values * block_scale(rng, shape, shards, -0.22, 0.18)
    return jnp.clip(with_spikes(values, jax.random.fold_in(rng, 3), *heavy), -bound, bound).astype(dtype)


def setup_inputs(seed: int = 0) -> dict:
    splits = jax.random.split(jax.random.key(seed), 7)
    queries = bell_draw(splits[0], (TOKENS, HD), 1.0, 6.0, ((0, 8), (1, 4)))
    keys = bell_draw(splits[1], (TOKENS, HD), 1.0, 6.0, ((0, 8), (1, 4)))
    values = bell_draw(splits[2], (TOKENS, HD), 1.0, 6.0, ((0, 8), (1, 4)))
    out_grad = bell_draw(splits[3], (TOKENS, HD), 1.0, 6.0, ((0, 8), (1, 4)))
    inputs = noise_with(splits[4], (TOKENS, D), 1.0, 6.0, ((0, 8), (1, 4)), (0, 1, 8, 2.0))
    value_weight = noise_with(splits[5], (D, HD), D ** -0.5, 0.125, ((0, 8), (1, 4)), (1, 0, 8, 2.0))
    return dict(queries=queries, keys=keys, values=values, out_grad=out_grad, inputs=inputs, value_weight=value_weight)


def reference(queries, keys, values, out_grad, inputs, value_weight):
    blocks = TOKENS // TOK_DEV
    factor = 1.0 / math.sqrt(DH * TOKENS)
    highest = lax.Precision.HIGHEST

    def split(array):
        return array.astype(jnp.float32).reshape(blocks, TOK_DEV, HEADS, DH)
    query_all = split(queries)
    key_all = split(keys)
    value_all = split(values)
    grad_all = split(out_grad)
    kv_state = jnp.einsum('bthd,bthe->bhde', key_all, value_all, precision=highest)
    qg_state = jnp.einsum('bthd,bthe->bhde', query_all, grad_all, precision=highest)
    prior = jnp.cumsum(kv_state, axis=0) - kv_state
    later = jnp.cumsum(qg_state[::-1], axis=0)[::-1] - qg_state
    rows = lax.broadcasted_iota(jnp.int32, (TOK_DEV, TOK_DEV), 0)
    cols = lax.broadcasted_iota(jnp.int32, (TOK_DEV, TOK_DEV), 1)
    causal = rows >= cols

    def rounded(array):
        return lax.optimization_barrier(array.astype(jnp.bfloat16)).astype(jnp.float32)

    def one_block(item):
        query_blk, key_blk, value_blk, grad_blk, prior_blk, later_blk = item
        grad_scores = rounded(jnp.where(causal[None], jnp.einsum('the,she->hts', grad_blk, value_blk, precision=highest), 0.0))
        key_scores = rounded(jnp.where(causal[None], jnp.einsum('thd,shd->hts', query_blk, key_blk, precision=highest), 0.0))
        query_out = factor * (jnp.einsum('the,hde->thd', grad_blk, prior_blk, precision=highest) + jnp.einsum('hts,shd->thd', grad_scores, key_blk, precision=highest))
        key_out = factor * (jnp.einsum('hts,thd->shd', grad_scores, query_blk, precision=highest) + jnp.einsum('she,hde->shd', value_blk, later_blk, precision=highest))
        value_out = factor * (jnp.einsum('hts,the->she', key_scores, grad_blk, precision=highest) + jnp.einsum('shd,hde->she', key_blk, later_blk, precision=highest))
        return (query_out.astype(jnp.bfloat16), key_out.astype(jnp.bfloat16), value_out.astype(jnp.bfloat16))
    query_out, key_out, value_out = lax.map(one_block, (query_all, key_all, value_all, grad_all, prior, later))
    query_grad = query_out.reshape(TOKENS, HD)
    key_grad = key_out.reshape(TOKENS, HD)
    value_grad = value_out.reshape(TOKENS, HD)
    input_grad = jnp.dot(value_grad, value_weight.T, preferred_element_type=jnp.float32).astype(jnp.bfloat16)
    weight_grad = jnp.dot(inputs.T, value_grad, preferred_element_type=jnp.float32) * (1.0 / math.sqrt(TOKENS))
    return (query_grad, key_grad, input_grad, weight_grad)
```

```python
import math

import jax
import jax.numpy as jnp
from jax import lax
from jax.sharding import PartitionSpec as P

DH = 128


def local(queries, keys, values, out_grad, inputs, value_weight):
    f32, bf16 = jnp.float32, jnp.bfloat16
    length, cols = queries.shape
    heads = cols // DH
    n_ctx, n_head = lax.axis_size("ctx"), lax.axis_size("head")
    pairs = n_ctx // 2
    ctx, head = lax.axis_index("ctx"), lax.axis_index("head")
    parity, pair = ctx % 2, ctx // 2
    factor = 1.0 / math.sqrt(DH * length * n_ctx)
    lines = [[2 * i + k for i in range(pairs)] for k in range(2)]

    def partner(x):
        return lax.ppermute(x, "ctx", [(i, i ^ 1) for i in range(n_ctx)])

    def across(x, bit):
        return lax.ppermute(x, "head", [(i, i ^ bit) for i in range(n_head)])

    def over_lines(x):
        return lax.all_gather(x, "ctx", axis_index_groups=lines)

    weight = lax.all_gather(
        value_weight, "ctx", axis=0, tiled=True, axis_index_groups=lines
    )

    query_heads = queries.reshape(length, heads, DH)
    key_heads = keys.reshape(length, heads, DH)
    value_heads = values.reshape(length, heads, DH)
    grad_heads = out_grad.reshape(length, heads, DH)

    def outside(state, reverse):
        mine = state.astype(bf16)
        theirs = partner(mine)
        both = (mine.astype(f32) + theirs.astype(f32)).astype(bf16)
        every = over_lines(both)
        at = lax.broadcasted_iota(jnp.int32, (pairs, 1, 1, 1), 0)
        reached = at > pair if reverse else at < pair
        total = jnp.sum(jnp.where(reached, every.astype(f32), 0.0), axis=0)
        near = parity == (0 if reverse else 1)
        return total + jnp.where(near, theirs.astype(f32), 0.0)

    qg = jnp.einsum("thd,the->hde", query_heads, grad_heads, preferred_element_type=f32)
    later = outside(qg, True)
    kv = jnp.einsum("thd,the->hde", key_heads, value_heads, preferred_element_type=f32)
    prior = outside(kv, False)

    per = n_ctx // n_head // 2
    width = inputs.shape[1] // (2 * per)
    block = per * width
    split = inputs.reshape(length, per, 2, width)
    even, odd = (split[:, :, k].reshape(length, block) for k in range(2))
    own = jnp.where(parity == 0, even, odd)
    theirs = partner(jnp.where(parity == 0, odd, even))
    rows = [jnp.concatenate([own, theirs], axis=0)]
    bit = n_head // 2
    bits = []
    while bit:
        bits.append(bit)
        rows = rows + [across(r, bit) for r in rows]
        bit //= 2
    offsets = [0]
    for b in bits:
        offsets = offsets + [o ^ b for o in offsets]

    idx_r = lax.broadcasted_iota(jnp.int32, (length, length), 0)
    idx_c = lax.broadcasted_iota(jnp.int32, (length, length), 1)
    causal = (idx_r >= idx_c)[None]

    def scores(a, b):
        s = jnp.einsum("the,she->hts", a, b, preferred_element_type=f32)
        return jnp.where(causal, s, 0.0).astype(bf16)

    def inter(x, state, spec):
        hi = state.astype(bf16)
        lo = (state - hi.astype(f32)).astype(bf16)
        return jnp.einsum(spec, x, hi, preferred_element_type=f32) + jnp.einsum(
            spec, x, lo, preferred_element_type=f32
        )

    key_scores = scores(query_heads, key_heads)
    value_out = factor * (
        jnp.einsum("hts,the->she", key_scores, grad_heads, preferred_element_type=f32)
        + inter(key_heads, later, "shd,hde->she")
    )
    value_grad = value_out.astype(bf16).reshape(length, cols)
    value_both = jnp.concatenate([value_grad, partner(value_grad)], axis=0)

    grad_scores = scores(grad_heads, value_heads)
    query_out = factor * (
        inter(grad_heads, prior, "the,hde->thd")
        + jnp.einsum("hts,shd->thd", grad_scores, key_heads, preferred_element_type=f32)
    )
    key_out = factor * (
        jnp.einsum("hts,thd->shd", grad_scores, query_heads, preferred_element_type=f32)
        + inter(value_heads, later, "she,hde->shd")
    )
    query_grad = query_out.astype(bf16).reshape(length, cols)
    key_grad = key_out.astype(bf16).reshape(length, cols)

    partial = jnp.zeros((n_head * block, cols), bf16)
    for off, r in zip(offsets, rows):
        piece = lax.dot_general(
            r, value_both, (((0,), (0,)), ((), ())), preferred_element_type=f32
        )
        partial = lax.dynamic_update_slice(
            partial, piece.astype(bf16), ((head ^ off) * block, 0)
        )
    summed = lax.psum_scatter(
        partial, "ctx", scatter_dimension=0, tiled=True, axis_index_groups=lines
    )
    weight_grad = summed.astype(f32) * (1.0 / math.sqrt(length * n_ctx))

    def part(off):
        w = lax.dynamic_slice_in_dim(weight, (head ^ off) * block, block, 0)
        return lax.dot_general(
            value_both, w, (((1,), (1,)), ((), ())), preferred_element_type=f32
        )

    pieces = {off: part(off) for off in range(n_head)}
    bit = 1
    while bit < n_head:
        for off in sorted(pieces):
            if off & bit:
                got = across(pieces.pop(off).astype(bf16), bit)
                pieces[off ^ bit] = pieces[off ^ bit] + got.astype(f32)
        bit *= 2
    total = pieces[0].astype(bf16)
    mine = total[:length].reshape(length, per, width)
    other = partner(total[length:]).reshape(length, per, width)
    first = jnp.where(parity == 0, mine, other)
    second = jnp.where(parity == 0, other, mine)
    input_grad = jnp.stack([first, second], axis=2).reshape(length, 2 * block)
    return (query_grad, key_grad, input_grad, weight_grad)


def solution(mesh):
    spec = P("ctx", "head")
    return jax.shard_map(
        local, mesh=mesh, in_specs=(spec,) * 6, out_specs=(spec,) * 4, check_vma=False
    )
```

```python
import math

import jax
import jax.numpy as jnp
from jax import lax
from jax.sharding import PartitionSpec as P

DH = 128


def local(queries, keys, values, out_grad, inputs, value_weight):
    f32, bf16 = jnp.float32, jnp.bfloat16
    length, cols = queries.shape
    heads = cols // DH
    n_ctx, n_head = lax.axis_size("ctx"), lax.axis_size("head")
    pairs = n_ctx // 2
    ctx, head = lax.axis_index("ctx"), lax.axis_index("head")
    parity, pair = ctx % 2, ctx // 2
    factor = 1.0 / math.sqrt(DH * length * n_ctx)
    lines = [[2 * i + k for i in range(pairs)] for k in range(2)]

    def partner(x):
        return lax.ppermute(x, "ctx", [(i, i ^ 1) for i in range(n_ctx)])

    def across(x, bit):
        return lax.ppermute(x, "head", [(i, i ^ bit) for i in range(n_head)])

    weight = lax.all_gather(value_weight, "ctx", axis_index_groups=lines)

    query_heads = queries.reshape(length, heads, DH)
    key_heads = keys.reshape(length, heads, DH)
    value_heads = values.reshape(length, heads, DH)
    grad_heads = out_grad.reshape(length, heads, DH)

    def state(a, b):
        s = jnp.einsum("thd,the->hde", a, b, preferred_element_type=f32).astype(bf16)
        return s.reshape(2, heads // 2, DH, DH)

    def pick(x, k):
        return jnp.where(k == 0, x[:, 0], x[:, 1])

    states = jnp.stack([state(query_heads, grad_heads), state(key_heads, value_heads)])
    their_half = partner(pick(states, 1 - parity))
    both = (pick(states, parity).astype(f32) + their_half.astype(f32)).astype(bf16)
    every = lax.all_gather(both, "ctx", axis_index_groups=lines)
    at = lax.broadcasted_iota(jnp.int32, (pairs, 1, 1, 1), 0)
    zero = jnp.zeros((), f32)
    after = jnp.sum(jnp.where(at > pair, every[:, 0].astype(f32), zero), axis=0)
    before = jnp.sum(jnp.where(at < pair, every[:, 1].astype(f32), zero), axis=0)
    far = jnp.stack([after, before]).astype(bf16)
    got = partner(jnp.stack([far, pick(states, parity)]))

    def whole(mine, theirs):
        a, b = mine.astype(f32), theirs.astype(f32)
        first = jnp.where(parity == 0, a, b)
        second = jnp.where(parity == 0, b, a)
        return jnp.concatenate([first, second], axis=0)

    near_later = jnp.where(parity == 0, whole(their_half[0], got[1, 0]), zero)
    near_prior = jnp.where(parity == 1, whole(their_half[1], got[1, 1]), zero)
    later = whole(far[0], got[0, 0]) + near_later
    prior = whole(far[1], got[0, 1]) + near_prior

    per = n_ctx // n_head // 2
    width = inputs.shape[1] // (2 * per)
    split = inputs.reshape(length, per, 2, width).transpose(1, 2, 0, 3)
    own = jnp.where(parity == 0, split[:, 0], split[:, 1])
    theirs = partner(jnp.where(parity == 0, split[:, 1], split[:, 0]))
    rows = [jnp.concatenate([own, theirs], axis=1)]
    offsets = [0]
    bit = n_head // 2
    while bit:
        rows = rows + [across(r, bit) for r in rows]
        offsets = offsets + [o ^ bit for o in offsets]
        bit //= 2
    features = jnp.zeros((pairs, 2 * length, width), bf16)
    for off, r in zip(offsets, rows):
        features = lax.dynamic_update_slice(features, r, ((head ^ off) * per, 0, 0))

    idx_r = lax.broadcasted_iota(jnp.int32, (length, length), 0)
    idx_c = lax.broadcasted_iota(jnp.int32, (length, length), 1)
    causal = (idx_r >= idx_c)[None]

    def scores(a, b):
        s = jnp.einsum("the,she->hts", a, b, preferred_element_type=f32)
        return jnp.where(causal, s, 0.0).astype(bf16)

    def inter(x, state, spec):
        hi = state.astype(bf16)
        lo = (state - hi.astype(f32)).astype(bf16)
        return jnp.einsum(spec, x, hi, preferred_element_type=f32) + jnp.einsum(
            spec, x, lo, preferred_element_type=f32
        )

    key_scores = scores(query_heads, key_heads)
    value_out = factor * (
        jnp.einsum("hts,the->she", key_scores, grad_heads, preferred_element_type=f32)
        + inter(key_heads, later, "shd,hde->she")
    )
    value_grad = value_out.astype(bf16).reshape(length, cols)
    value_both = jnp.concatenate([value_grad, partner(value_grad)], axis=0)

    grad_scores = scores(grad_heads, value_heads)
    query_out = factor * (
        inter(grad_heads, prior, "the,hde->thd")
        + jnp.einsum("hts,shd->thd", grad_scores, key_heads, preferred_element_type=f32)
    )
    key_out = factor * (
        jnp.einsum("hts,thd->shd", grad_scores, query_heads, preferred_element_type=f32)
        + inter(value_heads, later, "she,hde->shd")
    )
    query_grad = query_out.astype(bf16).reshape(length, cols)
    key_grad = key_out.astype(bf16).reshape(length, cols)

    order = list(range(0, pairs, 2)) + list(range(1, pairs, 2))[::-1]
    place = [order.index(i) for i in range(pairs)]
    ring = [
        (2 * order[i] + k, 2 * order[(i + 1) % pairs] + k)
        for i in range(pairs)
        for k in range(2)
    ]
    spot = jnp.asarray(place, jnp.int32)[pair]
    chains = 2
    span = cols // chains

    def piece(step, chain):
        which = jnp.asarray(order, jnp.int32)[(spot - 1 - step) % pairs]
        block = lax.dynamic_index_in_dim(features, which, 0, keepdims=False)
        return lax.dot_general(
            block,
            value_both[:, chain * span : (chain + 1) * span],
            (((0,), (0,)), ((), ())),
            preferred_element_type=f32,
        )

    sums = [piece(0, chain) for chain in range(chains)]
    for step in range(1, pairs):
        for chain in range(chains):
            moved = lax.ppermute(sums[chain].astype(bf16), "ctx", ring)
            sums[chain] = moved.astype(f32) + piece(step, chain)
    weight_grad = jnp.concatenate(sums, axis=1) * (1.0 / math.sqrt(length * n_ctx))

    def part(off, positions):
        w = lax.dynamic_slice_in_dim(weight, (head ^ off) * per, per, 0)
        return lax.dot_general(
            positions,
            w.reshape(per * width, cols),
            (((1,), (1,)), ((), ())),
            preferred_element_type=f32,
        )

    def over_heads(positions):
        pieces = {off: part(off, positions) for off in range(n_head)}
        bit = 1
        while bit < n_head:
            out = [off for off in sorted(pieces) if off & bit]
            got = across(jnp.stack([pieces.pop(o).astype(bf16) for o in out]), bit)
            for i, off in enumerate(out):
                pieces[off ^ bit] = pieces[off ^ bit] + got[i].astype(f32)
            bit *= 2
        return pieces[0].astype(bf16)

    other = partner(over_heads(value_both[length:])).reshape(length, per, width)
    mine = over_heads(value_both[:length]).reshape(length, per, width)
    first = jnp.where(parity == 0, mine, other)
    second = jnp.where(parity == 0, other, mine)
    input_grad = jnp.stack([first, second], axis=2).reshape(length, 2 * per * width)
    return (query_grad, key_grad, input_grad, weight_grad)


def solution(mesh):
    spec = P("ctx", "head")
    return jax.shard_map(
        local, mesh=mesh, in_specs=(spec,) * 6, out_specs=(spec,) * 4, check_vma=False
    )
```

```python
import functools
import math

import jax
import jax.numpy as jnp
from jax import lax
from jax.experimental import pallas as pl
from jax.experimental.pallas import tpu as pltpu
from jax.sharding import PartitionSpec as P

DH = 128
F32, BF16 = jnp.float32, jnp.bfloat16
VMEM = pl.BlockSpec(memory_space=pltpu.VMEM)
SMEM = pl.BlockSpec(memory_space=pltpu.SMEM)
ANY = pl.BlockSpec(memory_space=pl.ANY)
PARAMS = pltpu.CompilerParams(vmem_limit_bytes=48 * 2**20)


def dot(a, b, ca, cb):
    return lax.dot_general(a, b, (((ca,), (cb,)), ((), ())), preferred_element_type=F32)


def cost(flops, moved):
    return pl.CostEstimate(flops=flops, bytes_accessed=moved, transcendentals=0)


def states_kernel(par_ref, q_ref, k_ref, v_ref, g_ref, keep_ref, send_ref, near_ref):
    heads = q_ref.shape[1] // DH
    half = heads // 2
    for hd in range(heads):
        at = slice(hd * DH, (hd + 1) * DH)
        for kind, (a, b) in enumerate(((q_ref, g_ref), (k_ref, v_ref))):
            s = dot(a[:, at], b[:, at], 0, 0)
            own = par_ref[0] == hd // half

            @pl.when(own)
            def _():
                keep_ref[kind, hd % half] = s
                near_ref[kind, hd % half] = s.astype(BF16)

            @pl.when(jnp.logical_not(own))
            def _():
                send_ref[kind, hd % half] = s


def states(par, q, k, v, g):
    half = q.shape[1] // DH // 2
    shape = (2, half, DH, DH)
    return pl.pallas_call(
        states_kernel,
        in_specs=[SMEM] + [VMEM] * 4,
        out_specs=[VMEM] * 3,
        out_shape=[
            jax.ShapeDtypeStruct(shape, F32),
            jax.ShapeDtypeStruct(shape, F32),
            jax.ShapeDtypeStruct(shape, BF16),
        ],
        compiler_params=PARAMS,
        cost_estimate=cost(8 * 512 * 512 * DH, 4 * q.size * 2),
        name="states",
    )(par, q, k, v, g)


def split_kernel(per, par_ref, x_ref, _, own_ref, theirs_ref):
    width = x_ref.shape[1] // (2 * per)
    for k in range(2):
        for i in range(per):
            block = x_ref[:, (2 * i + k) * width : (2 * i + k + 1) * width]

            @pl.when(par_ref[0] == k)
            def _():
                own_ref[i] = block

            @pl.when(par_ref[0] != k)
            def _():
                theirs_ref[i] = block


def split(par, x, per, after):
    width = x.shape[1] // (2 * per)
    out = jax.ShapeDtypeStruct((per, x.shape[0], width), x.dtype)
    return pl.pallas_call(
        functools.partial(split_kernel, per),
        in_specs=[SMEM, VMEM, ANY],
        out_specs=[VMEM] * 2,
        out_shape=[out, out],
        compiler_params=PARAMS,
        cost_estimate=cost(0, x.size * 4),
        name="split",
    )(par, x, after)


def inside_kernel(q_ref, k_ref, v_ref, g_ref, _, vo_ref, qo_ref, ko_ref):
    q, k, v, g = q_ref[...], k_ref[...], v_ref[...], g_ref[...]
    n = q.shape[0]
    rows = lax.broadcasted_iota(jnp.int32, (n, n), 0)
    cols = lax.broadcasted_iota(jnp.int32, (n, n), 1)
    causal = rows >= cols
    ks = jnp.where(causal, dot(q, k, 1, 1), 0.0).astype(BF16)
    vo_ref[...] = dot(ks, g, 0, 0)
    gs = jnp.where(causal, dot(g, v, 1, 1), 0.0).astype(BF16)
    qo_ref[...] = dot(gs, k, 1, 0)
    ko_ref[...] = dot(gs, q, 0, 0)


def inside(q, k, v, g, after):
    n, cols = q.shape
    spec = pl.BlockSpec((n, DH), lambda h: (0, h))
    out = jax.ShapeDtypeStruct((n, cols), F32)
    return pl.pallas_call(
        inside_kernel,
        grid=(cols // DH,),
        in_specs=[spec] * 4 + [ANY],
        out_specs=[spec] * 3,
        out_shape=[out] * 3,
        compiler_params=PARAMS,
        cost_estimate=cost(10 * n * n * cols, 20 * n * cols),
        name="inside",
    )(q, k, v, g, after)


def far_kernel(pair_ref, every_ref, out_ref):
    for kind in range(2):
        total = jnp.zeros(out_ref.shape[1:], F32)
        for p in range(every_ref.shape[0]):
            reached = p > pair_ref[0] if kind == 0 else p < pair_ref[0]
            total = total + jnp.where(reached, every_ref[p, kind].astype(F32), 0.0)
        out_ref[kind] = total


def far_states(pair, every):
    return pl.pallas_call(
        far_kernel,
        in_specs=[SMEM, VMEM],
        out_specs=VMEM,
        out_shape=jax.ShapeDtypeStruct(every.shape[1:], F32),
        compiler_params=PARAMS,
        cost_estimate=cost(0, every.size * 2),
        name="far",
    )(pair, every)


def entering(par, hd, half, kind, far, got_far, near, got_near):
    mine = par == hd // half
    i = hd % half
    outer = jnp.where(mine, far[kind, i], got_far[kind, i])
    close = jnp.where(mine, near[kind, i], got_near[kind, i].astype(F32))
    total = outer + jnp.where(par == kind, close, 0.0)
    hi = total.astype(BF16)
    return hi, (total - hi.astype(F32)).astype(BF16)


def value_kernel(factor, par_ref, k_ref, vi_ref, far, got_far, near, got_near, *outs):
    heads = k_ref.shape[1] // DH
    span = outs[0].shape[1] // DH
    for hd in range(heads):
        at = slice(hd * DH, (hd + 1) * DH)
        hi, lo = entering(
            par_ref[0], hd, heads // 2, 0, far, got_far, near, got_near
        )
        k = k_ref[:, at]
        total = vi_ref[:, at] + (dot(k, hi, 1, 0) + dot(k, lo, 1, 0))
        to = (hd % span) * DH
        outs[hd // span][:, to : to + DH] = (factor * total).astype(BF16)


def finish_value(factor, par, k, vi, ends, chains):
    n, cols = k.shape
    out = jax.ShapeDtypeStruct((n, cols // chains), BF16)
    return pl.pallas_call(
        functools.partial(value_kernel, factor),
        in_specs=[SMEM] + [VMEM] * 6,
        out_specs=[VMEM] * chains,
        out_shape=[out] * chains,
        compiler_params=PARAMS,
        cost_estimate=cost(4 * n * cols * DH, 8 * n * cols),
        name="finish_value",
    )(par, k, vi, *ends)


def others_kernel(
    factor, par_ref, g_ref, v_ref, qi_ref, ki_ref, far, got_far, near, got_near, *outs
):
    heads = g_ref.shape[1] // DH
    for hd in range(heads):
        at = slice(hd * DH, (hd + 1) * DH)
        for kind, x_ref, i_ref in ((1, g_ref, qi_ref), (0, v_ref, ki_ref)):
            hi, lo = entering(
                par_ref[0], hd, heads // 2, kind, far, got_far, near, got_near
            )
            x = x_ref[:, at]
            total = i_ref[:, at] + (dot(x, hi, 1, 1) + dot(x, lo, 1, 1))
            outs[1 - kind][:, at] = (factor * total).astype(BF16)


def finish_others(factor, par, g, v, qi, ki, ends):
    out = jax.ShapeDtypeStruct(g.shape, BF16)
    return pl.pallas_call(
        functools.partial(others_kernel, factor),
        in_specs=[SMEM] + [VMEM] * 8,
        out_specs=[VMEM] * 2,
        out_shape=[out] * 2,
        compiler_params=PARAMS,
        cost_estimate=cost(8 * g.size * DH, 16 * g.size),
        name="finish_others",
    )(par, g, v, qi, ki, *ends)


def piece_kernel(count, dtype, offs_ref, subs_ref, a_ref, b_ref, *refs):
    own, theirs = refs[:count], refs[count : 2 * count]
    out_ref, x, y, sems = refs[2 * count :]
    step = pl.program_id(0)
    for i in range(count):

        @pl.when(offs_ref[step] == i)
        def _():
            one = pltpu.make_async_copy(own[i].at[subs_ref[step]], x, sems.at[0])
            two = pltpu.make_async_copy(theirs[i].at[subs_ref[step]], y, sems.at[1])
            one.start()
            two.start()
            one.wait()
            two.wait()

    total = dot(x[...], a_ref[...], 0, 0) + dot(y[...], b_ref[...], 0, 0)
    out_ref[0] = total.astype(dtype)


def pieces(dtype, offs, subs, a, b, own, theirs):
    steps = offs.shape[0]
    count = len(own)
    _, n, width = own[0].shape
    span = a.shape[1]
    return pl.pallas_call(
        functools.partial(piece_kernel, count, dtype),
        grid=(steps,),
        in_specs=[SMEM] * 2 + [VMEM] * 2 + [ANY] * (2 * count),
        out_specs=pl.BlockSpec((1, width, span), lambda s: (s, 0, 0)),
        out_shape=jax.ShapeDtypeStruct((steps, width, span), dtype),
        scratch_shapes=[
            pltpu.VMEM((n, width), BF16),
            pltpu.VMEM((n, width), BF16),
            pltpu.SemaphoreType.DMA((2,)),
        ],
        compiler_params=PARAMS,
        cost_estimate=cost(4 * n * width * span * steps, 4 * n * (width + span) * steps),
        name="pieces",
    )(offs, subs, a, b, *own, *theirs)


def local(queries, keys, values, out_grad, inputs, value_weight):
    length, cols = queries.shape
    n_ctx, n_head = lax.axis_size("ctx"), lax.axis_size("head")
    pairs = n_ctx // 2
    ctx, head = lax.axis_index("ctx"), lax.axis_index("head")
    parity, pair = ctx % 2, ctx // 2
    par = parity.astype(jnp.int32).reshape(1)
    factor = 1.0 / math.sqrt(DH * length * n_ctx)
    lines = [[2 * i + k for i in range(pairs)] for k in range(2)]
    chains = 2
    span = cols // chains

    def partner(x):
        return lax.ppermute(x, "ctx", [(i, i ^ 1) for i in range(n_ctx)])

    def across(x, bit):
        return lax.ppermute(x, "head", [(i, i ^ bit) for i in range(n_head)])

    part_rows = value_weight.shape[0] // 2
    weights = [
        lax.all_gather(
            value_weight[i * part_rows : (i + 1) * part_rows],
            "ctx",
            axis_index_groups=lines,
        )
        for i in range(2)
    ]

    keep, send, near16 = states(par, queries, keys, values, out_grad)
    their_half = partner(send)
    got_near = partner(near16)
    both = (keep + their_half).astype(BF16)

    per = n_ctx // n_head // 2
    own, theirs = split(par, inputs, per, send)
    own, theirs = [own], [partner(theirs)]
    offsets = [0]
    bit = n_head // 2
    while bit:
        own = own + [across(r, bit) for r in own]
        theirs = theirs + [across(r, bit) for r in theirs]
        offsets = offsets + [o ^ bit for o in offsets]
        bit //= 2
    own = [own[offsets.index(i)] for i in range(n_head)]
    theirs = [theirs[offsets.index(i)] for i in range(n_head)]

    vi, qi, ki = inside(queries, keys, values, out_grad, send)

    every = lax.all_gather(both, "ctx", axis_index_groups=lines)
    far = far_states(pair.astype(jnp.int32).reshape(1), every)
    ends = (far, partner(far), their_half, got_near)

    value_mine = finish_value(factor, par, keys, vi, ends, chains)
    value_theirs = [partner(x) for x in value_mine]
    query_grad, key_grad = finish_others(factor, par, out_grad, values, qi, ki, ends)

    order = list(range(0, pairs, 2)) + list(range(1, pairs, 2))[::-1]
    place = [order.index(i) for i in range(pairs)]
    ring = [
        (2 * order[i] + k, 2 * order[(i + 1) % pairs] + k)
        for i in range(pairs)
        for k in range(2)
    ]
    spot = jnp.asarray(place, jnp.int32)[pair]
    which = jnp.asarray(order, jnp.int32)[
        (spot - 1 - jnp.arange(pairs, dtype=jnp.int32)) % pairs
    ]
    offs, subs = (which // per) ^ head, which % per

    sums, rest = [], []
    for a, b in zip(value_mine, value_theirs):
        sums.append(pieces(BF16, offs[:1], subs[:1], a, b, own, theirs)[0])
        rest.append(pieces(F32, offs[1:], subs[1:], a, b, own, theirs))
    for step in range(1, pairs):
        for i in range(chains):
            moved = lax.ppermute(sums[i].astype(BF16), "ctx", ring)
            sums[i] = moved.astype(F32) + rest[i][step - 1]
    weight_grad = jnp.concatenate(sums, axis=1) * (1.0 / math.sqrt(length * n_ctx))

    value_both = jnp.concatenate(
        [jnp.concatenate(x, axis=1) for x in (value_theirs, value_mine)], axis=0
    )
    block = per * part_rows

    def over_heads(weight):
        found = {}
        for off in range(n_head):
            w = lax.dynamic_slice_in_dim(weight, (head ^ off) * per, per, 0)
            found[off] = dot(value_both, w.reshape(block, cols), 1, 1)
        bit = 1
        while bit < n_head:
            out = [off for off in sorted(found) if off & bit]
            got = across(jnp.stack([found.pop(o).astype(BF16) for o in out]), bit)
            for i, off in enumerate(out):
                found[off ^ bit] = found[off ^ bit] + got[i].astype(F32)
            bit *= 2
        return found[0].astype(BF16)

    mine, other = [], []
    for weight in weights:
        total = over_heads(weight)
        other.append(partner(total[:length]).reshape(length, per, part_rows))
        mine.append(total[length:].reshape(length, per, part_rows))
    mine, other = jnp.concatenate(mine, axis=2), jnp.concatenate(other, axis=2)
    first = jnp.where(parity == 0, mine, other)
    second = jnp.where(parity == 0, other, mine)
    input_grad = jnp.stack([first, second], axis=2).reshape(length, -1)
    return (query_grad, key_grad, input_grad, weight_grad)


def solution(mesh):
    spec = P("ctx", "head")
    return jax.shard_map(
        local, mesh=mesh, in_specs=(spec,) * 6, out_specs=(spec,) * 4, check_vma=False
    )
```

```python
import functools
import math

import jax
import jax.numpy as jnp
from jax import lax
from jax.experimental import pallas as pl
from jax.experimental.pallas import tpu as pltpu
from jax.sharding import PartitionSpec as P

DH = 128
F32, BF16 = jnp.float32, jnp.bfloat16
VMEM = pl.BlockSpec(memory_space=pltpu.VMEM)
SMEM = pl.BlockSpec(memory_space=pltpu.SMEM)
ANY = pl.BlockSpec(memory_space=pl.ANY)


def dot(a, b, ca, cb):
    return lax.dot_general(a, b, (((ca,), (cb,)), ((), ())), preferred_element_type=F32)


def cost(flops, moved):
    return pl.CostEstimate(flops=flops, bytes_accessed=moved, transcendentals=0)


def states_kernel(a_ref, b_ref, out_ref):
    for hd in range(a_ref.shape[1] // DH):
        at = slice(hd * DH, (hd + 1) * DH)
        out_ref[hd] = dot(a_ref[:, at], b_ref[:, at], 0, 0).astype(BF16)


def states(a, b):
    heads = a.shape[1] // DH
    return pl.pallas_call(
        states_kernel,
        in_specs=[VMEM] * 2,
        out_specs=VMEM,
        out_shape=jax.ShapeDtypeStruct((heads, DH, DH), BF16),
        cost_estimate=cost(2 * a.size * DH, 4 * a.size),
        name="states",
    )(a, b)


def split_kernel(per, par_ref, x_ref, own_ref, theirs_ref):
    width = x_ref.shape[1] // (2 * per)
    for k in range(2):
        for i in range(per):
            block = x_ref[:, (2 * i + k) * width : (2 * i + k + 1) * width]

            @pl.when(par_ref[0] == k)
            def _():
                own_ref[i] = block

            @pl.when(par_ref[0] != k)
            def _():
                theirs_ref[i] = block


def split(par, x, per):
    width = x.shape[1] // (2 * per)
    out = jax.ShapeDtypeStruct((per, x.shape[0], width), x.dtype)
    return pl.pallas_call(
        functools.partial(split_kernel, per),
        in_specs=[SMEM, VMEM],
        out_specs=[VMEM] * 2,
        out_shape=[out, out],
        cost_estimate=cost(0, x.size * 4),
        name="split",
    )(par, x)


def inside_kernel(q_ref, k_ref, v_ref, g_ref, vo_ref, qo_ref, ko_ref):
    q, k, v, g = q_ref[...], k_ref[...], v_ref[...], g_ref[...]
    n = q.shape[0]
    rows = lax.broadcasted_iota(jnp.int32, (n, n), 0)
    cols = lax.broadcasted_iota(jnp.int32, (n, n), 1)
    causal = rows >= cols
    ks = jnp.where(causal, dot(q, k, 1, 1), 0.0).astype(BF16)
    vo_ref[...] = dot(ks, g, 0, 0)
    gs = jnp.where(causal, dot(g, v, 1, 1), 0.0).astype(BF16)
    qo_ref[...] = dot(gs, k, 1, 0)
    ko_ref[...] = dot(gs, q, 0, 0)


def inside(q, k, v, g):
    n, cols = q.shape
    spec = pl.BlockSpec((n, DH), lambda h: (0, h))
    out = jax.ShapeDtypeStruct((n, cols), F32)
    return pl.pallas_call(
        inside_kernel,
        grid=(cols // DH,),
        in_specs=[spec] * 4,
        out_specs=[spec] * 3,
        out_shape=[out] * 3,
        cost_estimate=cost(10 * n * n * cols, 20 * n * cols),
        name="inside",
    )(q, k, v, g)


def far_kernel(count_ref, *refs):
    got, (out_ref, send_ref) = refs[:-2], refs[-2:]
    total = jnp.zeros(out_ref.shape, F32)
    for i, x in enumerate(got):
        total = total + jnp.where(i < count_ref[0], x[...].astype(F32), 0.0)
    out_ref[...] = total
    send_ref[...] = total.astype(BF16)


def far_states(count, got):
    shape = got[0].shape
    return pl.pallas_call(
        far_kernel,
        in_specs=[SMEM] + [VMEM] * len(got),
        out_specs=[VMEM] * 2,
        out_shape=[
            jax.ShapeDtypeStruct(shape, F32),
            jax.ShapeDtypeStruct(shape, BF16),
        ],
        cost_estimate=cost(0, got[0].size * (2 * len(got) + 6)),
        name="far",
    )(count, *got)


def entering(par, kind, hd, far, got_far, near):
    close = jnp.where(par == kind, near[hd].astype(F32), 0.0)
    total = far[hd] + got_far[hd].astype(F32) + close
    hi = total.astype(BF16)
    return hi, (total - hi.astype(F32)).astype(BF16)


def value_kernel(factor, par_ref, k_ref, vi_ref, far, got_far, near, *outs):
    heads = k_ref.shape[1] // DH
    span = outs[0].shape[1] // DH
    for hd in range(heads):
        at = slice(hd * DH, (hd + 1) * DH)
        hi, lo = entering(par_ref[0], 0, hd, far, got_far, near)
        k = k_ref[:, at]
        total = vi_ref[:, at] + (dot(k, hi, 1, 0) + dot(k, lo, 1, 0))
        to = (hd % span) * DH
        outs[hd // span][:, to : to + DH] = (factor * total).astype(BF16)


def finish_value(factor, par, k, vi, later, chains):
    n, cols = k.shape
    out = jax.ShapeDtypeStruct((n, cols // chains), BF16)
    return pl.pallas_call(
        functools.partial(value_kernel, factor),
        in_specs=[SMEM] + [VMEM] * 5,
        out_specs=[VMEM] * chains,
        out_shape=[out] * chains,
        cost_estimate=cost(4 * n * cols * DH, 8 * n * cols),
        name="finish_value",
    )(par, k, vi, *later)


def others_kernel(factor, par_ref, g_ref, v_ref, qi_ref, ki_ref, *refs):
    heads = g_ref.shape[1] // DH
    later, prior, outs = refs[:3], refs[3:6], refs[6:]
    for hd in range(heads):
        at = slice(hd * DH, (hd + 1) * DH)
        for kind, x_ref, i_ref, ends in (
            (1, g_ref, qi_ref, prior),
            (0, v_ref, ki_ref, later),
        ):
            hi, lo = entering(par_ref[0], kind, hd, *ends)
            x = x_ref[:, at]
            total = i_ref[:, at] + (dot(x, hi, 1, 1) + dot(x, lo, 1, 1))
            outs[1 - kind][:, at] = (factor * total).astype(BF16)


def finish_others(factor, par, g, v, qi, ki, later, prior):
    out = jax.ShapeDtypeStruct(g.shape, BF16)
    return pl.pallas_call(
        functools.partial(others_kernel, factor),
        in_specs=[SMEM] + [VMEM] * 10,
        out_specs=[VMEM] * 2,
        out_shape=[out] * 2,
        cost_estimate=cost(8 * g.size * DH, 16 * g.size),
        name="finish_others",
    )(par, g, v, qi, ki, *later, *prior)


def piece_kernel(count, offs_ref, subs_ref, a_ref, b_ref, *refs):
    own, theirs = refs[:count], refs[count : 2 * count]
    out_ref, x, y, at, bt, sems = refs[2 * count :]
    step = pl.program_id(0)
    for i in range(count):

        @pl.when(offs_ref[step] == i)
        def _():
            pltpu.make_async_copy(own[i].at[subs_ref[step]], x, sems.at[0]).start()
            pltpu.make_async_copy(theirs[i].at[subs_ref[step]], y, sems.at[1]).start()

    @pl.when(step == 0)
    def _():
        at[...] = a_ref[...].T
        bt[...] = b_ref[...].T

    pltpu.make_async_copy(own[0].at[0], x, sems.at[0]).wait()
    pltpu.make_async_copy(theirs[0].at[0], y, sems.at[1]).wait()
    total = dot(at[...], x[...], 1, 0) + dot(bt[...], y[...], 1, 0)
    out_ref[0] = total.astype(out_ref.dtype)


def pieces(dtype, offs, subs, a, b, own, theirs):
    steps = offs.shape[0]
    count = len(own)
    _, n, width = own[0].shape
    span = a.shape[1]
    return pl.pallas_call(
        functools.partial(piece_kernel, count),
        grid=(steps,),
        in_specs=[SMEM] * 2 + [VMEM] * 2 + [ANY] * (2 * count),
        out_specs=pl.BlockSpec((1, span, width), lambda s: (s, 0, 0)),
        out_shape=jax.ShapeDtypeStruct((steps, span, width), dtype),
        scratch_shapes=[
            pltpu.VMEM((n, width), BF16),
            pltpu.VMEM((n, width), BF16),
            pltpu.VMEM((span, n), BF16),
            pltpu.VMEM((span, n), BF16),
            pltpu.SemaphoreType.DMA((2,)),
        ],
        cost_estimate=cost(4 * n * width * span * steps, 4 * n * (width + span) * steps),
        name="pieces",
    )(offs, subs, a, b, *own, *theirs)


def weight_kernel(scale, *refs):
    chains = (len(refs) - 1) // 2
    out_ref = refs[-1]
    for i in range(chains):
        total = refs[i][...].astype(F32) + refs[chains + i][...]
        span = total.shape[0]
        out_ref[:, i * span : (i + 1) * span] = total.T * scale


def finish_weight(scale, moved, rest):
    span, width = moved[0].shape
    count = len(moved)
    return pl.pallas_call(
        functools.partial(weight_kernel, scale),
        in_specs=[VMEM] * (2 * count),
        out_specs=VMEM,
        out_shape=jax.ShapeDtypeStruct((width, count * span), F32),
        cost_estimate=cost(0, 10 * count * span * width),
        name="finish_weight",
    )(*moved, *rest)


def inputs_kernel(offs, per, chains, got, head_ref, w_ref, *refs):
    vals, refs = refs[: 2 * chains], refs[2 * chains :]
    got_ref, outs = (refs[0], refs[1:]) if got else (None, refs)
    n, span = vals[0].shape
    rows, cols = w_ref.shape[1:]
    for at, off in enumerate(offs):
        first = (head_ref[0] ^ off) * per
        w = w_ref[pl.ds(first, per)].reshape(per * rows, cols)
        for side in range(2):
            total = 0.0
            for c in range(chains):
                part = w[:, c * span : (c + 1) * span]
                total = total + dot(vals[side * chains + c][...], part, 1, 1)
            to = slice(side * n, (side + 1) * n)
            if got:
                total = total + got_ref[at, to].astype(F32)
            outs[at][to] = total.astype(outs[at].dtype)


def inputs_part(offs, dtypes, per, head, w, theirs, mine, got=None):
    chains = len(mine)
    n = mine[0].shape[0]
    block = per * w.shape[1]
    extra = [] if got is None else [got]
    return pl.pallas_call(
        functools.partial(inputs_kernel, offs, per, chains, got is not None),
        in_specs=[SMEM] + [VMEM] * (1 + 2 * chains + len(extra)),
        out_specs=[VMEM] * len(offs),
        out_shape=[jax.ShapeDtypeStruct((2 * n, block), d) for d in dtypes],
        cost_estimate=cost(4 * n * block * w.shape[2] * len(offs), 8 * w.size),
        name="inputs_part",
    )(head, w, *theirs, *mine, *extra)


def after(x, *earlier):
    return lax.optimization_barrier((x, *earlier))[0]


def local(queries, keys, values, out_grad, inputs, value_weight):
    length, cols = queries.shape
    n_ctx, n_head = lax.axis_size("ctx"), lax.axis_size("head")
    pairs = n_ctx // 2
    ctx, head = lax.axis_index("ctx"), lax.axis_index("head")
    parity, pair = ctx % 2, ctx // 2
    par = parity.astype(jnp.int32).reshape(1)
    factor = 1.0 / math.sqrt(DH * length * n_ctx)
    lines = [[2 * i + k for i in range(pairs)] for k in range(2)]
    chains = 2
    span = cols // chains

    def partner(x):
        return lax.ppermute(x, "ctx", [(i, i ^ 1) for i in range(n_ctx)])

    def across(x, bit):
        return lax.ppermute(x, "head", [(i, i ^ bit) for i in range(n_head)])

    part_rows = value_weight.shape[0] // 2
    weights = [
        lax.all_gather(
            value_weight[i * part_rows : (i + 1) * part_rows],
            "ctx",
            axis_index_groups=lines,
        )
        for i in range(2)
    ]

    per = n_ctx // n_head // 2
    own, theirs = split(par, inputs, per)

    def line_move(x, by):
        moves = [
            (i, i + 2 * by) for i in range(n_ctx) if 0 <= i + 2 * by < n_ctx
        ]
        return lax.ppermute(x, "ctx", moves)

    def far_of(x, sign):
        got = [line_move(x, sign * d) for d in range(1, pairs)]
        count = pairs - 1 - pair if sign < 0 else pair
        return far_states(count.astype(jnp.int32).reshape(1), got)

    qg = states(queries, out_grad)
    far_qg, send_qg = far_of(qg, -1)
    kv = states(keys, values)
    near = partner(jnp.stack([qg, kv]))
    theirs = partner(theirs)
    later = (far_qg, partner(send_qg), near[0])

    own, theirs = [own], [theirs]
    offsets = [0]
    bit = n_head // 2
    while bit:
        own = own + [across(r, bit) for r in own]
        theirs = theirs + [across(r, bit) for r in theirs]
        offsets = offsets + [o ^ bit for o in offsets]
        bit //= 2
    own = [own[offsets.index(i)] for i in range(n_head)]
    theirs = [theirs[offsets.index(i)] for i in range(n_head)]

    vi, qi, ki = inside(queries, keys, values, out_grad)
    mine = finish_value(factor, par, keys, vi, later, chains)
    other = []
    for x in mine:
        other.append(partner(after(x, *other)))
    far_kv, send_kv = far_of(after(kv, far_qg), 1)
    prior = (far_kv, partner(after(send_kv, *other)), near[1])

    order = list(range(0, pairs, 2)) + list(range(1, pairs, 2))[::-1]
    place = [order.index(i) for i in range(pairs)]
    ring = [
        (2 * order[i] + k, 2 * order[(i + 1) % pairs] + k)
        for i in range(pairs)
        for k in range(2)
    ]
    spot = jnp.asarray(place, jnp.int32)[pair]
    which = jnp.asarray(order, jnp.int32)[
        (spot - 1 - jnp.arange(pairs, dtype=jnp.int32)) % pairs
    ]
    offs, subs = (which // per) ^ head, which % per

    sums = []
    for a, b in zip(mine, other):
        sums.append(pieces(BF16, offs[:1], subs[:1], a, b, own, theirs)[0])
    token = sums[-1]
    rest = []
    for a, b in zip(mine, other):
        rest.append(
            pieces(F32, offs[1:], subs[1:], after(a, token), b, own, theirs)
        )
        token = rest[-1]

    hd = head.astype(jnp.int32).reshape(1)
    odd = [o for o in range(n_head) if o & 1]
    even = [o for o in range(n_head) if not o & 1]
    state = [{} for _ in weights]

    def first_part(i, token):
        vals = (after(other[0], token), *other[1:])
        out = inputs_part(odd, [BF16] * len(odd), per, hd, weights[i], vals, mine)
        state[i]["got"] = across(jnp.stack(out), 1)
        return out[0]

    def second_part(i, token):
        vals = (after(other[0], token), *other[1:])
        kinds = [BF16 if o & 2 else F32 for o in even]
        out = inputs_part(
            even, kinds, per, hd, weights[i], vals, mine, state[i]["got"]
        )
        state[i]["found"] = found = dict(zip(even, out))
        if n_head > 2:
            gone = [o for o in even if o & 2]
            state[i]["got"] = across(jnp.stack([found.pop(o) for o in gone]), 2)
        return out[0]

    def third_part(i, token):
        found, bit = state[i]["found"], 2
        while bit < n_head:
            for j, o in enumerate(sorted(found)):
                moved = after(state[i]["got"][j], token).astype(F32)
                found[o] = found[o] + moved
            bit *= 2
            if bit < n_head:
                gone = [o for o in sorted(found) if o & bit]
                moved = jnp.stack([found.pop(o).astype(BF16) for o in gone])
                state[i]["got"] = across(moved, bit)
        total = found[0].astype(BF16)
        state[i]["mine"] = total[length:]
        state[i]["other"] = partner(total[:length])
        return total

    moved = [None] * chains

    def ring_step(step, i, token):
        moved[i] = lax.ppermute(sums[i], "ctx", ring)
        if step < pairs - 1:
            local_part = after(rest[i], token)[step - 1]
            sums[i] = (moved[i].astype(F32) + local_part).astype(BF16)
            return sums[i]
        return token

    plan = [
        lambda t: first_part(0, t),
        lambda t: ring_step(1, 0, t),
        lambda t: second_part(0, t),
        lambda t: ring_step(1, 1, t),
        lambda t: first_part(1, t),
        lambda t: ring_step(2, 0, t),
        lambda t: second_part(1, t),
        lambda t: ring_step(2, 1, t),
    ]
    for act in plan:
        token = act(token)
    token = third_part(0, token)
    query_grad, key_grad = finish_others(
        factor, par, after(out_grad, token), values, qi, ki, later, prior
    )
    for step in range(3, pairs):
        for i in range(chains):
            token = ring_step(step, i, token)
    weight_grad = finish_weight(
        1.0 / math.sqrt(length * n_ctx), moved, [r[-1] for r in rest]
    )
    third_part(1, token)

    mine, other = (
        jnp.concatenate(
            [s[k].reshape(length, per, part_rows) for s in state], axis=2
        )
        for k in ("mine", "other")
    )
    first = jnp.where(parity == 0, mine, other)
    second = jnp.where(parity == 0, other, mine)
    input_grad = jnp.stack([first, second], axis=2).reshape(length, -1)
    return (query_grad, key_grad, input_grad, weight_grad)


def solution(mesh):
    spec = P("ctx", "head")
    return jax.shard_map(
        local, mesh=mesh, in_specs=(spec,) * 6, out_specs=(spec,) * 4, check_vma=False
    )
```

```python
import functools
import math

import jax
import jax.numpy as jnp
from jax import lax
from jax.experimental import pallas as pl
from jax.experimental.pallas import tpu as pltpu
from jax.sharding import PartitionSpec as P

DH = 128
F32, BF16 = jnp.float32, jnp.bfloat16
VMEM = pl.BlockSpec(memory_space=pltpu.VMEM)
SMEM = pl.BlockSpec(memory_space=pltpu.SMEM)
ANY = pl.BlockSpec(memory_space=pl.ANY)


def dot(a, b, ca, cb):
    return lax.dot_general(a, b, (((ca,), (cb,)), ((), ())), preferred_element_type=F32)


def call(kernel, **kw):
    hint = pl.CostEstimate(flops=1, bytes_accessed=1, transcendentals=0)
    return pl.pallas_call(kernel, cost_estimate=hint, **kw)


def states_kernel(a_ref, b_ref, out_ref):
    for hd in range(a_ref.shape[1] // DH):
        at = slice(hd * DH, (hd + 1) * DH)
        out_ref[hd] = dot(a_ref[:, at], b_ref[:, at], 0, 0).astype(BF16)


def states(a, b):
    heads = a.shape[1] // DH
    return call(
        states_kernel,
        in_specs=[VMEM] * 2,
        out_specs=VMEM,
        out_shape=jax.ShapeDtypeStruct((heads, DH, DH), BF16),
        name="states",
    )(a, b)


def split_kernel(per, par_ref, x_ref, own_ref, theirs_ref):
    width = x_ref.shape[1] // (2 * per)
    for k in range(2):
        for i in range(per):
            block = x_ref[:, (2 * i + k) * width : (2 * i + k + 1) * width]

            @pl.when(par_ref[0] == k)
            def _():
                own_ref[i] = block

            @pl.when(par_ref[0] != k)
            def _():
                theirs_ref[i] = block


def split(par, x, per):
    width = x.shape[1] // (2 * per)
    out = jax.ShapeDtypeStruct((per, x.shape[0], width), x.dtype)
    return call(
        functools.partial(split_kernel, per),
        in_specs=[SMEM, VMEM],
        out_specs=[VMEM] * 2,
        out_shape=[out, out],
        name="split",
    )(par, x)


def inside_kernel(q_ref, k_ref, v_ref, g_ref, vo_ref, qo_ref, ko_ref):
    q, k, v, g = q_ref[...], k_ref[...], v_ref[...], g_ref[...]
    n = q.shape[0]
    rows = lax.broadcasted_iota(jnp.int32, (n, n), 0)
    cols = lax.broadcasted_iota(jnp.int32, (n, n), 1)
    causal = rows >= cols
    ks = jnp.where(causal, dot(q, k, 1, 1), 0.0).astype(BF16)
    vo_ref[...] = dot(ks, g, 0, 0)
    gs = jnp.where(causal, dot(g, v, 1, 1), 0.0).astype(BF16)
    qo_ref[...] = dot(gs, k, 1, 0)
    ko_ref[...] = dot(gs, q, 0, 0)


def inside(q, k, v, g):
    n, cols = q.shape
    spec = pl.BlockSpec((n, DH), lambda h: (0, h))
    out = jax.ShapeDtypeStruct((n, cols), F32)
    return call(
        inside_kernel,
        grid=(cols // DH,),
        in_specs=[spec] * 4,
        out_specs=[spec] * 3,
        out_shape=[out] * 3,
        name="inside",
    )(q, k, v, g)


def added(count, got, hd):
    total = jnp.zeros(got[0].shape[1:], F32)
    for i, x in enumerate(got):
        total = total + jnp.where(i < count, x[hd].astype(F32), 0.0)
    return total


def far_kernel(count_ref, *refs):
    got, out_ref = refs[:-1], refs[-1]
    for hd in range(out_ref.shape[0]):
        out_ref[hd] = added(count_ref[0], got, hd).astype(BF16)


def far_states(count, got):
    return call(
        far_kernel,
        in_specs=[SMEM] + [VMEM] * len(got),
        out_specs=VMEM,
        out_shape=jax.ShapeDtypeStruct(got[0].shape, BF16),
        name="far",
    )(count, *got)


def entering(par, kind, hd, count, near, got_far, *got):
    close = jnp.where(par == kind, near[hd].astype(F32), 0.0)
    total = added(count, got, hd) + got_far[hd].astype(F32) + close
    hi = total.astype(BF16)
    return hi, (total - hi.astype(F32)).astype(BF16)


def value_kernel(factor, par_ref, count_ref, k_ref, vi_ref, *refs):
    ends, out_ref = refs[:-1], refs[-1]
    for hd in range(k_ref.shape[1] // DH):
        at = slice(hd * DH, (hd + 1) * DH)
        hi, lo = entering(par_ref[0], 0, hd, count_ref[0], *ends)
        k = k_ref[:, at]
        total = vi_ref[:, at] + (dot(k, hi, 1, 0) + dot(k, lo, 1, 0))
        out_ref[:, at] = (factor * total).astype(BF16)


def finish_value(factor, par, count, k, vi, later):
    return call(
        functools.partial(value_kernel, factor),
        in_specs=[SMEM] * 2 + [VMEM] * (2 + len(later)),
        out_specs=VMEM,
        out_shape=jax.ShapeDtypeStruct(k.shape, BF16),
        name="finish_value",
    )(par, count, k, vi, *later)


def others_kernel(factor, par_ref, counts_ref, g_ref, v_ref, qi_ref, ki_ref, *refs):
    half = (len(refs) - 2) // 2
    later, prior, outs = refs[:half], refs[half : 2 * half], refs[2 * half :]
    for hd in range(g_ref.shape[1] // DH):
        at = slice(hd * DH, (hd + 1) * DH)
        for kind, x_ref, i_ref, ends in (
            (1, g_ref, qi_ref, prior),
            (0, v_ref, ki_ref, later),
        ):
            hi, lo = entering(par_ref[0], kind, hd, counts_ref[kind], *ends)
            x = x_ref[:, at]
            total = i_ref[:, at] + (dot(x, hi, 1, 1) + dot(x, lo, 1, 1))
            outs[1 - kind][:, at] = (factor * total).astype(BF16)


def finish_others(factor, par, counts, g, v, qi, ki, later, prior):
    out = jax.ShapeDtypeStruct(g.shape, BF16)
    return call(
        functools.partial(others_kernel, factor),
        in_specs=[SMEM] * 2 + [VMEM] * (4 + len(later) + len(prior)),
        out_specs=[VMEM] * 2,
        out_shape=[out] * 2,
        name="finish_others",
    )(par, counts, g, v, qi, ki, *later, *prior)


def piece_kernel(count, offs_ref, subs_ref, a_ref, b_ref, *refs):
    own, theirs = refs[:count], refs[count : 2 * count]
    out_ref, x, y, at, bt, sems = refs[2 * count :]
    step, steps = pl.program_id(0), pl.num_programs(0)
    slot = lax.rem(step, 2)

    def fetch(k, to):
        for i in range(count):

            @pl.when(offs_ref[k] == i)
            def _():
                for j, (src, dst) in enumerate(((own, x), (theirs, y))):
                    pltpu.make_async_copy(
                        src[i].at[subs_ref[k]], dst.at[to], sems.at[j, to]
                    ).start()

    @pl.when(step == 0)
    def _():
        fetch(0, 0)

    @pl.when(step + 1 < steps)
    def _():
        fetch(step + 1, 1 - slot)

    @pl.when(step == 0)
    def _():
        at[...] = a_ref[...].T
        bt[...] = b_ref[...].T

    for j, (src, dst) in enumerate(((own, x), (theirs, y))):
        pltpu.make_async_copy(src[0].at[0], dst.at[slot], sems.at[j, slot]).wait()
    total = dot(at[...], x[slot], 1, 0) + dot(bt[...], y[slot], 1, 0)
    out_ref[0] = total.astype(out_ref.dtype)


def pieces(offs, subs, a, b, own, theirs):
    steps = offs.shape[0]
    count = len(own)
    _, n, width = own[0].shape
    cols = a.shape[1]
    return call(
        functools.partial(piece_kernel, count),
        grid=(steps,),
        in_specs=[SMEM] * 2 + [VMEM] * 2 + [ANY] * (2 * count),
        out_specs=pl.BlockSpec((1, cols, width), lambda s: (s, 0, 0)),
        out_shape=jax.ShapeDtypeStruct((steps, cols, width), BF16),
        scratch_shapes=[
            pltpu.VMEM((2, n, width), BF16),
            pltpu.VMEM((2, n, width), BF16),
            pltpu.VMEM((cols, n), BF16),
            pltpu.VMEM((cols, n), BF16),
            pltpu.SemaphoreType.DMA((2, 2)),
        ],
        name="pieces",
    )(offs, subs, a, b, *own, *theirs)


def weight_kernel(scale, x_ref, out_ref):
    out_ref[...] = x_ref[...].astype(F32).T * scale


def finish_weight(scale, x):
    return call(
        functools.partial(weight_kernel, scale),
        in_specs=[VMEM],
        out_specs=VMEM,
        out_shape=jax.ShapeDtypeStruct(x.shape[::-1], F32),
        name="finish_weight",
    )(x)


def odd_kernel(at_ref, w_ref, theirs_ref, mine_ref, out_ref):
    n = mine_ref.shape[0]
    w = w_ref[...].reshape(-1, w_ref.shape[2])
    out_ref[0, :n] = dot(theirs_ref[...], w, 1, 1).astype(BF16)
    out_ref[0, n:] = dot(mine_ref[...], w, 1, 1).astype(BF16)


def odd_parts(at, per, w, theirs, mine):
    _, rows, cols = w.shape
    n = mine.shape[0]
    steps = at.shape[0]
    whole = pl.BlockSpec((n, cols), lambda s, a: (0, 0))
    return call(
        odd_kernel,
        grid_spec=pltpu.PrefetchScalarGridSpec(
            num_scalar_prefetch=1,
            grid=(steps,),
            in_specs=[
                pl.BlockSpec((per, rows, cols), lambda s, a: (a[s], 0, 0)),
                whole,
                whole,
            ],
            out_specs=pl.BlockSpec((1, 2 * n, per * rows), lambda s, a: (s, 0, 0)),
        ),
        out_shape=jax.ShapeDtypeStruct((steps, 2 * n, per * rows), BF16),
        name="odd_parts",
    )(at, w, theirs, mine)


def even_kernel(go, at_ref, w_ref, theirs_ref, mine_ref, got_ref, send_ref, keep_ref):
    step = pl.program_id(0)
    n = mine_ref.shape[0]
    half = got_ref.shape[2]
    part = go[1]
    w = w_ref[...].reshape(-1, w_ref.shape[2])[part * half : (part + 1) * half]
    for side, x_ref in enumerate((theirs_ref, mine_ref)):
        to = slice(side * n, (side + 1) * n)
        total = dot(x_ref[...], w, 1, 1) + got_ref[0, to].astype(F32)

        @pl.when(step < go[0])
        def _():
            send_ref[0, to] = total.astype(BF16)

        @pl.when(step >= go[0])
        def _():
            keep_ref[0, to] = total


def even_parts(part, at, per, w, theirs, mine, got):
    _, rows, cols = w.shape
    n = mine.shape[0]
    steps = at.shape[0]
    go = steps // 2
    half = per * rows // 2
    whole = pl.BlockSpec((n, cols), lambda s, a: (0, 0))
    block = (1, 2 * n, half)
    return call(
        functools.partial(even_kernel, (go, part)),
        grid_spec=pltpu.PrefetchScalarGridSpec(
            num_scalar_prefetch=1,
            grid=(steps,),
            in_specs=[
                pl.BlockSpec((per, rows, cols), lambda s, a: (a[s], 0, 0)),
                whole,
                whole,
                pl.BlockSpec(block, lambda s, a: (s, 0, part)),
            ],
            out_specs=[
                pl.BlockSpec(block, lambda s, a: (jnp.minimum(s, go - 1), 0, 0)),
                pl.BlockSpec(block, lambda s, a: (jnp.maximum(s - go, 0), 0, 0)),
            ],
        ),
        out_shape=[
            jax.ShapeDtypeStruct((go, 2 * n, half), BF16),
            jax.ShapeDtypeStruct((steps - go, 2 * n, half), F32),
        ],
        name="even_parts",
    )(at, w, theirs, mine, got)


def swap_kernel(keep_ref, got_ref, out_ref):
    out_ref[...] = (keep_ref[...] + got_ref[...].astype(F32)).astype(BF16)


def for_partner(keep, got):
    n, half = keep.shape[0] // 2, keep.shape[1]
    spec = pl.BlockSpec((n, half), lambda s: (0, 0))
    return call(
        swap_kernel,
        grid=(1,),
        in_specs=[spec] * 2,
        out_specs=spec,
        out_shape=jax.ShapeDtypeStruct((n, half), BF16),
        name="for_partner",
    )(keep, got)


def join_kernel(rows, par_ref, *refs):
    *refs, out_ref = refs
    count = len(refs) // 3
    half = refs[0].shape[1]
    for part in range(count):
        keep, got, other = refs[part], refs[count + part], refs[2 * count + part]
        mine = (keep[...] + got[...].astype(F32)).astype(BF16)
        both = (mine, other[...])
        for f in range(0, half, min(rows, half)):
            size = min(rows, half)
            block, at = divmod(part * half + f, rows)
            for k in range(2):
                for flip in range(2):

                    @pl.when(par_ref[0] == (k ^ flip))
                    def _():
                        to = (2 * block + k) * rows + at
                        out_ref[:, to : to + size] = both[flip][:, f : f + size]


def join(par, rows, keep, got, other):
    n, half = other[0].shape
    lower = pl.BlockSpec((n, half), lambda s: (1, 0))
    whole = pl.BlockSpec((n, half), lambda s: (0, 0))
    count = len(keep)
    out = (n, 2 * count * half)
    return call(
        functools.partial(join_kernel, rows),
        grid=(1,),
        in_specs=[SMEM] + [lower] * (2 * count) + [whole] * count,
        out_specs=pl.BlockSpec(out, lambda s: (0, 0)),
        out_shape=jax.ShapeDtypeStruct(out, BF16),
        name="join",
    )(par, *keep, *got, *other)


def after(x, *earlier):
    return lax.optimization_barrier((x, *earlier))[0]


def local(queries, keys, values, out_grad, inputs, value_weight):
    length, cols = queries.shape
    n_ctx, n_head = lax.axis_size("ctx"), lax.axis_size("head")
    pairs = n_ctx // 2
    ctx, head = lax.axis_index("ctx"), lax.axis_index("head")
    parity, pair = ctx % 2, ctx // 2
    par = parity.astype(jnp.int32).reshape(1)
    factor = 1.0 / math.sqrt(DH * length * n_ctx)
    lines = [[2 * i + k for i in range(pairs)] for k in range(2)]
    def partner(x):
        return lax.ppermute(x, "ctx", [(i, i ^ 1) for i in range(n_ctx)])

    def across(x, bit):
        return lax.ppermute(x, "head", [(i, i ^ bit) for i in range(n_head)])

    weight = lax.all_gather(value_weight, "ctx", axis_index_groups=lines)

    per = n_ctx // n_head // 2
    own, theirs = split(par, inputs, per)

    def line_move(x, by):
        moves = [
            (i, i + 2 * by) for i in range(n_ctx) if 0 <= i + 2 * by < n_ctx
        ]
        return lax.ppermute(x, "ctx", moves)

    def far_of(x, sign):
        got = [line_move(x, sign * d) for d in range(1, pairs)]
        count = pairs - 1 - pair if sign < 0 else pair
        count = count.astype(jnp.int32).reshape(1)
        return count, got, far_states(count, got)

    qg = states(queries, out_grad)
    count_qg, got_qg, far_qg = far_of(qg, -1)
    kv = states(keys, values)
    near = partner(jnp.stack([qg, kv]))
    theirs = partner(theirs)
    later = (near[0], partner(far_qg), *got_qg)

    own, theirs = [own], [theirs]
    offsets = [0]
    bit = n_head // 2
    while bit:
        own = own + [across(r, bit) for r in own]
        theirs = theirs + [across(r, bit) for r in theirs]
        offsets = offsets + [o ^ bit for o in offsets]
        bit //= 2
    own = [own[offsets.index(i)] for i in range(n_head)]
    theirs = [theirs[offsets.index(i)] for i in range(n_head)]

    vi, qi, ki = inside(queries, keys, values, out_grad)
    mine = finish_value(factor, par, count_qg, keys, vi, later)
    other = partner(mine)
    count_kv, got_kv, far_kv = far_of(after(kv, far_qg), 1)
    prior = (near[1], partner(after(far_kv, other)), *got_kv)

    which = jnp.arange(pairs, dtype=jnp.int32)
    found = pieces((which // per) ^ head, which % per, mine, other, own, theirs)
    summed = lax.psum_scatter(found, "ctx", axis_index_groups=lines)
    weight_grad = finish_weight(1.0 / math.sqrt(length * n_ctx), summed)

    odd = jnp.asarray([o for o in range(1, n_head, 2)][::-1], jnp.int32) ^ head
    even = jnp.asarray([o for o in range(0, n_head, 2)][::-1], jnp.int32) ^ head
    got = across(odd_parts(odd, per, weight, after(other, found), mine), 1)
    keep, back = [], []
    token = got
    for part in range(2):
        vals = after(other, token)
        send, kept = even_parts(part, even, per, weight, vals, mine, got)
        token = send
        keep.append(kept[0])
        back.append(across(send[0], 2))
    query_grad, key_grad = finish_others(
        factor,
        par,
        jnp.concatenate([count_qg, count_kv]),
        after(out_grad, token),
        values,
        qi,
        ki,
        later,
        prior,
    )
    swapped = [partner(for_partner(k, b)) for k, b in zip(keep, back)]
    input_grad = join(par, value_weight.shape[0], keep, back, swapped)
    return (query_grad, key_grad, input_grad, weight_grad)


def solution(mesh):
    spec = P("ctx", "head")
    return jax.shard_map(
        local, mesh=mesh, in_specs=(spec,) * 6, out_specs=(spec,) * 4, check_vma=False
    )
```

```python
import functools
import math

import jax
import jax.numpy as jnp
from jax import lax
from jax.experimental import pallas as pl
from jax.experimental.pallas import tpu as pltpu
from jax.sharding import PartitionSpec as P

DH = 128
F32, BF16 = jnp.float32, jnp.bfloat16
VMEM = pl.BlockSpec(memory_space=pltpu.VMEM)
SMEM = pl.BlockSpec(memory_space=pltpu.SMEM)
ANY = pl.BlockSpec(memory_space=pl.ANY)


def dot(a, b, ca, cb):
    return lax.dot_general(a, b, (((ca,), (cb,)), ((), ())), preferred_element_type=F32)


def call(kernel, **kw):
    hint = pl.CostEstimate(flops=1, bytes_accessed=1, transcendentals=0)
    params = pltpu.CompilerParams(vmem_limit_bytes=16 * 2**20)
    return pl.pallas_call(kernel, cost_estimate=hint, compiler_params=params, **kw)


def states_kernel(par_ref, q_ref, k_ref, v_ref, g_ref, keep_ref, send_ref, near_ref):
    heads = q_ref.shape[1] // DH
    half = heads // 2
    for hd in range(heads):
        at = slice(hd * DH, (hd + 1) * DH)
        for kind, (a, b) in enumerate(((q_ref, g_ref), (k_ref, v_ref))):
            s = dot(a[:, at], b[:, at], 0, 0)
            own = par_ref[0] == hd // half

            @pl.when(own)
            def _():
                keep_ref[kind, hd % half] = s
                near_ref[kind, hd % half] = s.astype(BF16)

            @pl.when(jnp.logical_not(own))
            def _():
                send_ref[kind, hd % half] = s.astype(BF16)


def states(par, q, k, v, g):
    shape = (2, q.shape[1] // DH // 2, DH, DH)
    return call(
        states_kernel,
        in_specs=[SMEM] + [VMEM] * 4,
        out_specs=[VMEM] * 3,
        out_shape=[jax.ShapeDtypeStruct(shape, d) for d in (F32, BF16, BF16)],
        name="states",
    )(par, q, k, v, g)


def split_kernel(per, par_ref, x_ref, own_ref, theirs_ref):
    width = x_ref.shape[1] // (2 * per)
    for k in range(2):
        for i in range(per):
            block = x_ref[:, (2 * i + k) * width : (2 * i + k + 1) * width]

            @pl.when(par_ref[0] == k)
            def _():
                own_ref[i] = block

            @pl.when(par_ref[0] != k)
            def _():
                theirs_ref[i] = block


def split(par, x, per):
    width = x.shape[1] // (2 * per)
    out = jax.ShapeDtypeStruct((per, x.shape[0], width), x.dtype)
    return call(
        functools.partial(split_kernel, per),
        in_specs=[SMEM, VMEM],
        out_specs=[VMEM] * 2,
        out_shape=[out, out],
        name="split",
    )(par, x)


def inside_kernel(q_ref, k_ref, g_ref, out_ref):
    n = q_ref.shape[0]
    rows = lax.broadcasted_iota(jnp.int32, (n, n), 0)
    cols = lax.broadcasted_iota(jnp.int32, (n, n), 1)
    scores = dot(q_ref[...], k_ref[...], 1, 1)
    scores = jnp.where(rows >= cols, scores, 0.0).astype(BF16)
    out_ref[...] = dot(scores, g_ref[...], 0, 0)


def inside(q, k, g):
    n, cols = q.shape
    spec = pl.BlockSpec((n, DH), lambda h: (0, h))
    return call(
        inside_kernel,
        grid=(cols // DH,),
        in_specs=[spec] * 3,
        out_specs=spec,
        out_shape=jax.ShapeDtypeStruct((n, cols), F32),
        name="inside",
    )(q, k, g)


def far_kernel(pair_ref, every_ref, out_ref, send_ref):
    for kind in range(2):
        total = jnp.zeros(out_ref.shape[1:], F32)
        for p in range(every_ref.shape[0]):
            reached = p > pair_ref[0] if kind == 0 else p < pair_ref[0]
            total = total + jnp.where(reached, every_ref[p, kind].astype(F32), 0.0)
        out_ref[kind] = total
        send_ref[kind] = total.astype(BF16)


def far_states(pair, every):
    shape = every.shape[1:]
    return call(
        far_kernel,
        in_specs=[SMEM, VMEM],
        out_specs=[VMEM] * 2,
        out_shape=[jax.ShapeDtypeStruct(shape, d) for d in (F32, BF16)],
        name="far",
    )(pair, every)


def entering(par, kind, hd, half, far, got_far, near, got_near):
    mine = par == hd // half
    i = hd % half
    outer = jnp.where(mine, far[kind, i], got_far[kind, i].astype(F32))
    close = jnp.where(mine, near[kind, i].astype(F32), got_near[kind, i].astype(F32))
    total = outer + jnp.where(par == kind, close, 0.0)
    hi = total.astype(BF16)
    return hi, (total - hi.astype(F32)).astype(BF16)


def value_kernel(factor, half, par_ref, k_ref, vi_ref, *refs):
    ends, out_ref = refs[:-1], refs[-1]
    for hd in range(2 * half):
        at = slice(hd * DH, (hd + 1) * DH)
        hi, lo = entering(par_ref[0], 0, hd, half, *ends)
        k = k_ref[:, at]
        total = vi_ref[:, at] + (dot(k, hi, 1, 0) + dot(k, lo, 1, 0))
        out_ref[:, at] = (factor * total).astype(BF16)


def finish_value(factor, par, k, vi, ends):
    return call(
        functools.partial(value_kernel, factor, k.shape[1] // DH // 2),
        in_specs=[SMEM] + [VMEM] * (2 + len(ends)),
        out_specs=VMEM,
        out_shape=jax.ShapeDtypeStruct(k.shape, BF16),
        name="finish_value",
    )(par, k, vi, *ends)


def others_kernel(factor, half, par_ref, q_ref, k_ref, v_ref, g_ref, *refs):
    ends, (qo_ref, ko_ref) = refs[:-2], refs[-2:]
    hd = pl.program_id(0)
    q, k, v, g = q_ref[...], k_ref[...], v_ref[...], g_ref[...]
    n = q.shape[0]
    rows = lax.broadcasted_iota(jnp.int32, (n, n), 0)
    cols = lax.broadcasted_iota(jnp.int32, (n, n), 1)
    scores = jnp.where(rows >= cols, dot(g, v, 1, 1), 0.0).astype(BF16)
    hi, lo = entering(par_ref[0], 1, hd, half, *ends)
    total = dot(scores, k, 1, 0) + (dot(g, hi, 1, 1) + dot(g, lo, 1, 1))
    qo_ref[...] = (factor * total).astype(BF16)
    hi, lo = entering(par_ref[0], 0, hd, half, *ends)
    total = dot(scores, q, 0, 0) + (dot(v, hi, 1, 1) + dot(v, lo, 1, 1))
    ko_ref[...] = (factor * total).astype(BF16)


def others(factor, par, q, k, v, g, ends):
    n, cols = q.shape
    spec = pl.BlockSpec((n, DH), lambda h: (0, h))
    shape = ends[0].shape
    state = pl.BlockSpec(shape, lambda h: (0, 0, 0, 0))
    out = jax.ShapeDtypeStruct(q.shape, BF16)
    return call(
        functools.partial(others_kernel, factor, cols // DH // 2),
        grid=(cols // DH,),
        in_specs=[SMEM] + [spec] * 4 + [state] * len(ends),
        out_specs=[spec] * 2,
        out_shape=[out] * 2,
        name="others",
    )(par, q, k, v, g, *ends)


def piece_kernel(count, offs_ref, subs_ref, a_ref, b_ref, *refs):
    own, theirs = refs[:count], refs[count : 2 * count]
    out_ref, x, y, at, bt, sems = refs[2 * count :]
    step, steps = pl.program_id(0), pl.num_programs(0)
    slot = lax.rem(step, 2)

    def fetch(k, to):
        for i in range(count):

            @pl.when(offs_ref[k] == i)
            def _():
                for j, (src, dst) in enumerate(((own, x), (theirs, y))):
                    pltpu.make_async_copy(
                        src[i].at[subs_ref[k]], dst.at[to], sems.at[j, to]
                    ).start()

    @pl.when(step == 0)
    def _():
        fetch(0, 0)

    @pl.when(step + 1 < steps)
    def _():
        fetch(step + 1, 1 - slot)

    @pl.when(step == 0)
    def _():
        at[...] = a_ref[...].T
        bt[...] = b_ref[...].T

    for j, (src, dst) in enumerate(((own, x), (theirs, y))):
        pltpu.make_async_copy(src[0].at[0], dst.at[slot], sems.at[j, slot]).wait()
    total = dot(at[...], x[slot], 1, 0) + dot(bt[...], y[slot], 1, 0)
    out_ref[0] = total.astype(out_ref.dtype)


def pieces(offs, subs, a, b, own, theirs):
    steps = offs.shape[0]
    count = len(own)
    _, n, width = own[0].shape
    cols = a.shape[1]
    return call(
        functools.partial(piece_kernel, count),
        grid=(steps,),
        in_specs=[SMEM] * 2 + [VMEM] * 2 + [ANY] * (2 * count),
        out_specs=pl.BlockSpec((1, cols, width), lambda s: (s, 0, 0)),
        out_shape=jax.ShapeDtypeStruct((steps, cols, width), BF16),
        scratch_shapes=[
            pltpu.VMEM((2, n, width), BF16),
            pltpu.VMEM((2, n, width), BF16),
            pltpu.VMEM((cols, n), BF16),
            pltpu.VMEM((cols, n), BF16),
            pltpu.SemaphoreType.DMA((2, 2)),
        ],
        name="pieces",
    )(offs, subs, a, b, *own, *theirs)


def weight_kernel(scale, x_ref, out_ref):
    out_ref[...] = x_ref[...].astype(F32).T * scale


def finish_weight(scale, x):
    return call(
        functools.partial(weight_kernel, scale),
        in_specs=[VMEM],
        out_specs=VMEM,
        out_shape=jax.ShapeDtypeStruct(x.shape[::-1], F32),
        name="finish_weight",
    )(x)


def block_product(per, at_ref, x_ref, y_ref, w_ref, wy_ref):
    w = w_ref[pl.ds(at_ref[0] * per, per)].reshape(-1, w_ref.shape[2])
    wy = wy_ref[at_ref[0] // 2]
    return dot(x_ref[...], w, 1, 1) + dot(y_ref[...], wy, 1, 1)


def part_kernel(per, count, at_ref, x_ref, y_ref, w_ref, wy_ref, *refs):
    total = block_product(per, at_ref, x_ref, y_ref, w_ref, wy_ref)
    for got in refs[:count]:
        total = total + got[...].astype(F32)
    refs[-1][...] = total.astype(BF16)


def head_part(at, per, x, y, w, wy, got=()):
    return call(
        functools.partial(part_kernel, per, len(got)),
        in_specs=[SMEM] + [VMEM] * (4 + len(got)),
        out_specs=VMEM,
        out_shape=jax.ShapeDtypeStruct((x.shape[0], per * w.shape[1]), BF16),
        name="head_part",
    )(at, x, y, w, wy, *got)


def join_kernel(per, count, par_ref, at_ref, x_ref, y_ref, w_ref, wy_ref, *refs):
    total = block_product(per, at_ref, x_ref, y_ref, w_ref, wy_ref)
    for got in refs[:count]:
        total = total + got[...].astype(F32)
    other_ref, out_ref = refs[count:]
    rows = w_ref.shape[1]
    both = (total.astype(BF16), other_ref[...])
    for k in range(2):

        @pl.when(par_ref[0] == k)
        def _():
            for i in range(per):
                at = slice(i * rows, (i + 1) * rows)
                for j in range(2):
                    to = (2 * i + j) * rows
                    out_ref[:, to : to + rows] = both[j ^ k][:, at]


def join(par, at, per, x, y, w, wy, got, other):
    return call(
        functools.partial(join_kernel, per, len(got)),
        in_specs=[SMEM] * 2 + [VMEM] * (5 + len(got)),
        out_specs=VMEM,
        out_shape=jax.ShapeDtypeStruct((x.shape[0], 2 * other.shape[1]), BF16),
        name="join",
    )(par, at, x, y, w, wy, *got, other)


def after(x, *earlier):
    return lax.optimization_barrier((x, *earlier))[0]


def local(queries, keys, values, out_grad, inputs, value_weight):
    length, cols = queries.shape
    n_ctx, n_head = lax.axis_size("ctx"), lax.axis_size("head")
    pairs = n_ctx // 2
    ctx, head = lax.axis_index("ctx"), lax.axis_index("head")
    parity, pair = ctx % 2, ctx // 2
    par = parity.astype(jnp.int32).reshape(1)
    factor = 1.0 / math.sqrt(DH * length * n_ctx)
    lines = [[2 * i + k for i in range(pairs)] for k in range(2)]
    def partner(x):
        return lax.ppermute(x, "ctx", [(i, i ^ 1) for i in range(n_ctx)])

    def across(x, bit):
        return lax.ppermute(x, "head", [(i, i ^ bit) for i in range(n_head)])

    weight = lax.all_gather(value_weight, "ctx", axis_index_groups=lines)

    keep, send, near16 = states(par, queries, keys, values, out_grad)
    their_half = partner(send)
    both = (keep + their_half.astype(F32)).astype(BF16)

    per = n_ctx // n_head // 2
    own, theirs = split(after(par, send), inputs, per)
    got_near = partner(after(near16, their_half))
    own, theirs = [own], [partner(after(theirs, their_half))]

    every = lax.all_gather(both, "ctx", axis_index_groups=lines)
    far, send_far = far_states(pair.astype(jnp.int32).reshape(1), every)
    ends = (far, partner(send_far), their_half, got_near)
    vi = inside(queries, after(keys, send_far), out_grad)
    mine = finish_value(factor, par, keys, vi, ends)
    other = partner(mine)

    offsets = [0]
    bit = n_head // 2
    while bit:
        own = own + [across(r, bit) for r in own]
        theirs = theirs + [across(r, bit) for r in theirs]
        offsets = offsets + [o ^ bit for o in offsets]
        bit //= 2
    own = [own[offsets.index(i)] for i in range(n_head)]
    theirs = [theirs[offsets.index(i)] for i in range(n_head)]

    query_grad, key_grad = others(
        factor, par, queries, keys, after(values, mine), out_grad, ends
    )

    which = jnp.arange(pairs, dtype=jnp.int32)
    found = pieces(
        (which // per) ^ head,
        which % per,
        after(mine, query_grad),
        other,
        own,
        theirs,
    )
    summed = lax.psum_scatter(found, "ctx", axis_index_groups=lines)
    weight_grad = finish_weight(1.0 / math.sqrt(length * n_ctx), summed)

    weight = after(weight, found)
    split_heads = weight.reshape(n_head // 2, 2, -1, cols)
    lent = across(jnp.where(head % 2 == 0, split_heads[:, 1], split_heads[:, 0]), 1)
    mine_too, other_too = across(mine, 1), across(other, 1)
    here = head.astype(jnp.int32).reshape(1)

    def summed_parts(x, y):
        return [
            across(head_part(here ^ off, per, x, y, weight, lent), off)
            for off in range(2, n_head, 2)
        ]

    got_other = summed_parts(other, other_too)
    got_mine = summed_parts(mine, mine_too)
    swapped = partner(
        head_part(here, per, other, other_too, weight, lent, got_other)
    )
    input_grad = join(
        par, here, per, mine, mine_too, weight, lent, got_mine, swapped
    )
    return (query_grad, key_grad, input_grad, weight_grad)


def solution(mesh):
    spec = P("ctx", "head")
    return jax.shard_map(
        local, mesh=mesh, in_specs=(spec,) * 6, out_specs=(spec,) * 4, check_vma=False
    )
```

```python
import functools
import math

import jax
import jax.numpy as jnp
from jax import lax
from jax.experimental import pallas as pl
from jax.experimental.pallas import tpu as pltpu
from jax.sharding import PartitionSpec as P

DH = 128
F32, BF16 = jnp.float32, jnp.bfloat16
VMEM = pl.BlockSpec(memory_space=pltpu.VMEM)
SMEM = pl.BlockSpec(memory_space=pltpu.SMEM)
ANY = pl.BlockSpec(memory_space=pl.ANY)


def dot(a, b, ca, cb):
    return lax.dot_general(a, b, (((ca,), (cb,)), ((), ())), preferred_element_type=F32)


def call(kernel, vmem=16, **kw):
    hint = pl.CostEstimate(flops=1, bytes_accessed=1, transcendentals=0)
    params = pltpu.CompilerParams(vmem_limit_bytes=vmem * 2**20)
    return pl.pallas_call(kernel, cost_estimate=hint, compiler_params=params, **kw)


def states_kernel(par_ref, q_ref, k_ref, v_ref, g_ref, keep_ref, send_ref, near_ref):
    heads = q_ref.shape[1] // DH
    half = heads // 2
    for hd in range(heads):
        at = slice(hd * DH, (hd + 1) * DH)
        for kind, (a, b) in enumerate(((q_ref, g_ref), (k_ref, v_ref))):
            s = dot(a[:, at], b[:, at], 0, 0)
            own = par_ref[0] == hd // half

            @pl.when(own)
            def _():
                keep_ref[kind, hd % half] = s
                near_ref[kind, hd % half] = s.astype(BF16)

            @pl.when(jnp.logical_not(own))
            def _():
                send_ref[kind, hd % half] = s.astype(BF16)


def states(par, q, k, v, g):
    shape = (2, q.shape[1] // DH // 2, DH, DH)
    return call(
        states_kernel,
        vmem=60,
        in_specs=[SMEM] + [VMEM] * 4,
        out_specs=[VMEM] * 3,
        out_shape=[jax.ShapeDtypeStruct(shape, d) for d in (F32, BF16, BF16)],
        name="states",
    )(par, q, k, v, g)


def split_kernel(per, par_ref, x_ref, own_ref, theirs_ref):
    width = x_ref.shape[1] // (2 * per)
    for k in range(2):
        for i in range(per):
            block = x_ref[:, (2 * i + k) * width : (2 * i + k + 1) * width]

            @pl.when(par_ref[0] == k)
            def _():
                own_ref[i] = block

            @pl.when(par_ref[0] != k)
            def _():
                theirs_ref[i] = block


def split(par, x, per):
    width = x.shape[1] // (2 * per)
    out = jax.ShapeDtypeStruct((per, x.shape[0], width), x.dtype)
    return call(
        functools.partial(split_kernel, per),
        in_specs=[SMEM, VMEM],
        out_specs=[VMEM] * 2,
        out_shape=[out, out],
        name="split",
    )(par, x)


def inside_kernel(q_ref, k_ref, g_ref, out_ref):
    n = q_ref.shape[0]
    rows = lax.broadcasted_iota(jnp.int32, (n, n), 0)
    cols = lax.broadcasted_iota(jnp.int32, (n, n), 1)
    scores = dot(q_ref[...], k_ref[...], 1, 1)
    scores = jnp.where(rows >= cols, scores, 0.0).astype(BF16)
    out_ref[...] = dot(scores, g_ref[...], 0, 0)


def inside(q, k, g):
    n, cols = q.shape
    spec = pl.BlockSpec((n, DH), lambda h: (0, h))
    return call(
        inside_kernel,
        grid=(cols // DH,),
        in_specs=[spec] * 3,
        out_specs=spec,
        out_shape=jax.ShapeDtypeStruct((n, cols), F32),
        name="inside",
    )(q, k, g)


def offer_kernel(pair_ref, keep_ref, got_ref, out_ref):
    sums = [(keep_ref[k] + got_ref[k].astype(F32)).astype(BF16) for k in range(2)]
    for p in range(out_ref.shape[0]):
        out_ref[p] = jnp.where(p < pair_ref[0], sums[0], sums[1])


def offer(pair, keep, got, pairs):
    return call(
        offer_kernel,
        in_specs=[SMEM, VMEM, VMEM],
        out_specs=VMEM,
        out_shape=jax.ShapeDtypeStruct((pairs, *keep.shape[1:]), BF16),
        name="offer",
    )(pair, keep, got)


def far_kernel(pair_ref, every_ref, out_ref, send_ref):
    for kind in range(2):
        total = jnp.zeros(out_ref.shape[1:], F32)
        for p in range(every_ref.shape[0]):
            reached = p > pair_ref[0] if kind == 0 else p < pair_ref[0]
            total = total + jnp.where(reached, every_ref[p].astype(F32), 0.0)
        out_ref[kind] = total
        send_ref[kind] = total.astype(BF16)


def far_states(pair, every):
    shape = (2, *every.shape[1:])
    return call(
        far_kernel,
        in_specs=[SMEM, VMEM],
        out_specs=[VMEM] * 2,
        out_shape=[jax.ShapeDtypeStruct(shape, d) for d in (F32, BF16)],
        name="far",
    )(pair, every)


def entering(par, kind, hd, half, far, got_far, near, got_near):
    mine = par == hd // half
    i = hd % half
    outer = jnp.where(mine, far[kind, i], got_far[kind, i].astype(F32))
    close = jnp.where(mine, near[kind, i].astype(F32), got_near[kind, i].astype(F32))
    total = outer + jnp.where(par == kind, close, 0.0)
    hi = total.astype(BF16)
    return hi, (total - hi.astype(F32)).astype(BF16)


def value_kernel(factor, half, par_ref, k_ref, vi_ref, *refs):
    ends, out_ref = refs[:-1], refs[-1]
    for hd in range(2 * half):
        at = slice(hd * DH, (hd + 1) * DH)
        hi, lo = entering(par_ref[0], 0, hd, half, *ends)
        k = k_ref[:, at]
        total = vi_ref[:, at] + (dot(k, hi, 1, 0) + dot(k, lo, 1, 0))
        out_ref[:, at] = (factor * total).astype(BF16)


def finish_value(factor, par, k, vi, ends):
    return call(
        functools.partial(value_kernel, factor, k.shape[1] // DH // 2),
        in_specs=[SMEM] + [VMEM] * (2 + len(ends)),
        out_specs=VMEM,
        out_shape=jax.ShapeDtypeStruct(k.shape, BF16),
        name="finish_value",
    )(par, k, vi, *ends)


def others_kernel(factor, half, par_ref, q_ref, k_ref, v_ref, g_ref, *refs):
    ends, (qo_ref, ko_ref) = refs[:-2], refs[-2:]
    hd = pl.program_id(0)
    q, k, v, g = q_ref[...], k_ref[...], v_ref[...], g_ref[...]
    n = q.shape[0]
    rows = lax.broadcasted_iota(jnp.int32, (n, n), 0)
    cols = lax.broadcasted_iota(jnp.int32, (n, n), 1)
    scores = jnp.where(rows >= cols, dot(g, v, 1, 1), 0.0).astype(BF16)
    hi, lo = entering(par_ref[0], 1, hd, half, *ends)
    total = dot(scores, k, 1, 0) + (dot(g, hi, 1, 1) + dot(g, lo, 1, 1))
    qo_ref[...] = (factor * total).astype(BF16)
    hi, lo = entering(par_ref[0], 0, hd, half, *ends)
    total = dot(scores, q, 0, 0) + (dot(v, hi, 1, 1) + dot(v, lo, 1, 1))
    ko_ref[...] = (factor * total).astype(BF16)


def others(factor, par, q, k, v, g, ends):
    n, cols = q.shape
    spec = pl.BlockSpec((n, DH), lambda h: (0, h))
    shape = ends[0].shape
    state = pl.BlockSpec(shape, lambda h: (0, 0, 0, 0))
    out = jax.ShapeDtypeStruct(q.shape, BF16)
    return call(
        functools.partial(others_kernel, factor, cols // DH // 2),
        grid=(cols // DH,),
        in_specs=[SMEM] + [spec] * 4 + [state] * len(ends),
        out_specs=[spec] * 2,
        out_shape=[out] * 2,
        name="others",
    )(par, q, k, v, g, *ends)


def piece_kernel(count, offs_ref, subs_ref, a_ref, b_ref, *refs):
    own, theirs = refs[:count], refs[count : 2 * count]
    out_ref, x, y, at, bt, sems = refs[2 * count :]
    step, steps = pl.program_id(0), pl.num_programs(0)
    slot = lax.rem(step, 2)

    def fetch(k, to):
        for i in range(count):

            @pl.when(offs_ref[k] == i)
            def _():
                for j, (src, dst) in enumerate(((own, x), (theirs, y))):
                    pltpu.make_async_copy(
                        src[i].at[subs_ref[k]], dst.at[to], sems.at[j, to]
                    ).start()

    @pl.when(step == 0)
    def _():
        fetch(0, 0)

    @pl.when(step + 1 < steps)
    def _():
        fetch(step + 1, 1 - slot)

    @pl.when(step == 0)
    def _():
        at[...] = a_ref[...].T
        bt[...] = b_ref[...].T

    for j, (src, dst) in enumerate(((own, x), (theirs, y))):
        pltpu.make_async_copy(src[0].at[0], dst.at[slot], sems.at[j, slot]).wait()
    total = dot(at[...], x[slot], 1, 0) + dot(bt[...], y[slot], 1, 0)
    out_ref[0] = total.astype(out_ref.dtype)


def pieces(offs, subs, a, b, own, theirs):
    steps = offs.shape[0]
    count = len(own)
    _, n, width = own[0].shape
    cols = a.shape[1]
    return call(
        functools.partial(piece_kernel, count),
        grid=(steps,),
        in_specs=[SMEM] * 2 + [VMEM] * 2 + [ANY] * (2 * count),
        out_specs=pl.BlockSpec((1, cols, width), lambda s: (s, 0, 0)),
        out_shape=jax.ShapeDtypeStruct((steps, cols, width), BF16),
        scratch_shapes=[
            pltpu.VMEM((2, n, width), BF16),
            pltpu.VMEM((2, n, width), BF16),
            pltpu.VMEM((cols, n), BF16),
            pltpu.VMEM((cols, n), BF16),
            pltpu.SemaphoreType.DMA((2, 2)),
        ],
        name="pieces",
    )(offs, subs, a, b, *own, *theirs)


def weight_kernel(scale, x_ref, out_ref):
    out_ref[...] = x_ref[...].astype(F32).T * scale


def finish_weight(scale, x):
    return call(
        functools.partial(weight_kernel, scale),
        in_specs=[VMEM],
        out_specs=VMEM,
        out_shape=jax.ShapeDtypeStruct(x.shape[::-1], F32),
        name="finish_weight",
    )(x)


def block_product(per, at_ref, x_ref, y_ref, w_ref, wy_ref):
    w = w_ref[pl.ds(at_ref[0] * per, per)].reshape(-1, w_ref.shape[2])
    wy = wy_ref[at_ref[0] // 2]
    return dot(x_ref[...], w, 1, 1) + dot(y_ref[...], wy, 1, 1)


def part_kernel(per, count, at_ref, x_ref, y_ref, w_ref, wy_ref, *refs):
    total = block_product(per, at_ref, x_ref, y_ref, w_ref, wy_ref)
    for got in refs[:count]:
        total = total + got[...].astype(F32)
    refs[-1][...] = total.astype(BF16)


def head_part(at, per, x, y, w, wy, got=()):
    return call(
        functools.partial(part_kernel, per, len(got)),
        in_specs=[SMEM] + [VMEM] * (4 + len(got)),
        out_specs=VMEM,
        out_shape=jax.ShapeDtypeStruct((x.shape[0], per * w.shape[1]), BF16),
        name="head_part",
    )(at, x, y, w, wy, *got)


def join_kernel(per, count, par_ref, at_ref, x_ref, y_ref, w_ref, wy_ref, *refs):
    total = block_product(per, at_ref, x_ref, y_ref, w_ref, wy_ref)
    for got in refs[:count]:
        total = total + got[...].astype(F32)
    other_ref, out_ref = refs[count:]
    rows = w_ref.shape[1]
    both = (total.astype(BF16), other_ref[...])
    for k in range(2):

        @pl.when(par_ref[0] == k)
        def _():
            for i in range(per):
                at = slice(i * rows, (i + 1) * rows)
                for j in range(2):
                    to = (2 * i + j) * rows
                    out_ref[:, to : to + rows] = both[j ^ k][:, at]


def join(par, at, per, x, y, w, wy, got, other):
    return call(
        functools.partial(join_kernel, per, len(got)),
        in_specs=[SMEM] * 2 + [VMEM] * (5 + len(got)),
        out_specs=VMEM,
        out_shape=jax.ShapeDtypeStruct((x.shape[0], 2 * other.shape[1]), BF16),
        name="join",
    )(par, at, x, y, w, wy, *got, other)


def after(x, *earlier):
    return lax.optimization_barrier((x, *earlier))[0]


def local(queries, keys, values, out_grad, inputs, value_weight):
    length, cols = queries.shape
    n_ctx, n_head = lax.axis_size("ctx"), lax.axis_size("head")
    pairs = n_ctx // 2
    ctx, head = lax.axis_index("ctx"), lax.axis_index("head")
    parity, pair = ctx % 2, ctx // 2
    par = parity.astype(jnp.int32).reshape(1)
    factor = 1.0 / math.sqrt(DH * length * n_ctx)
    lines = [[2 * i + k for i in range(pairs)] for k in range(2)]
    def partner(x):
        return lax.ppermute(x, "ctx", [(i, i ^ 1) for i in range(n_ctx)])

    def across(x, bit):
        return lax.ppermute(x, "head", [(i, i ^ bit) for i in range(n_head)])

    weight = lax.all_gather(value_weight, "ctx", axis_index_groups=lines)

    keep, send, near16 = states(par, queries, keys, values, out_grad)
    their_half = partner(send)
    line = pair.astype(jnp.int32).reshape(1)
    offered = offer(line, keep, their_half, pairs)

    per = n_ctx // n_head // 2
    own, theirs = split(after(par, send), inputs, per)
    got_near = partner(after(near16, their_half))
    own, theirs = [own], [partner(after(theirs, their_half))]

    every = lax.all_to_all(
        offered, "ctx", split_axis=0, concat_axis=0, axis_index_groups=lines
    )
    far, send_far = far_states(line, every)
    theirs = [after(theirs[0], send_far)]
    ends = (far, partner(send_far), their_half, got_near)
    vi = inside(queries, after(keys, send_far), out_grad)
    mine = finish_value(factor, par, keys, vi, ends)
    other = partner(mine)

    offsets = [0]
    bit = n_head // 2
    while bit:
        own = own + [across(r, bit) for r in own]
        theirs = theirs + [across(r, bit) for r in theirs]
        offsets = offsets + [o ^ bit for o in offsets]
        bit //= 2
    own = [own[offsets.index(i)] for i in range(n_head)]
    theirs = [theirs[offsets.index(i)] for i in range(n_head)]

    query_grad, key_grad = others(
        factor, par, queries, keys, after(values, mine), out_grad, ends
    )

    which = jnp.arange(pairs, dtype=jnp.int32)
    found = pieces(
        (which // per) ^ head,
        which % per,
        after(mine, query_grad),
        other,
        own,
        theirs,
    )
    summed = lax.psum_scatter(found, "ctx", axis_index_groups=lines)
    weight_grad = finish_weight(1.0 / math.sqrt(length * n_ctx), summed)

    weight = after(weight, found)
    split_heads = weight.reshape(n_head // 2, 2, -1, cols)
    lent = across(jnp.where(head % 2 == 0, split_heads[:, 1], split_heads[:, 0]), 1)
    mine_too, other_too = across(mine, 1), across(other, 1)
    here = head.astype(jnp.int32).reshape(1)

    def summed_parts(x, y):
        return [
            across(head_part(here ^ off, per, x, y, weight, lent), off)
            for off in range(2, n_head, 2)
        ]

    got_other = summed_parts(other, other_too)
    got_mine = summed_parts(mine, mine_too)
    swapped = partner(
        head_part(here, per, other, other_too, weight, lent, got_other)
    )
    input_grad = join(
        par, here, per, mine, mine_too, weight, lent, got_mine, swapped
    )
    return (query_grad, key_grad, input_grad, weight_grad)


def solution(mesh):
    spec = P("ctx", "head")
    return jax.shard_map(
        local, mesh=mesh, in_specs=(spec,) * 6, out_specs=(spec,) * 4, check_vma=False
    )
```

```python
import functools
import math

import jax
import jax.numpy as jnp
from jax import lax
from jax.experimental import pallas as pl
from jax.experimental.pallas import tpu as pltpu
from jax.sharding import PartitionSpec as P

DH = 128
F32, BF16 = jnp.float32, jnp.bfloat16
VMEM = pl.BlockSpec(memory_space=pltpu.VMEM)
SMEM = pl.BlockSpec(memory_space=pltpu.SMEM)
ANY = pl.BlockSpec(memory_space=pl.ANY)


def dot(a, b, ca, cb):
    return lax.dot_general(a, b, (((ca,), (cb,)), ((), ())), preferred_element_type=F32)


def call(kernel, vmem=16, **kw):
    hint = pl.CostEstimate(flops=1, bytes_accessed=1, transcendentals=0)
    params = pltpu.CompilerParams(vmem_limit_bytes=vmem * 2**20)
    return pl.pallas_call(kernel, cost_estimate=hint, compiler_params=params, **kw)


def states_kernel(par_ref, *refs):
    arrays, (keep_ref, send_ref, near_ref), bufs, sems = (
        refs[:4],
        refs[4:7],
        refs[7:11],
        refs[11],
    )
    heads = arrays[0].shape[1] // DH
    half = heads // 2

    def copy(j, hd):
        at = pl.ds(hd * DH, DH)
        return pltpu.make_async_copy(
            arrays[j].at[:, at], bufs[j].at[:, at], sems.at[j, hd]
        )

    for hd in range(heads):
        for j in range(4):
            copy(j, hd).start()
    for hd in range(heads):
        at = slice(hd * DH, (hd + 1) * DH)
        for j in range(4):
            copy(j, hd).wait()
        for kind, (a, b) in enumerate(((0, 3), (1, 2))):
            s = dot(bufs[a][:, at], bufs[b][:, at], 0, 0)
            own = par_ref[0] == hd // half

            @pl.when(own)
            def _():
                keep_ref[kind, hd % half] = s
                near_ref[kind, hd % half] = s.astype(BF16)

            @pl.when(jnp.logical_not(own))
            def _():
                send_ref[kind, hd % half] = s.astype(BF16)


def states(par, *arrays):
    n, cols = arrays[0].shape
    heads = cols // DH
    shape = (2, heads // 2, DH, DH)
    return call(
        states_kernel,
        in_specs=[SMEM] + [pl.BlockSpec(memory_space=pltpu.HBM)] * 4,
        out_specs=[VMEM] * 3,
        out_shape=[jax.ShapeDtypeStruct(shape, d) for d in (F32, BF16, BF16)],
        scratch_shapes=[pltpu.VMEM((n, cols), BF16)] * 4
        + [pltpu.SemaphoreType.DMA((4, heads))],
        name="states",
    )(par, *arrays)


def split_kernel(per, par_ref, x_ref, own_ref, theirs_ref):
    width = x_ref.shape[1] // (2 * per)
    for k in range(2):
        for i in range(per):
            block = x_ref[:, (2 * i + k) * width : (2 * i + k + 1) * width]

            @pl.when(par_ref[0] == k)
            def _():
                own_ref[i] = block

            @pl.when(par_ref[0] != k)
            def _():
                theirs_ref[i] = block


def split(par, x, per):
    width = x.shape[1] // (2 * per)
    out = jax.ShapeDtypeStruct((per, x.shape[0], width), x.dtype)
    return call(
        functools.partial(split_kernel, per),
        in_specs=[SMEM, VMEM],
        out_specs=[VMEM] * 2,
        out_shape=[out, out],
        name="split",
    )(par, x)


def inside_kernel(q_ref, k_ref, g_ref, out_ref):
    n = q_ref.shape[0]
    rows = lax.broadcasted_iota(jnp.int32, (n, n), 0)
    cols = lax.broadcasted_iota(jnp.int32, (n, n), 1)
    scores = dot(q_ref[...], k_ref[...], 1, 1)
    scores = jnp.where(rows >= cols, scores, 0.0).astype(BF16)
    out_ref[...] = dot(scores, g_ref[...], 0, 0)


def inside(q, k, g):
    n, cols = q.shape
    spec = pl.BlockSpec((n, DH), lambda h: (0, h))
    return call(
        inside_kernel,
        grid=(cols // DH,),
        in_specs=[spec] * 3,
        out_specs=spec,
        out_shape=jax.ShapeDtypeStruct((n, cols), F32),
        name="inside",
    )(q, k, g)


def offer_kernel(pair_ref, keep_ref, got_ref, out_ref):
    sums = [(keep_ref[k] + got_ref[k].astype(F32)).astype(BF16) for k in range(2)]
    for p in range(out_ref.shape[0]):
        out_ref[p] = jnp.where(p < pair_ref[0], sums[0], sums[1])


def offer(pair, keep, got, pairs):
    return call(
        offer_kernel,
        in_specs=[SMEM, VMEM, VMEM],
        out_specs=VMEM,
        out_shape=jax.ShapeDtypeStruct((pairs, *keep.shape[1:]), BF16),
        name="offer",
    )(pair, keep, got)


def far_kernel(pair_ref, every_ref, out_ref, send_ref):
    for kind in range(2):
        total = jnp.zeros(out_ref.shape[1:], F32)
        for p in range(every_ref.shape[0]):
            reached = p > pair_ref[0] if kind == 0 else p < pair_ref[0]
            total = total + jnp.where(reached, every_ref[p].astype(F32), 0.0)
        out_ref[kind] = total
        send_ref[kind] = total.astype(BF16)


def far_states(pair, every):
    shape = (2, *every.shape[1:])
    return call(
        far_kernel,
        in_specs=[SMEM, VMEM],
        out_specs=[VMEM] * 2,
        out_shape=[jax.ShapeDtypeStruct(shape, d) for d in (F32, BF16)],
        name="far",
    )(pair, every)


def entering(par, kind, hd, half, far, got_far, near, got_near):
    mine = par == hd // half
    i = hd % half
    outer = jnp.where(mine, far[kind, i], got_far[kind, i].astype(F32))
    close = jnp.where(mine, near[kind, i].astype(F32), got_near[kind, i].astype(F32))
    total = outer + jnp.where(par == kind, close, 0.0)
    hi = total.astype(BF16)
    return hi, (total - hi.astype(F32)).astype(BF16)


def value_kernel(factor, half, par_ref, k_ref, vi_ref, *refs):
    ends, outs = refs[:-2], refs[-2:]
    for hd in range(2 * half):
        at = slice(hd * DH, (hd + 1) * DH)
        hi, lo = entering(par_ref[0], 0, hd, half, *ends)
        k = k_ref[:, at]
        total = vi_ref[:, at] + (dot(k, hi, 1, 0) + dot(k, lo, 1, 0))
        to = (hd % half) * DH
        outs[hd // half][:, to : to + DH] = (factor * total).astype(BF16)


def finish_value(factor, par, k, vi, ends):
    return call(
        functools.partial(value_kernel, factor, k.shape[1] // DH // 2),
        in_specs=[SMEM] + [VMEM] * (2 + len(ends)),
        out_specs=[VMEM] * 2,
        out_shape=[jax.ShapeDtypeStruct((k.shape[0], k.shape[1] // 2), BF16)] * 2,
        name="finish_value",
    )(par, k, vi, *ends)


def others_kernel(factor, half, par_ref, q_ref, k_ref, v_ref, g_ref, *refs):
    ends, (qo_ref, ko_ref) = refs[:-2], refs[-2:]
    hd = pl.program_id(0)
    q, k, v, g = q_ref[...], k_ref[...], v_ref[...], g_ref[...]
    n = q.shape[0]
    rows = lax.broadcasted_iota(jnp.int32, (n, n), 0)
    cols = lax.broadcasted_iota(jnp.int32, (n, n), 1)
    scores = jnp.where(rows >= cols, dot(g, v, 1, 1), 0.0).astype(BF16)
    hi, lo = entering(par_ref[0], 1, hd, half, *ends)
    total = dot(scores, k, 1, 0) + (dot(g, hi, 1, 1) + dot(g, lo, 1, 1))
    qo_ref[...] = (factor * total).astype(BF16)
    hi, lo = entering(par_ref[0], 0, hd, half, *ends)
    total = dot(scores, q, 0, 0) + (dot(v, hi, 1, 1) + dot(v, lo, 1, 1))
    ko_ref[...] = (factor * total).astype(BF16)


def others(factor, par, q, k, v, g, ends):
    n, cols = q.shape
    spec = pl.BlockSpec((n, DH), lambda h: (0, h))
    shape = ends[0].shape
    state = pl.BlockSpec(shape, lambda h: (0, 0, 0, 0))
    out = jax.ShapeDtypeStruct(q.shape, BF16)
    return call(
        functools.partial(others_kernel, factor, cols // DH // 2),
        grid=(cols // DH,),
        in_specs=[SMEM] + [spec] * 4 + [state] * len(ends),
        out_specs=[spec] * 2,
        out_shape=[out] * 2,
        name="others",
    )(par, q, k, v, g, *ends)


def piece_kernel(count, offs_ref, subs_ref, a_ref, b_ref, *refs):
    own, theirs = refs[:count], refs[count : 2 * count]
    out_ref, at, bt = refs[2 * count :]
    step = pl.program_id(0)

    @pl.when(step == 0)
    def _():
        at[...] = a_ref[...].T
        bt[...] = b_ref[...].T

    sub = subs_ref[step]
    for i in range(count):

        @pl.when(offs_ref[step] == i)
        def _():
            total = dot(at[...], own[i][sub], 1, 0) + dot(bt[...], theirs[i][sub], 1, 0)
            out_ref[0] = total.astype(out_ref.dtype)


def pieces(offs, subs, a, b, own, theirs):
    steps = offs.shape[0]
    count = len(own)
    _, n, width = own[0].shape
    cols = a.shape[1]
    return call(
        functools.partial(piece_kernel, count),
        vmem=20,
        grid=(steps,),
        in_specs=[SMEM] * 2 + [VMEM] * (2 + 2 * count),
        out_specs=pl.BlockSpec((1, cols, width), lambda s: (s, 0, 0)),
        out_shape=jax.ShapeDtypeStruct((steps, cols, width), BF16),
        scratch_shapes=[pltpu.VMEM((cols, n), BF16)] * 2,
        name="pieces",
    )(offs, subs, a, b, *own, *theirs)


def weight_kernel(scale, *refs):
    span = refs[0].shape[0]
    for i, x_ref in enumerate(refs[:-1]):
        refs[-1][:, i * span : (i + 1) * span] = x_ref[...].astype(F32).T * scale


def finish_weight(scale, parts):
    span, width = parts[0].shape
    return call(
        functools.partial(weight_kernel, scale),
        in_specs=[VMEM] * len(parts),
        out_specs=VMEM,
        out_shape=jax.ShapeDtypeStruct((width, span * len(parts)), F32),
        name="finish_weight",
    )(*parts)


def block_product(per, at_ref, vals, w_ref, wy_ref):
    w = w_ref[pl.ds(at_ref[0] * per, per)].reshape(-1, w_ref.shape[2])
    wy = wy_ref[at_ref[0] // 2]
    span = vals[0].shape[1]
    half = len(vals) // 2
    total = 0.0
    for i, x in enumerate(vals):
        part = (w, wy)[i // half]
        at = (i % half) * span
        total = total + dot(x[...], part[:, at : at + span], 1, 1)
    return total


def part_kernel(per, count, at_ref, w_ref, wy_ref, *refs):
    total = block_product(per, at_ref, refs[:count], w_ref, wy_ref)
    for got in refs[count:-1]:
        total = total + got[...].astype(F32)
    refs[-1][...] = total.astype(BF16)


def head_part(at, per, w, wy, vals, got=()):
    return call(
        functools.partial(part_kernel, per, len(vals)),
        in_specs=[SMEM] + [VMEM] * (2 + len(vals) + len(got)),
        out_specs=VMEM,
        out_shape=jax.ShapeDtypeStruct((vals[0].shape[0], per * w.shape[1]), BF16),
        name="head_part",
    )(at, w, wy, *vals, *got)


def join_kernel(per, count, par_ref, at_ref, w_ref, wy_ref, *refs):
    total = block_product(per, at_ref, refs[:count], w_ref, wy_ref)
    for got in refs[count:-2]:
        total = total + got[...].astype(F32)
    other_ref, out_ref = refs[-2:]
    rows = w_ref.shape[1]
    both = (total.astype(BF16), other_ref[...])
    for k in range(2):

        @pl.when(par_ref[0] == k)
        def _():
            for i in range(per):
                at = slice(i * rows, (i + 1) * rows)
                for j in range(2):
                    to = (2 * i + j) * rows
                    out_ref[:, to : to + rows] = both[j ^ k][:, at]


def join(par, at, per, w, wy, vals, got, other):
    return call(
        functools.partial(join_kernel, per, len(vals)),
        in_specs=[SMEM] * 2 + [VMEM] * (3 + len(vals) + len(got)),
        out_specs=VMEM,
        out_shape=jax.ShapeDtypeStruct((other.shape[0], 2 * other.shape[1]), BF16),
        name="join",
    )(par, at, w, wy, *vals, *got, other)


def after(x, *earlier):
    return lax.optimization_barrier((x, *earlier))[0]


def local(queries, keys, values, out_grad, inputs, value_weight):
    length, cols = queries.shape
    n_ctx, n_head = lax.axis_size("ctx"), lax.axis_size("head")
    pairs = n_ctx // 2
    ctx, head = lax.axis_index("ctx"), lax.axis_index("head")
    parity, pair = ctx % 2, ctx // 2
    par = parity.astype(jnp.int32).reshape(1)
    factor = 1.0 / math.sqrt(DH * length * n_ctx)
    lines = [[2 * i + k for i in range(pairs)] for k in range(2)]
    def partner(x):
        return lax.ppermute(x, "ctx", [(i, i ^ 1) for i in range(n_ctx)])

    def across(x, bit):
        return lax.ppermute(x, "head", [(i, i ^ bit) for i in range(n_head)])

    weight = lax.all_gather(value_weight, "ctx", axis_index_groups=lines)

    keep, send, near16 = states(par, queries, keys, values, out_grad)
    their_half = partner(send)
    line = pair.astype(jnp.int32).reshape(1)
    offered = offer(line, keep, their_half, pairs)

    per = n_ctx // n_head // 2
    own, theirs = split(after(par, send), inputs, per)
    got_near = partner(after(near16, their_half))
    own, theirs = [own], [partner(after(theirs, their_half))]

    every = lax.all_to_all(
        offered, "ctx", split_axis=0, concat_axis=0, axis_index_groups=lines
    )
    far, send_far = far_states(line, every)
    ends = (far, partner(send_far), their_half, got_near)
    vi = inside(queries, after(keys, offered), out_grad)
    theirs = [after(theirs[0], vi)]
    mine = finish_value(factor, par, keys, vi, ends)
    other = [partner(x) for x in mine]

    offsets = [0]
    bit = n_head // 2
    while bit:
        own = own + [across(r, bit) for r in own]
        theirs = theirs + [across(r, bit) for r in theirs]
        offsets = offsets + [o ^ bit for o in offsets]
        bit //= 2
    own = [own[offsets.index(i)] for i in range(n_head)]
    theirs = [theirs[offsets.index(i)] for i in range(n_head)]

    query_grad, key_grad = others(
        factor, par, queries, keys, after(values, mine[0]), out_grad, ends
    )

    which = jnp.arange(pairs, dtype=jnp.int32)
    offs, subs = (which // per) ^ head, which % per
    mine_too = [across(x, 1) for x in mine]
    first = pieces(offs, subs, after(mine[0], query_grad), other[0], own, theirs)
    weight = after(weight, first)
    split_heads = weight.reshape(n_head // 2, 2, -1, cols)
    lend = jnp.where(head % 2 == 0, split_heads[:, 1], split_heads[:, 0])
    lent = across(lend, 1)
    other_too = [across(x, 1) for x in other]
    second = pieces(offs, subs, after(mine[1], lend), other[1], own, theirs)
    sums = [
        lax.psum_scatter(x, "ctx", axis_index_groups=lines) for x in (first, second)
    ]
    weight_grad = finish_weight(1.0 / math.sqrt(length * n_ctx), sums)

    here = head.astype(jnp.int32).reshape(1)
    mine_vals = (after(mine[0], second), mine[1], *mine_too)
    other_vals = (after(other[0], second), other[1], *other_too)

    def summed_parts(vals):
        return [
            across(head_part(here ^ off, per, weight, lent, vals), off)
            for off in range(2, n_head, 2)
        ]

    got_other = summed_parts(other_vals)
    got_mine = summed_parts(mine_vals)
    swapped = partner(head_part(here, per, weight, lent, other_vals, got_other))
    input_grad = join(par, here, per, weight, lent, mine_vals, got_mine, swapped)
    return (query_grad, key_grad, input_grad, weight_grad)


def solution(mesh):
    spec = P("ctx", "head")
    return jax.shard_map(
        local, mesh=mesh, in_specs=(spec,) * 6, out_specs=(spec,) * 4, check_vma=False
    )
```

```python
import functools
import math

import jax
import jax.numpy as jnp
from jax import lax
from jax.experimental import pallas as pl
from jax.experimental.pallas import tpu as pltpu
from jax.sharding import PartitionSpec as P

DH = 128
F32, BF16 = jnp.float32, jnp.bfloat16
VMEM = pl.BlockSpec(memory_space=pltpu.VMEM)
SMEM = pl.BlockSpec(memory_space=pltpu.SMEM)
ANY = pl.BlockSpec(memory_space=pl.ANY)


def dot(a, b, ca, cb):
    return lax.dot_general(a, b, (((ca,), (cb,)), ((), ())), preferred_element_type=F32)


def call(kernel, vmem=16, **kw):
    hint = pl.CostEstimate(flops=1, bytes_accessed=1, transcendentals=0)
    params = pltpu.CompilerParams(vmem_limit_bytes=vmem * 2**20)
    return pl.pallas_call(kernel, cost_estimate=hint, compiler_params=params, **kw)


def states_kernel(par_ref, *refs):
    arrays, (keep_ref, send_ref, near_ref), bufs, sems = (
        refs[:4],
        refs[4:7],
        refs[7:11],
        refs[11],
    )
    heads = arrays[0].shape[1] // DH
    half = heads // 2

    def copy(j, hd):
        at = pl.ds(hd * DH, DH)
        return pltpu.make_async_copy(
            arrays[j].at[:, at], bufs[j].at[:, at], sems.at[j, hd]
        )

    for hd in range(heads):
        for j in range(4):
            copy(j, hd).start()
    for hd in range(heads):
        at = slice(hd * DH, (hd + 1) * DH)
        for j in range(4):
            copy(j, hd).wait()
        for kind, (a, b) in enumerate(((0, 3), (1, 2))):
            s = dot(bufs[a][:, at], bufs[b][:, at], 0, 0)
            own = par_ref[0] == hd // half

            @pl.when(own)
            def _():
                keep_ref[kind, hd % half] = s
                near_ref[kind, hd % half] = s.astype(BF16)

            @pl.when(jnp.logical_not(own))
            def _():
                send_ref[kind, hd % half] = s.astype(BF16)


def states(par, *arrays):
    n, cols = arrays[0].shape
    heads = cols // DH
    shape = (2, heads // 2, DH, DH)
    return call(
        states_kernel,
        vmem=60,
        in_specs=[SMEM] + [pl.BlockSpec(memory_space=pltpu.HBM)] * 4,
        out_specs=[VMEM] * 3,
        out_shape=[jax.ShapeDtypeStruct(shape, d) for d in (F32, BF16, BF16)],
        scratch_shapes=[pltpu.VMEM((n, cols), BF16)] * 4
        + [pltpu.SemaphoreType.DMA((4, heads))],
        name="states",
    )(par, *arrays)


def split_kernel(per, par_ref, x_ref, own_ref, theirs_ref):
    width = x_ref.shape[1] // (2 * per)
    for k in range(2):
        for i in range(per):
            block = x_ref[:, (2 * i + k) * width : (2 * i + k + 1) * width]

            @pl.when(par_ref[0] == k)
            def _():
                own_ref[i] = block

            @pl.when(par_ref[0] != k)
            def _():
                theirs_ref[i] = block


def split(par, x, per):
    width = x.shape[1] // (2 * per)
    out = jax.ShapeDtypeStruct((per, x.shape[0], width), x.dtype)
    return call(
        functools.partial(split_kernel, per),
        in_specs=[SMEM, VMEM],
        out_specs=[VMEM] * 2,
        out_shape=[out, out],
        name="split",
    )(par, x)


def inside_kernel(*refs):
    arrays, out_ref, bufs, sems = refs[:3], refs[3], refs[4:7], refs[7]
    n, cols = out_ref.shape
    heads = cols // DH

    def copy(j, hd):
        at = pl.ds(hd * DH, DH)
        return pltpu.make_async_copy(
            arrays[j].at[:, at], bufs[j].at[:, at], sems.at[j, hd]
        )

    for hd in range(heads):
        for j in range(3):
            copy(j, hd).start()
    rows = lax.broadcasted_iota(jnp.int32, (n, n), 0)
    causal = rows >= lax.broadcasted_iota(jnp.int32, (n, n), 1)
    for hd in range(heads):
        at = slice(hd * DH, (hd + 1) * DH)
        for j in range(3):
            copy(j, hd).wait()
        q, k, g = (x[:, at] for x in bufs)
        scores = jnp.where(causal, dot(q, k, 1, 1), 0.0).astype(BF16)
        out_ref[:, at] = dot(scores, g, 0, 0)


def inside(*arrays):
    n, cols = arrays[0].shape
    return call(
        inside_kernel,
        in_specs=[pl.BlockSpec(memory_space=pltpu.HBM)] * 3,
        out_specs=VMEM,
        out_shape=jax.ShapeDtypeStruct((n, cols), F32),
        scratch_shapes=[pltpu.VMEM((n, cols), BF16)] * 3
        + [pltpu.SemaphoreType.DMA((3, cols // DH))],
        name="inside",
    )(*arrays)


def offer_kernel(pair_ref, keep_ref, got_ref, out_ref):
    sums = [(keep_ref[k] + got_ref[k].astype(F32)).astype(BF16) for k in range(2)]
    for p in range(out_ref.shape[0]):
        out_ref[p] = jnp.where(p < pair_ref[0], sums[0], sums[1])


def offer(pair, keep, got, pairs):
    return call(
        offer_kernel,
        in_specs=[SMEM, VMEM, VMEM],
        out_specs=VMEM,
        out_shape=jax.ShapeDtypeStruct((pairs, *keep.shape[1:]), BF16),
        name="offer",
    )(pair, keep, got)


def far_kernel(pair_ref, every_ref, out_ref, send_ref):
    for kind in range(2):
        total = jnp.zeros(out_ref.shape[1:], F32)
        for p in range(every_ref.shape[0]):
            reached = p > pair_ref[0] if kind == 0 else p < pair_ref[0]
            total = total + jnp.where(reached, every_ref[p].astype(F32), 0.0)
        out_ref[kind] = total
        send_ref[kind] = total.astype(BF16)


def far_states(pair, every):
    shape = (2, *every.shape[1:])
    return call(
        far_kernel,
        in_specs=[SMEM, VMEM],
        out_specs=[VMEM] * 2,
        out_shape=[jax.ShapeDtypeStruct(shape, d) for d in (F32, BF16)],
        name="far",
    )(pair, every)


def entering(par, kind, hd, half, far, got_far, near, got_near):
    mine = par == hd // half
    i = hd % half
    outer = jnp.where(mine, far[kind, i], got_far[kind, i].astype(F32))
    close = jnp.where(mine, near[kind, i].astype(F32), got_near[kind, i].astype(F32))
    total = outer + jnp.where(par == kind, close, 0.0)
    hi = total.astype(BF16)
    return hi, (total - hi.astype(F32)).astype(BF16)


def value_kernel(factor, half, par_ref, k_ref, vi_ref, *refs):
    ends, out_ref = refs[:-1], refs[-1]
    for hd in range(2 * half):
        at = slice(hd * DH, (hd + 1) * DH)
        hi, lo = entering(par_ref[0], 0, hd, half, *ends)
        k = k_ref[:, at]
        total = vi_ref[:, at] + (dot(k, hi, 1, 0) + dot(k, lo, 1, 0))
        out_ref[:, at] = (factor * total).astype(BF16)


def finish_value(factor, par, k, vi, ends):
    return call(
        functools.partial(value_kernel, factor, k.shape[1] // DH // 2),
        in_specs=[SMEM] + [VMEM] * (2 + len(ends)),
        out_specs=VMEM,
        out_shape=jax.ShapeDtypeStruct(k.shape, BF16),
        name="finish_value",
    )(par, k, vi, *ends)


def others_kernel(factor, half, par_ref, q_ref, k_ref, v_ref, g_ref, *refs):
    ends, (qo_ref, ko_ref) = refs[:-2], refs[-2:]
    hd = pl.program_id(0)
    q, k, v, g = q_ref[...], k_ref[...], v_ref[...], g_ref[...]
    n = q.shape[0]
    rows = lax.broadcasted_iota(jnp.int32, (n, n), 0)
    cols = lax.broadcasted_iota(jnp.int32, (n, n), 1)
    scores = jnp.where(rows >= cols, dot(g, v, 1, 1), 0.0).astype(BF16)
    hi, lo = entering(par_ref[0], 1, hd, half, *ends)
    total = dot(scores, k, 1, 0) + (dot(g, hi, 1, 1) + dot(g, lo, 1, 1))
    qo_ref[...] = (factor * total).astype(BF16)
    hi, lo = entering(par_ref[0], 0, hd, half, *ends)
    total = dot(scores, q, 0, 0) + (dot(v, hi, 1, 1) + dot(v, lo, 1, 1))
    ko_ref[...] = (factor * total).astype(BF16)


def others(factor, par, q, k, v, g, ends):
    n, cols = q.shape
    spec = pl.BlockSpec((n, DH), lambda h: (0, h))
    shape = ends[0].shape
    state = pl.BlockSpec(shape, lambda h: (0, 0, 0, 0))
    out = jax.ShapeDtypeStruct(q.shape, BF16)
    return call(
        functools.partial(others_kernel, factor, cols // DH // 2),
        grid=(cols // DH,),
        in_specs=[SMEM] + [spec] * 4 + [state] * len(ends),
        out_specs=[spec] * 2,
        out_shape=[out] * 2,
        name="others",
    )(par, q, k, v, g, *ends)


def piece_kernel(count, offs_ref, subs_ref, a_ref, b_ref, *refs):
    own, theirs = refs[:count], refs[count : 2 * count]
    outs, (x, y, at, bt, sems) = refs[2 * count : -5], refs[-5:]
    step, steps = pl.program_id(0), pl.num_programs(0)
    slot = lax.rem(step, 2)

    def fetch(k, to):
        for i in range(count):

            @pl.when(offs_ref[k] == i)
            def _():
                for j, (src, dst) in enumerate(((own, x), (theirs, y))):
                    pltpu.make_async_copy(
                        src[i].at[subs_ref[k]], dst.at[to], sems.at[j, to]
                    ).start()

    @pl.when(step == 0)
    def _():
        fetch(0, 0)

    @pl.when(step + 1 < steps)
    def _():
        fetch(step + 1, 1 - slot)

    @pl.when(step == 0)
    def _():
        at[...] = a_ref[...].T
        bt[...] = b_ref[...].T

    for j, (src, dst) in enumerate(((own, x), (theirs, y))):
        pltpu.make_async_copy(src[0].at[0], dst.at[slot], sems.at[j, slot]).wait()
    total = dot(at[...], x[slot], 1, 0) + dot(bt[...], y[slot], 1, 0)
    for i, out_ref in enumerate(outs):

        @pl.when(step == i)
        def _():
            out_ref[...] = total.astype(out_ref.dtype)


def pieces(dtype, offs, subs, a, b, own, theirs):
    steps = offs.shape[0]
    count = len(own)
    _, n, width = own[0].shape
    cols = a.shape[1]
    return call(
        functools.partial(piece_kernel, count),
        grid=(steps,),
        in_specs=[SMEM] * 2 + [VMEM] * 2 + [ANY] * (2 * count),
        out_specs=[VMEM] * steps,
        out_shape=[jax.ShapeDtypeStruct((cols, width), dtype)] * steps,
        scratch_shapes=[
            pltpu.VMEM((2, n, width), BF16),
            pltpu.VMEM((2, n, width), BF16),
            pltpu.VMEM((cols, n), BF16),
            pltpu.VMEM((cols, n), BF16),
            pltpu.SemaphoreType.DMA((2, 2)),
        ],
        name="pieces",
    )(offs, subs, a, b, *own, *theirs)


def weight_kernel(scale, moved_ref, own_ref, out_ref):
    out_ref[...] = (moved_ref[...].astype(F32) + own_ref[...]).T * scale


def finish_weight(scale, moved, own):
    return call(
        functools.partial(weight_kernel, scale),
        in_specs=[VMEM] * 2,
        out_specs=VMEM,
        out_shape=jax.ShapeDtypeStruct(moved.shape[::-1], F32),
        name="finish_weight",
    )(moved, own)


def add_kernel(moved_ref, own_ref, out_ref):
    out_ref[...] = (moved_ref[...].astype(F32) + own_ref[...]).astype(BF16)


def add_own(moved, own):
    return call(
        add_kernel,
        in_specs=[VMEM] * 2,
        out_specs=VMEM,
        out_shape=jax.ShapeDtypeStruct(moved.shape, BF16),
        name="add_own",
    )(moved, own)


def arrange_kernel(per, head_ref, which_ref, *refs):
    count = which_ref.shape[0]
    blocks, out_ref, lend_ref, sems = refs[:count], refs[-3], refs[-2], refs[-1]
    rows = blocks[0].shape[0]

    def copies(s):
        p = which_ref[s]
        to = lend_ref.at[p // per // 2, pl.ds((p % per) * rows, rows)]
        keep = pltpu.make_async_copy(blocks[s], out_ref.at[p], sems.at[0, s])
        lend = pltpu.make_async_copy(blocks[s], to, sems.at[1, s])
        return keep, lend, (p // per) % 2 != head_ref[0] % 2

    for s in range(count):
        keep, lend, needed = copies(s)
        keep.start()
        pl.when(needed)(lend.start)
    for s in range(count):
        keep, lend, needed = copies(s)
        keep.wait()
        pl.when(needed)(lend.wait)


def arrange(per, n_head, head, which, blocks):
    rows, cols = blocks[0].shape
    count = len(blocks)
    return call(
        functools.partial(arrange_kernel, per),
        in_specs=[SMEM] * 2 + [ANY] * count,
        out_specs=[VMEM] * 2,
        out_shape=[
            jax.ShapeDtypeStruct((count, rows, cols), BF16),
            jax.ShapeDtypeStruct((n_head // 2, per * rows, cols), BF16),
        ],
        scratch_shapes=[pltpu.SemaphoreType.DMA((2, count))],
        name="arrange",
    )(head, which, *blocks)


def block_product(per, at_ref, x_ref, y_ref, w_ref, wy_ref):
    w = w_ref[pl.ds(at_ref[0] * per, per)].reshape(-1, w_ref.shape[2])
    wy = wy_ref[at_ref[0] // 2]
    return dot(x_ref[...], w, 1, 1) + dot(y_ref[...], wy, 1, 1)


def part_kernel(per, count, at_ref, x_ref, y_ref, w_ref, wy_ref, *refs):
    total = block_product(per, at_ref, x_ref, y_ref, w_ref, wy_ref)
    for got in refs[:count]:
        total = total + got[...].astype(F32)
    refs[-1][...] = total.astype(BF16)


def head_part(at, per, x, y, w, wy, got=()):
    return call(
        functools.partial(part_kernel, per, len(got)),
        in_specs=[SMEM] + [VMEM] * (4 + len(got)),
        out_specs=VMEM,
        out_shape=jax.ShapeDtypeStruct((x.shape[0], per * w.shape[1]), BF16),
        name="head_part",
    )(at, x, y, w, wy, *got)


def join_kernel(per, count, par_ref, at_ref, x_ref, y_ref, w_ref, wy_ref, *refs):
    total = block_product(per, at_ref, x_ref, y_ref, w_ref, wy_ref)
    for got in refs[:count]:
        total = total + got[...].astype(F32)
    other_ref, out_ref = refs[count:]
    rows = w_ref.shape[1]
    both = (total.astype(BF16), other_ref[...])
    for k in range(2):

        @pl.when(par_ref[0] == k)
        def _():
            for i in range(per):
                at = slice(i * rows, (i + 1) * rows)
                for j in range(2):
                    to = (2 * i + j) * rows
                    out_ref[:, to : to + rows] = both[j ^ k][:, at]


def join(par, at, per, x, y, w, wy, got, other):
    return call(
        functools.partial(join_kernel, per, len(got)),
        in_specs=[SMEM] * 2 + [VMEM] * (5 + len(got)),
        out_specs=VMEM,
        out_shape=jax.ShapeDtypeStruct((x.shape[0], 2 * other.shape[1]), BF16),
        name="join",
    )(par, at, x, y, w, wy, *got, other)


def after(x, *earlier):
    return lax.optimization_barrier((x, *earlier))[0]


def local(queries, keys, values, out_grad, inputs, value_weight):
    length, cols = queries.shape
    n_ctx, n_head = lax.axis_size("ctx"), lax.axis_size("head")
    pairs = n_ctx // 2
    ctx, head = lax.axis_index("ctx"), lax.axis_index("head")
    parity, pair = ctx % 2, ctx // 2
    par = parity.astype(jnp.int32).reshape(1)
    factor = 1.0 / math.sqrt(DH * length * n_ctx)
    lines = [[2 * i + k for i in range(pairs)] for k in range(2)]
    def partner(x):
        return lax.ppermute(x, "ctx", [(i, i ^ 1) for i in range(n_ctx)])

    def across(x, bit):
        return lax.ppermute(x, "head", [(i, i ^ bit) for i in range(n_head)])

    order = list(range(0, pairs, 2)) + list(range(1, pairs, 2))[::-1]
    place = [order.index(i) for i in range(pairs)]
    moves = [
        (2 * order[i] + k, 2 * order[(i + 1) % pairs] + k)
        for i in range(pairs)
        for k in range(2)
    ]
    spot = jnp.asarray(place, jnp.int32)[pair]
    steps = jnp.arange(pairs, dtype=jnp.int32)

    def ring(x):
        return lax.ppermute(x, "ctx", moves)

    keep, send, near16 = states(par, queries, keys, values, out_grad)
    their_half = partner(send)
    line = pair.astype(jnp.int32).reshape(1)

    per = n_ctx // n_head // 2
    own, theirs = split(after(par, send), inputs, per)
    vi = inside(after(queries, own), keys, out_grad)
    blocks = [value_weight, ring(after(value_weight, send))]
    got_near = partner(after(near16, their_half))
    own, theirs = [own], [partner(after(theirs, their_half))]

    offered = offer(line, after(keep, vi), their_half, pairs)
    every = lax.all_to_all(
        offered, "ctx", split_axis=0, concat_axis=0, axis_index_groups=lines
    )
    far, send_far = far_states(line, every)
    ends = (far, partner(send_far), their_half, got_near)
    theirs = [after(theirs[0], send_far)]
    token = send_far
    mine = finish_value(factor, par, keys, vi, ends)
    other = partner(mine)
    query_grad, key_grad = others(
        factor, par, queries, keys, after(values, mine), out_grad, ends
    )
    for _ in range(2, pairs):
        blocks.append(ring(after(blocks[-1], token)))
        token = mine

    offsets = [0]
    bit = n_head // 2
    while bit:
        own = own + [across(r, bit) for r in own]
        theirs = theirs + [across(r, bit) for r in theirs]
        offsets = offsets + [o ^ bit for o in offsets]
        bit //= 2
    own = [own[offsets.index(i)] for i in range(n_head)]
    theirs = [theirs[offsets.index(i)] for i in range(n_head)]

    which = jnp.asarray(order, jnp.int32)[(spot - 1 - steps) % pairs]
    offs, subs = (which // per) ^ head, which % per
    vals = (after(mine, query_grad), other, own, theirs)
    (total,) = pieces(BF16, offs[:1], subs[:1], *vals)
    moved = ring(total)
    vals = (after(mine, total), other, own, theirs)
    rest = pieces(F32, offs[1:], subs[1:], *vals)

    here = head.astype(jnp.int32).reshape(1)
    held = jnp.asarray(order, jnp.int32)[(spot - steps) % pairs]
    weight, lend = arrange(per, n_head, here, held, [after(blocks[0], rest[0])] + blocks[1:])
    lent = across(lend, 1)
    mine_too, other_too = across(after(mine, total), 1), across(other, 1)

    def summed_parts(x, y):
        sent = [
            head_part(here ^ off, per, x, y, weight, lent)
            for off in range(2, n_head, 2)
        ]
        return sent[-1], [across(x, 2 * i + 2) for i, x in enumerate(sent)]

    token, got_other = summed_parts(other, other_too)
    total = add_own(moved, after(rest[0], token))
    moved = ring(total)
    token, got_mine = summed_parts(after(mine, total), mine_too)
    for i in range(1, pairs - 2):
        total = add_own(moved, after(rest[i], token))
        moved = ring(total)
    part = head_part(
        here, per, after(other, total), other_too, weight, lent, got_other
    )
    swapped = partner(part)
    weight_grad = finish_weight(
        1.0 / math.sqrt(length * n_ctx), moved, after(rest[-1], part)
    )
    input_grad = join(
        par, here, per, after(mine, weight_grad), mine_too, weight, lent, got_mine, swapped
    )
    return (query_grad, key_grad, input_grad, weight_grad)


def solution(mesh):
    spec = P("ctx", "head")
    return jax.shard_map(
        local, mesh=mesh, in_specs=(spec,) * 6, out_specs=(spec,) * 4, check_vma=False
    )
```

```python
import functools
import math

import jax
import jax.numpy as jnp
from jax import lax
from jax.experimental import pallas as pl
from jax.experimental.pallas import tpu as pltpu
from jax.sharding import PartitionSpec as P

DH = 128
F32, BF16 = jnp.float32, jnp.bfloat16
VMEM = pl.BlockSpec(memory_space=pltpu.VMEM)
SMEM = pl.BlockSpec(memory_space=pltpu.SMEM)
ANY = pl.BlockSpec(memory_space=pl.ANY)


def dot(a, b, ca, cb):
    return lax.dot_general(a, b, (((ca,), (cb,)), ((), ())), preferred_element_type=F32)


def call(kernel, vmem=16, **kw):
    hint = pl.CostEstimate(flops=1, bytes_accessed=1, transcendentals=0)
    params = pltpu.CompilerParams(vmem_limit_bytes=vmem * 2**20)
    return pl.pallas_call(kernel, cost_estimate=hint, compiler_params=params, **kw)


def states_kernel(par_ref, *refs):
    arrays, (keep_ref, send_ref, near_ref), bufs, sems = (
        refs[:4],
        refs[4:7],
        refs[7:11],
        refs[11],
    )
    heads = arrays[0].shape[1] // DH
    half = heads // 2

    def copy(j, hd):
        at = pl.ds(hd * DH, DH)
        return pltpu.make_async_copy(
            arrays[j].at[:, at], bufs[j].at[:, at], sems.at[j, hd]
        )

    for hd in range(heads):
        for j in range(4):
            copy(j, hd).start()
    for hd in range(heads):
        at = slice(hd * DH, (hd + 1) * DH)
        for j in range(4):
            copy(j, hd).wait()
        for kind, (a, b) in enumerate(((0, 3), (1, 2))):
            s = dot(bufs[a][:, at], bufs[b][:, at], 0, 0)
            own = par_ref[0] == hd // half

            @pl.when(own)
            def _():
                keep_ref[kind, hd % half] = s
                near_ref[kind, hd % half] = s.astype(BF16)

            @pl.when(jnp.logical_not(own))
            def _():
                send_ref[kind, hd % half] = s.astype(BF16)


def states(par, *arrays):
    n, cols = arrays[0].shape
    heads = cols // DH
    shape = (2, heads // 2, DH, DH)
    return call(
        states_kernel,
        vmem=60,
        in_specs=[SMEM] + [pl.BlockSpec(memory_space=pltpu.HBM)] * 4,
        out_specs=[VMEM] * 3,
        out_shape=[jax.ShapeDtypeStruct(shape, d) for d in (F32, BF16, BF16)],
        scratch_shapes=[pltpu.VMEM((n, cols), BF16)] * 4
        + [pltpu.SemaphoreType.DMA((4, heads))],
        name="states",
    )(par, *arrays)


def split_kernel(per, par_ref, x_ref, own_ref, theirs_ref, sems):
    width = own_ref.shape[2]
    for k in range(2):

        @pl.when(par_ref[0] == k)
        def _():
            copies = []
            for i in range(per):
                for j, out_ref in enumerate((own_ref, theirs_ref)):
                    at = (2 * i + (k ^ j)) * width
                    if width % 128:
                        out_ref[i] = x_ref[:, at : at + width]
                    else:
                        src = x_ref.at[:, pl.ds(at, width)]
                        copies.append(
                            pltpu.make_async_copy(src, out_ref.at[i], sems.at[j, i])
                        )
            for c in copies:
                c.start()
            for c in copies:
                c.wait()


def split(par, x, per):
    width = x.shape[1] // (2 * per)
    out = jax.ShapeDtypeStruct((per, x.shape[0], width), x.dtype)
    place = VMEM if width % 128 else pl.BlockSpec(memory_space=pltpu.HBM)
    return call(
        functools.partial(split_kernel, per),
        in_specs=[SMEM, place],
        out_specs=[VMEM] * 2,
        out_shape=[out, out],
        scratch_shapes=[pltpu.SemaphoreType.DMA((2, per))],
        name="split",
    )(par, x)


def inside_kernel(*refs):
    arrays, (out_ref, k_ref), bufs, sems = refs[:3], refs[3:5], refs[5:8], refs[8]
    n, cols = out_ref.shape
    heads = cols // DH

    def copy(j, hd):
        at = pl.ds(hd * DH, DH)
        return pltpu.make_async_copy(
            arrays[j].at[:, at], bufs[j].at[:, at], sems.at[j, hd]
        )

    for hd in range(heads):
        for j in range(3):
            copy(j, hd).start()
    rows = lax.broadcasted_iota(jnp.int32, (n, n), 0)
    causal = rows >= lax.broadcasted_iota(jnp.int32, (n, n), 1)
    for hd in range(heads):
        at = slice(hd * DH, (hd + 1) * DH)
        for j in range(3):
            copy(j, hd).wait()
        q, k, g = (x[:, at] for x in bufs)
        scores = jnp.where(causal, dot(q, k, 1, 1), 0.0).astype(BF16)
        out_ref[:, at] = dot(scores, g, 0, 0)
        k_ref[:, at] = k


def inside(*arrays):
    n, cols = arrays[0].shape
    return call(
        inside_kernel,
        in_specs=[pl.BlockSpec(memory_space=pltpu.HBM)] * 3,
        out_specs=[VMEM] * 2,
        out_shape=[jax.ShapeDtypeStruct((n, cols), d) for d in (F32, BF16)],
        scratch_shapes=[pltpu.VMEM((n, cols), BF16)] * 3
        + [pltpu.SemaphoreType.DMA((3, cols // DH))],
        name="inside",
    )(*arrays)


def offer_kernel(pair_ref, keep_ref, got_ref, out_ref):
    sums = [(keep_ref[k] + got_ref[k].astype(F32)).astype(BF16) for k in range(2)]
    for p in range(out_ref.shape[0]):
        out_ref[p] = jnp.where(p < pair_ref[0], sums[0], sums[1])


def offer(pair, keep, got, pairs):
    return call(
        offer_kernel,
        in_specs=[SMEM, VMEM, VMEM],
        out_specs=VMEM,
        out_shape=jax.ShapeDtypeStruct((pairs, *keep.shape[1:]), BF16),
        name="offer",
    )(pair, keep, got)


def far_kernel(pair_ref, every_ref, near_ref, out_ref, send_ref):
    for kind in range(2):
        total = jnp.zeros(out_ref.shape[1:], F32)
        for p in range(every_ref.shape[0]):
            reached = p > pair_ref[0] if kind == 0 else p < pair_ref[0]
            total = total + jnp.where(reached, every_ref[p].astype(F32), 0.0)
        out_ref[kind] = total
        send_ref[0, kind] = total.astype(BF16)
        send_ref[1, kind] = near_ref[kind]


def far_states(pair, every, near):
    shape = (2, *every.shape[1:])
    return call(
        far_kernel,
        in_specs=[SMEM, VMEM, VMEM],
        out_specs=[VMEM] * 2,
        out_shape=[
            jax.ShapeDtypeStruct(shape, F32),
            jax.ShapeDtypeStruct((2, *shape), BF16),
        ],
        name="far",
    )(pair, every, near)


def entering(par, kind, hd, half, far, got, near):
    mine = par == hd // half
    i = hd % half
    outer = jnp.where(mine, far[kind, i], got[0, kind, i].astype(F32))
    close = jnp.where(mine, near[kind, i].astype(F32), got[1, kind, i].astype(F32))
    total = outer + jnp.where(par == kind, close, 0.0)
    hi = total.astype(BF16)
    return hi, (total - hi.astype(F32)).astype(BF16)


def value_kernel(factor, half, par_ref, k_ref, vi_ref, *refs):
    ends, out_ref = refs[:-1], refs[-1]
    for hd in range(2 * half):
        at = slice(hd * DH, (hd + 1) * DH)
        hi, lo = entering(par_ref[0], 0, hd, half, *ends)
        k = k_ref[:, at]
        total = vi_ref[:, at] + (dot(k, hi, 1, 0) + dot(k, lo, 1, 0))
        out_ref[:, at] = (factor * total).astype(BF16)


def finish_value(factor, par, k, vi, ends):
    return call(
        functools.partial(value_kernel, factor, k.shape[1] // DH // 2),
        in_specs=[SMEM] + [VMEM] * (2 + len(ends)),
        out_specs=VMEM,
        out_shape=jax.ShapeDtypeStruct(k.shape, BF16),
        name="finish_value",
    )(par, k, vi, *ends)


def others_kernel(factor, half, par_ref, q_ref, k_ref, v_ref, g_ref, *refs):
    ends, (qo_ref, ko_ref) = refs[:-2], refs[-2:]
    hd = pl.program_id(0)
    q, k, v, g = q_ref[...], k_ref[...], v_ref[...], g_ref[...]
    n = q.shape[0]
    rows = lax.broadcasted_iota(jnp.int32, (n, n), 0)
    cols = lax.broadcasted_iota(jnp.int32, (n, n), 1)
    scores = jnp.where(rows >= cols, dot(g, v, 1, 1), 0.0).astype(BF16)
    hi, lo = entering(par_ref[0], 1, hd, half, *ends)
    total = dot(scores, k, 1, 0) + (dot(g, hi, 1, 1) + dot(g, lo, 1, 1))
    qo_ref[...] = (factor * total).astype(BF16)
    hi, lo = entering(par_ref[0], 0, hd, half, *ends)
    total = dot(scores, q, 0, 0) + (dot(v, hi, 1, 1) + dot(v, lo, 1, 1))
    ko_ref[...] = (factor * total).astype(BF16)


def others(factor, par, q, k, v, g, ends):
    n, cols = q.shape
    spec = pl.BlockSpec((n, DH), lambda h: (0, h))
    held = [pl.BlockSpec(x.shape, lambda h, d=x.ndim: (0,) * d) for x in ends]
    out = jax.ShapeDtypeStruct(q.shape, BF16)
    return call(
        functools.partial(others_kernel, factor, cols // DH // 2),
        grid=(cols // DH,),
        in_specs=[SMEM] + [spec] * 4 + held,
        out_specs=[spec] * 2,
        out_shape=[out] * 2,
        name="others",
    )(par, q, k, v, g, *ends)


def piece_kernel(count, offs_ref, subs_ref, a_ref, b_ref, *refs):
    own, theirs = refs[:count], refs[count : 2 * count]
    outs, (x, y, at, bt, sems) = refs[2 * count : -5], refs[-5:]
    step, steps = pl.program_id(0), pl.num_programs(0)
    slot = lax.rem(step, 2)

    def fetch(k, to):
        for i in range(count):

            @pl.when(offs_ref[k] == i)
            def _():
                for j, (src, dst) in enumerate(((own, x), (theirs, y))):
                    pltpu.make_async_copy(
                        src[i].at[subs_ref[k]], dst.at[to], sems.at[j, to]
                    ).start()

    @pl.when(step == 0)
    def _():
        fetch(0, 0)

    @pl.when(step + 1 < steps)
    def _():
        fetch(step + 1, 1 - slot)

    @pl.when(step == 0)
    def _():
        at[...] = a_ref[...].T
        bt[...] = b_ref[...].T

    for j, (src, dst) in enumerate(((own, x), (theirs, y))):
        pltpu.make_async_copy(src[0].at[0], dst.at[slot], sems.at[j, slot]).wait()
    total = dot(at[...], x[slot], 1, 0) + dot(bt[...], y[slot], 1, 0)
    for i, out_ref in enumerate(outs):

        @pl.when(step == i)
        def _():
            out_ref[...] = total.astype(out_ref.dtype)


def pieces(dtype, offs, subs, a, b, own, theirs):
    steps = offs.shape[0]
    count = len(own)
    _, n, width = own[0].shape
    cols = a.shape[1]
    return call(
        functools.partial(piece_kernel, count),
        grid=(steps,),
        in_specs=[SMEM] * 2 + [VMEM] * 2 + [ANY] * (2 * count),
        out_specs=[VMEM] * steps,
        out_shape=[jax.ShapeDtypeStruct((cols, width), dtype)] * steps,
        scratch_shapes=[
            pltpu.VMEM((2, n, width), BF16),
            pltpu.VMEM((2, n, width), BF16),
            pltpu.VMEM((cols, n), BF16),
            pltpu.VMEM((cols, n), BF16),
            pltpu.SemaphoreType.DMA((2, 2)),
        ],
        name="pieces",
    )(offs, subs, a, b, *own, *theirs)


def weight_kernel(scale, moved_ref, own_ref, out_ref):
    out_ref[...] = (moved_ref[...].astype(F32) + own_ref[...]).T * scale


def finish_weight(scale, moved, own):
    return call(
        functools.partial(weight_kernel, scale),
        in_specs=[VMEM] * 2,
        out_specs=VMEM,
        out_shape=jax.ShapeDtypeStruct(moved.shape[::-1], F32),
        name="finish_weight",
    )(moved, own)


def add_kernel(moved_ref, own_ref, out_ref):
    out_ref[...] = (moved_ref[...].astype(F32) + own_ref[...]).astype(BF16)


def add_own(moved, own):
    return call(
        add_kernel,
        in_specs=[VMEM] * 2,
        out_specs=VMEM,
        out_shape=jax.ShapeDtypeStruct(moved.shape, BF16),
        name="add_own",
    )(moved, own)


def arrange_kernel(per, head_ref, which_ref, *refs):
    count = which_ref.shape[0]
    outs, sems = refs[-3:-1], refs[-1]
    rows = refs[0].shape[0]

    def copies(s):
        p = which_ref[s]
        at = (p // per // 2, pl.ds((p % per) * rows, rows))
        pair = [
            pltpu.make_async_copy(refs[j * count + s], outs[j].at[at], sems.at[j, s])
            for j in range(2)
        ]
        return pair, (p // per) % 2 == head_ref[0] % 2

    for act in ("start", "wait"):
        for s in range(count):
            pair, needed = copies(s)

            @pl.when(needed)
            def _():
                for c in pair:
                    getattr(c, act)()


def arrange(per, n_head, head, which, blocks, lent):
    rows, cols = blocks[0].shape
    count = len(blocks)
    out = jax.ShapeDtypeStruct((n_head // 2, per * rows, cols), BF16)
    return call(
        functools.partial(arrange_kernel, per),
        in_specs=[SMEM] * 2 + [ANY] * (2 * count),
        out_specs=[VMEM] * 2,
        out_shape=[out] * 2,
        scratch_shapes=[pltpu.SemaphoreType.DMA((2, count))],
        name="arrange",
    )(head, which, *blocks, *lent)


def block_product(at_ref, x_ref, y_ref, w_ref, wy_ref):
    at = at_ref[0] // 2
    return dot(x_ref[...], w_ref[at], 1, 1) + dot(y_ref[...], wy_ref[at], 1, 1)


def part_kernel(at_ref, x_ref, y_ref, w_ref, wy_ref, *refs):
    total = block_product(at_ref, x_ref, y_ref, w_ref, wy_ref)
    for got in refs[:-1]:
        total = total + got[...].astype(F32)
    refs[-1][...] = total.astype(BF16)


def head_part(at, x, y, w, wy, got=()):
    return call(
        part_kernel,
        in_specs=[SMEM] + [VMEM] * (4 + len(got)),
        out_specs=VMEM,
        out_shape=jax.ShapeDtypeStruct((x.shape[0], w.shape[1]), BF16),
        name="head_part",
    )(at, x, y, w, wy, *got)


def join_kernel(per, par_ref, at_ref, x_ref, y_ref, w_ref, wy_ref, *refs):
    total = block_product(at_ref, x_ref, y_ref, w_ref, wy_ref)
    for got in refs[:-2]:
        total = total + got[...].astype(F32)
    other_ref, out_ref = refs[-2:]
    rows = other_ref.shape[1] // per
    both = (total.astype(BF16), other_ref[...])
    for k in range(2):

        @pl.when(par_ref[0] == k)
        def _():
            for i in range(per):
                at = slice(i * rows, (i + 1) * rows)
                for j in range(2):
                    to = (2 * i + j) * rows
                    out_ref[:, to : to + rows] = both[j ^ k][:, at]


def join(par, at, per, x, y, w, wy, got, other):
    return call(
        functools.partial(join_kernel, per),
        in_specs=[SMEM] * 2 + [VMEM] * (5 + len(got)),
        out_specs=VMEM,
        out_shape=jax.ShapeDtypeStruct((x.shape[0], 2 * other.shape[1]), BF16),
        name="join",
    )(par, at, x, y, w, wy, *got, other)


def after(x, *earlier):
    return lax.optimization_barrier((x, *earlier))[0]


def local(queries, keys, values, out_grad, inputs, value_weight):
    length, cols = queries.shape
    n_ctx, n_head = lax.axis_size("ctx"), lax.axis_size("head")
    pairs = n_ctx // 2
    ctx, head = lax.axis_index("ctx"), lax.axis_index("head")
    parity, pair = ctx % 2, ctx // 2
    par = parity.astype(jnp.int32).reshape(1)
    factor = 1.0 / math.sqrt(DH * length * n_ctx)
    lines = [[2 * i + k for i in range(pairs)] for k in range(2)]
    def partner(x):
        return lax.ppermute(x, "ctx", [(i, i ^ 1) for i in range(n_ctx)])

    def across(x, bit):
        return lax.ppermute(x, "head", [(i, i ^ bit) for i in range(n_head)])

    order = list(range(0, pairs, 2)) + list(range(1, pairs, 2))[::-1]
    place = [order.index(i) for i in range(pairs)]
    moves = [
        (2 * order[i] + k, 2 * order[(i + 1) % pairs] + k)
        for i in range(pairs)
        for k in range(2)
    ]
    spot = jnp.asarray(place, jnp.int32)[pair]
    steps = jnp.arange(pairs, dtype=jnp.int32)

    def ring(x):
        return lax.ppermute(x, "ctx", moves)

    keep, send, near16 = states(par, queries, keys, values, out_grad)
    their_half = partner(send)
    line = pair.astype(jnp.int32).reshape(1)

    per = n_ctx // n_head // 2
    own, theirs = split(after(par, send), inputs, per)
    vi, keys_too = inside(after(queries, own), keys, out_grad)
    blocks = [value_weight, ring(after(value_weight, send))]
    own, theirs = [own], [partner(after(theirs, their_half))]

    offered = offer(line, after(keep, vi), their_half, pairs)
    every = lax.all_to_all(
        offered, "ctx", split_axis=0, concat_axis=0, axis_index_groups=lines
    )
    far, send_far = far_states(line, every, near16)
    ends = (far, partner(send_far), their_half)
    mine = finish_value(factor, par, keys_too, vi, ends)
    other = partner(mine)
    theirs = [after(theirs[0], mine)]
    query_grad, key_grad = others(
        factor, par, queries, keys, after(values, mine), out_grad, ends
    )
    for _ in range(2, pairs):
        blocks.append(ring(after(blocks[-1], mine)))
    lent = [across(after(x, mine), 1) for x in blocks[:-1]]
    mine_too = across(mine, 1)

    offsets = [0]
    bit = n_head // 2
    while bit:
        own = own + [across(r, bit) for r in own]
        theirs = theirs + [across(r, bit) for r in theirs]
        offsets = offsets + [o ^ bit for o in offsets]
        bit //= 2
    own = [own[offsets.index(i)] for i in range(n_head)]
    theirs = [theirs[offsets.index(i)] for i in range(n_head)]

    which = jnp.asarray(order, jnp.int32)[(spot - 1 - steps) % pairs]
    offs, subs = (which // per) ^ head, which % per
    vals = (after(mine, query_grad), other, own, theirs)
    (total,) = pieces(BF16, offs[:1], subs[:1], *vals)
    moved = ring(total)
    other_too = across(after(other, total), 1)
    vals = (after(mine, other_too), other, own, theirs)
    rest = pieces(F32, offs[1:], subs[1:], *vals)
    lent.append(across(after(blocks[-1], rest[0]), 1))

    here = head.astype(jnp.int32).reshape(1)
    held = jnp.asarray(order, jnp.int32)[(spot - steps) % pairs]

    def summed_parts(x, y):
        sent = [
            head_part(here ^ off, x, y, weight, borrowed)
            for off in range(2, n_head, 2)
        ]
        return sent[-1], [across(x, 2 * i + 2) for i, x in enumerate(sent)]

    total = add_own(moved, rest[0])
    moved = ring(total)
    weight, borrowed = arrange(
        per, n_head, here, held, [after(blocks[0], total)] + blocks[1:], lent
    )
    token, got_other = summed_parts(other, other_too)
    token, got_mine = summed_parts(after(mine, token), mine_too)
    for i in range(1, pairs - 2):
        total = add_own(moved, after(rest[i], token))
        moved = ring(total)
    part = head_part(here, after(other, total), other_too, weight, borrowed, got_other)
    swapped = partner(part)
    weight_grad = finish_weight(
        1.0 / math.sqrt(length * n_ctx), moved, after(rest[-1], part)
    )
    mine = after(mine, weight_grad)
    input_grad = join(
        par, here, per, mine, mine_too, weight, borrowed, got_mine, swapped
    )
    return (query_grad, key_grad, input_grad, weight_grad)


def solution(mesh):
    spec = P("ctx", "head")
    return jax.shard_map(
        local, mesh=mesh, in_specs=(spec,) * 6, out_specs=(spec,) * 4, check_vma=False
    )
```

```python
import functools
import math

import jax
import jax.numpy as jnp
from jax import lax
from jax.experimental import pallas as pl
from jax.experimental.pallas import tpu as pltpu
from jax.sharding import PartitionSpec as P

DH = 128
F32, BF16 = jnp.float32, jnp.bfloat16
VMEM = pl.BlockSpec(memory_space=pltpu.VMEM)
SMEM = pl.BlockSpec(memory_space=pltpu.SMEM)
ANY = pl.BlockSpec(memory_space=pl.ANY)


def dot(a, b, ca, cb):
    return lax.dot_general(a, b, (((ca,), (cb,)), ((), ())), preferred_element_type=F32)


def call(kernel, vmem=16, **kw):
    hint = pl.CostEstimate(flops=1, bytes_accessed=1, transcendentals=0)
    params = pltpu.CompilerParams(vmem_limit_bytes=vmem * 2**20)
    return pl.pallas_call(kernel, cost_estimate=hint, compiler_params=params, **kw)


def states_kernel(par_ref, *refs):
    arrays, (keep_ref, send_ref, near_ref), bufs, sems = (
        refs[:4],
        refs[4:7],
        refs[7:11],
        refs[11],
    )
    heads = arrays[0].shape[1] // DH
    half = heads // 2

    def copy(j, hd):
        at = pl.ds(hd * DH, DH)
        return pltpu.make_async_copy(
            arrays[j].at[:, at], bufs[j].at[:, at], sems.at[j, hd]
        )

    for hd in range(heads):
        for j in range(4):
            copy(j, hd).start()
    for hd in range(heads):
        at = slice(hd * DH, (hd + 1) * DH)
        for j in range(4):
            copy(j, hd).wait()
        for kind, (a, b) in enumerate(((0, 3), (1, 2))):
            s = dot(bufs[a][:, at], bufs[b][:, at], 0, 0)
            own = par_ref[0] == hd // half

            @pl.when(own)
            def _():
                keep_ref[kind, hd % half] = s
                near_ref[kind, hd % half] = s.astype(BF16)

            @pl.when(jnp.logical_not(own))
            def _():
                send_ref[kind, hd % half] = s.astype(BF16)


def states(par, *arrays):
    n, cols = arrays[0].shape
    heads = cols // DH
    shape = (2, heads // 2, DH, DH)
    return call(
        states_kernel,
        vmem=60,
        in_specs=[SMEM] + [pl.BlockSpec(memory_space=pltpu.HBM)] * 4,
        out_specs=[VMEM] * 3,
        out_shape=[jax.ShapeDtypeStruct(shape, d) for d in (F32, BF16, BF16)],
        scratch_shapes=[pltpu.VMEM((n, cols), BF16)] * 4
        + [pltpu.SemaphoreType.DMA((4, heads))],
        name="states",
    )(par, *arrays)


def split_kernel(per, par_ref, x_ref, own_ref, theirs_ref, sems):
    width = own_ref.shape[2]
    for k in range(2):

        @pl.when(par_ref[0] == k)
        def _():
            copies = []
            for i in range(per):
                for j, out_ref in enumerate((own_ref, theirs_ref)):
                    at = (2 * i + (k ^ j)) * width
                    if width % 128:
                        out_ref[i] = x_ref[:, at : at + width]
                    else:
                        src = x_ref.at[:, pl.ds(at, width)]
                        copies.append(
                            pltpu.make_async_copy(src, out_ref.at[i], sems.at[j, i])
                        )
            for c in copies:
                c.start()
            for c in copies:
                c.wait()


def split(par, x, per):
    width = x.shape[1] // (2 * per)
    out = jax.ShapeDtypeStruct((per, x.shape[0], width), x.dtype)
    place = VMEM if width % 128 else pl.BlockSpec(memory_space=pltpu.HBM)
    return call(
        functools.partial(split_kernel, per),
        in_specs=[SMEM, place],
        out_specs=[VMEM] * 2,
        out_shape=[out, out],
        scratch_shapes=[pltpu.SemaphoreType.DMA((2, per))],
        name="split",
    )(par, x)


def inside_kernel(*refs):
    arrays, (out_ref, k_ref), bufs, sems = refs[:3], refs[3:5], refs[5:8], refs[8]
    n, cols = out_ref.shape
    heads = cols // DH

    def copy(j, hd):
        at = pl.ds(hd * DH, DH)
        return pltpu.make_async_copy(
            arrays[j].at[:, at], bufs[j].at[:, at], sems.at[j, hd]
        )

    for hd in range(heads):
        for j in range(3):
            copy(j, hd).start()
    rows = lax.broadcasted_iota(jnp.int32, (n, n), 0)
    causal = rows >= lax.broadcasted_iota(jnp.int32, (n, n), 1)
    for hd in range(heads):
        at = slice(hd * DH, (hd + 1) * DH)
        for j in range(3):
            copy(j, hd).wait()
        q, k, g = (x[:, at] for x in bufs)
        scores = jnp.where(causal, dot(q, k, 1, 1), 0.0).astype(BF16)
        out_ref[:, at] = dot(scores, g, 0, 0)
        k_ref[:, at] = k


def inside(*arrays):
    n, cols = arrays[0].shape
    return call(
        inside_kernel,
        in_specs=[pl.BlockSpec(memory_space=pltpu.HBM)] * 3,
        out_specs=[VMEM] * 2,
        out_shape=[jax.ShapeDtypeStruct((n, cols), d) for d in (F32, BF16)],
        scratch_shapes=[pltpu.VMEM((n, cols), BF16)] * 3
        + [pltpu.SemaphoreType.DMA((3, cols // DH))],
        name="inside",
    )(*arrays)


def offer_kernel(pair_ref, keep_ref, got_ref, out_ref):
    sums = [(keep_ref[k] + got_ref[k].astype(F32)).astype(BF16) for k in range(2)]
    for p in range(out_ref.shape[0]):
        out_ref[p] = jnp.where(p < pair_ref[0], sums[0], sums[1])


def offer(pair, keep, got, pairs):
    return call(
        offer_kernel,
        in_specs=[SMEM, VMEM, VMEM],
        out_specs=VMEM,
        out_shape=jax.ShapeDtypeStruct((pairs, *keep.shape[1:]), BF16),
        name="offer",
    )(pair, keep, got)


def far_kernel(pair_ref, every_ref, near_ref, out_ref, send_ref):
    for kind in range(2):
        total = jnp.zeros(out_ref.shape[1:], F32)
        for p in range(every_ref.shape[0]):
            reached = p > pair_ref[0] if kind == 0 else p < pair_ref[0]
            total = total + jnp.where(reached, every_ref[p].astype(F32), 0.0)
        out_ref[kind] = total
        send_ref[0, kind] = total.astype(BF16)
        send_ref[1, kind] = near_ref[kind]


def far_states(pair, every, near):
    shape = (2, *every.shape[1:])
    return call(
        far_kernel,
        in_specs=[SMEM, VMEM, VMEM],
        out_specs=[VMEM] * 2,
        out_shape=[
            jax.ShapeDtypeStruct(shape, F32),
            jax.ShapeDtypeStruct((2, *shape), BF16),
        ],
        name="far",
    )(pair, every, near)


def entering(par, kind, hd, half, far, got, near):
    mine = par == hd // half
    i = hd % half
    outer = jnp.where(mine, far[kind, i], got[0, kind, i].astype(F32))
    close = jnp.where(mine, near[kind, i].astype(F32), got[1, kind, i].astype(F32))
    total = outer + jnp.where(par == kind, close, 0.0)
    hi = total.astype(BF16)
    return hi, (total - hi.astype(F32)).astype(BF16)


def value_kernel(factor, half, par_ref, k_ref, vi_ref, *refs):
    ends, out_ref = refs[:-1], refs[-1]
    for hd in range(2 * half):
        at = slice(hd * DH, (hd + 1) * DH)
        hi, lo = entering(par_ref[0], 0, hd, half, *ends)
        k = k_ref[:, at]
        total = vi_ref[:, at] + (dot(k, hi, 1, 0) + dot(k, lo, 1, 0))
        out_ref[:, at] = (factor * total).astype(BF16)


def finish_value(factor, par, k, vi, ends):
    return call(
        functools.partial(value_kernel, factor, k.shape[1] // DH // 2),
        in_specs=[SMEM] + [VMEM] * (2 + len(ends)),
        out_specs=VMEM,
        out_shape=jax.ShapeDtypeStruct(k.shape, BF16),
        name="finish_value",
    )(par, k, vi, *ends)


def others_kernel(factor, half, par_ref, q_ref, k_ref, v_ref, g_ref, *refs):
    ends, (qo_ref, ko_ref) = refs[:-2], refs[-2:]
    hd = pl.program_id(0)
    q, k, v, g = q_ref[...], k_ref[...], v_ref[...], g_ref[...]
    n = q.shape[0]
    rows = lax.broadcasted_iota(jnp.int32, (n, n), 0)
    cols = lax.broadcasted_iota(jnp.int32, (n, n), 1)
    scores = jnp.where(rows >= cols, dot(g, v, 1, 1), 0.0).astype(BF16)
    hi, lo = entering(par_ref[0], 1, hd, half, *ends)
    total = dot(scores, k, 1, 0) + (dot(g, hi, 1, 1) + dot(g, lo, 1, 1))
    qo_ref[...] = (factor * total).astype(BF16)
    hi, lo = entering(par_ref[0], 0, hd, half, *ends)
    total = dot(scores, q, 0, 0) + (dot(v, hi, 1, 1) + dot(v, lo, 1, 1))
    ko_ref[...] = (factor * total).astype(BF16)


def others(factor, par, q, k, v, g, ends):
    n, cols = q.shape
    spec = pl.BlockSpec((n, DH), lambda h: (0, h))
    held = [pl.BlockSpec(x.shape, lambda h, d=x.ndim: (0,) * d) for x in ends]
    out = jax.ShapeDtypeStruct(q.shape, BF16)
    return call(
        functools.partial(others_kernel, factor, cols // DH // 2),
        grid=(cols // DH,),
        in_specs=[SMEM] + [spec] * 4 + held,
        out_specs=[spec] * 2,
        out_shape=[out] * 2,
        name="others",
    )(par, q, k, v, g, *ends)


def piece_kernel(count, offs_ref, subs_ref, a_ref, b_ref, *refs):
    own, theirs = refs[:count], refs[count : 2 * count]
    outs, (x, y, at, bt, sems) = refs[2 * count : -5], refs[-5:]
    step, steps = pl.program_id(0), pl.num_programs(0)
    slot = lax.rem(step, 2)

    def fetch(k, to):
        for i in range(count):

            @pl.when(offs_ref[k] == i)
            def _():
                for j, (src, dst) in enumerate(((own, x), (theirs, y))):
                    pltpu.make_async_copy(
                        src[i].at[subs_ref[k]], dst.at[to], sems.at[j, to]
                    ).start()

    @pl.when(step == 0)
    def _():
        fetch(0, 0)

    @pl.when(step + 1 < steps)
    def _():
        fetch(step + 1, 1 - slot)

    @pl.when(step == 0)
    def _():
        at[...] = a_ref[...].T
        bt[...] = b_ref[...].T

    for j, (src, dst) in enumerate(((own, x), (theirs, y))):
        pltpu.make_async_copy(src[0].at[0], dst.at[slot], sems.at[j, slot]).wait()
    total = dot(at[...], x[slot], 1, 0) + dot(bt[...], y[slot], 1, 0)
    for i, out_ref in enumerate(outs):

        @pl.when(step == i)
        def _():
            out_ref[...] = total.astype(out_ref.dtype)


def pieces(dtype, offs, subs, a, b, own, theirs):
    steps = offs.shape[0]
    count = len(own)
    _, n, width = own[0].shape
    cols = a.shape[1]
    return call(
        functools.partial(piece_kernel, count),
        grid=(steps,),
        in_specs=[SMEM] * 2 + [VMEM] * 2 + [ANY] * (2 * count),
        out_specs=[VMEM] * steps,
        out_shape=[jax.ShapeDtypeStruct((cols, width), dtype)] * steps,
        scratch_shapes=[
            pltpu.VMEM((2, n, width), BF16),
            pltpu.VMEM((2, n, width), BF16),
            pltpu.VMEM((cols, n), BF16),
            pltpu.VMEM((cols, n), BF16),
            pltpu.SemaphoreType.DMA((2, 2)),
        ],
        name="pieces",
    )(offs, subs, a, b, *own, *theirs)


def weight_kernel(scale, moved_ref, own_ref, out_ref):
    out_ref[...] = (moved_ref[...].astype(F32) + own_ref[...]).T * scale


def finish_weight(scale, moved, own):
    return call(
        functools.partial(weight_kernel, scale),
        in_specs=[VMEM] * 2,
        out_specs=VMEM,
        out_shape=jax.ShapeDtypeStruct(moved.shape[::-1], F32),
        name="finish_weight",
    )(moved, own)


def add_kernel(moved_ref, own_ref, out_ref):
    out_ref[...] = (moved_ref[...].astype(F32) + own_ref[...]).astype(BF16)


def add_own(moved, own):
    return call(
        add_kernel,
        in_specs=[VMEM] * 2,
        out_specs=VMEM,
        out_shape=jax.ShapeDtypeStruct(moved.shape, BF16),
        name="add_own",
    )(moved, own)


def arrange_kernel(per, head_ref, which_ref, *refs):
    count = which_ref.shape[0]
    outs, sems = refs[-3:-1], refs[-1]
    rows = refs[0].shape[0]

    def copies(s):
        p = which_ref[s]
        at = (p // per // 2, pl.ds((p % per) * rows, rows))
        pair = [
            pltpu.make_async_copy(refs[j * count + s], outs[j].at[at], sems.at[j, s])
            for j in range(2)
        ]
        return pair, (p // per) % 2 == head_ref[0] % 2

    for act in ("start", "wait"):
        for s in range(count):
            pair, needed = copies(s)

            @pl.when(needed)
            def _():
                for c in pair:
                    getattr(c, act)()


def arrange(per, n_head, head, which, blocks, lent):
    rows, cols = blocks[0].shape
    count = len(blocks)
    out = jax.ShapeDtypeStruct((n_head // 2, per * rows, cols), BF16)
    return call(
        functools.partial(arrange_kernel, per),
        in_specs=[SMEM] * 2 + [ANY] * (2 * count),
        out_specs=[VMEM] * 2,
        out_shape=[out] * 2,
        scratch_shapes=[pltpu.SemaphoreType.DMA((2, count))],
        name="arrange",
    )(head, which, *blocks, *lent)


def block_product(at_ref, x_ref, y_ref, w_ref, wy_ref):
    at = at_ref[0] // 2
    return dot(x_ref[...], w_ref[at], 1, 1) + dot(y_ref[...], wy_ref[at], 1, 1)


def part_kernel(at_ref, x_ref, y_ref, w_ref, wy_ref, *refs):
    total = block_product(at_ref, x_ref, y_ref, w_ref, wy_ref)
    for got in refs[:-1]:
        total = total + got[...].astype(F32)
    refs[-1][...] = total.astype(BF16)


def head_part(at, x, y, w, wy, got=()):
    return call(
        part_kernel,
        in_specs=[SMEM] + [VMEM] * (4 + len(got)),
        out_specs=VMEM,
        out_shape=jax.ShapeDtypeStruct((x.shape[0], w.shape[1]), BF16),
        name="head_part",
    )(at, x, y, w, wy, *got)


def join_kernel(per, par_ref, at_ref, x_ref, y_ref, w_ref, wy_ref, *refs):
    total = block_product(at_ref, x_ref, y_ref, w_ref, wy_ref)
    for got in refs[:-2]:
        total = total + got[...].astype(F32)
    other_ref, out_ref = refs[-2:]
    rows = other_ref.shape[1] // per
    both = (total.astype(BF16), other_ref[...])
    for k in range(2):

        @pl.when(par_ref[0] == k)
        def _():
            for i in range(per):
                at = slice(i * rows, (i + 1) * rows)
                for j in range(2):
                    to = (2 * i + j) * rows
                    out_ref[:, to : to + rows] = both[j ^ k][:, at]


def join(par, at, per, x, y, w, wy, got, other):
    return call(
        functools.partial(join_kernel, per),
        in_specs=[SMEM] * 2 + [VMEM] * (5 + len(got)),
        out_specs=VMEM,
        out_shape=jax.ShapeDtypeStruct((x.shape[0], 2 * other.shape[1]), BF16),
        name="join",
    )(par, at, x, y, w, wy, *got, other)


def after(x, *earlier):
    return lax.optimization_barrier((x, *earlier))[0]


def local(queries, keys, values, out_grad, inputs, value_weight):
    length, cols = queries.shape
    n_ctx, n_head = lax.axis_size("ctx"), lax.axis_size("head")
    pairs = n_ctx // 2
    ctx, head = lax.axis_index("ctx"), lax.axis_index("head")
    parity, pair = ctx % 2, ctx // 2
    par = parity.astype(jnp.int32).reshape(1)
    factor = 1.0 / math.sqrt(DH * length * n_ctx)
    lines = [[2 * i + k for i in range(pairs)] for k in range(2)]
    def partner(x):
        return lax.ppermute(x, "ctx", [(i, i ^ 1) for i in range(n_ctx)])

    def across(x, bit):
        return lax.ppermute(x, "head", [(i, i ^ bit) for i in range(n_head)])

    order = list(range(0, pairs, 2)) + list(range(1, pairs, 2))[::-1]
    place = [order.index(i) for i in range(pairs)]
    moves = [
        (2 * order[i] + k, 2 * order[(i + 1) % pairs] + k)
        for i in range(pairs)
        for k in range(2)
    ]
    spot = jnp.asarray(place, jnp.int32)[pair]
    steps = jnp.arange(pairs, dtype=jnp.int32)

    def ring(x):
        return lax.ppermute(x, "ctx", moves)

    keep, send, near16 = states(par, queries, keys, values, out_grad)
    their_half = partner(send)
    line = pair.astype(jnp.int32).reshape(1)

    per = n_ctx // n_head // 2
    own, theirs = split(after(par, send), inputs, per)
    blocks = [value_weight, ring(after(value_weight, send))]
    own, theirs = [own], [partner(after(theirs, their_half))]

    offered = offer(line, keep, their_half, pairs)
    every = lax.all_to_all(
        offered, "ctx", split_axis=0, concat_axis=0, axis_index_groups=lines
    )
    far, send_far = far_states(line, every, near16)
    ends = (far, partner(send_far), their_half)
    vi, keys_too = inside(after(queries, send_far), keys, out_grad)
    theirs = [after(theirs[0], send_far)]
    mine = finish_value(factor, par, keys_too, vi, ends)
    other = partner(mine)
    query_grad, key_grad = others(
        factor, par, queries, keys, after(values, mine), out_grad, ends
    )
    token = send_far
    for _ in range(2, pairs):
        blocks.append(ring(after(blocks[-1], token)))
        token = mine
    lent = [across(after(x, mine), 1) for x in blocks[:-1]]
    mine_too = across(mine, 1)

    offsets = [0]
    bit = n_head // 2
    while bit:
        own = own + [across(r, bit) for r in own]
        theirs = theirs + [across(r, bit) for r in theirs]
        offsets = offsets + [o ^ bit for o in offsets]
        bit //= 2
    own = [own[offsets.index(i)] for i in range(n_head)]
    theirs = [theirs[offsets.index(i)] for i in range(n_head)]

    which = jnp.asarray(order, jnp.int32)[(spot - 1 - steps) % pairs]
    offs, subs = (which // per) ^ head, which % per

    def piece(dtype, step, token):
        at = (offs[step : step + 1], subs[step : step + 1])
        return pieces(dtype, *at, after(mine, token), other, own, theirs)[0]

    total = piece(BF16, 0, query_grad)
    moved = ring(total)
    other_too = across(after(other, total), 1)
    local_part = piece(F32, 1, other_too)
    lent.append(across(after(blocks[-1], local_part), 1))

    here = head.astype(jnp.int32).reshape(1)
    held = jnp.asarray(order, jnp.int32)[(spot - steps) % pairs]

    def summed_parts(x, y):
        sent = [
            head_part(here ^ off, x, y, weight, borrowed)
            for off in range(2, n_head, 2)
        ]
        return sent[-1], [across(x, 2 * i + 2) for i, x in enumerate(sent)]

    total = add_own(moved, local_part)
    moved = ring(total)
    weight, borrowed = arrange(
        per, n_head, here, held, [after(blocks[0], total)] + blocks[1:], lent
    )
    token, got_other = summed_parts(other, other_too)
    token, got_mine = summed_parts(after(mine, token), mine_too)
    for step in range(2, pairs - 1):
        total = add_own(moved, piece(F32, step, token))
        moved = ring(total)
        token = total
    local_part = piece(F32, pairs - 1, token)
    part = head_part(
        here, after(other, local_part), other_too, weight, borrowed, got_other
    )
    swapped = partner(part)
    weight_grad = finish_weight(
        1.0 / math.sqrt(length * n_ctx), moved, after(local_part, part)
    )
    mine = after(mine, weight_grad)
    input_grad = join(
        par, here, per, mine, mine_too, weight, borrowed, got_mine, swapped
    )
    return (query_grad, key_grad, input_grad, weight_grad)


def solution(mesh):
    spec = P("ctx", "head")
    return jax.shard_map(
        local, mesh=mesh, in_specs=(spec,) * 6, out_specs=(spec,) * 4, check_vma=False
    )
```

```python
import functools
import math

import jax
import jax.numpy as jnp
from jax import lax
from jax.experimental import pallas as pl
from jax.experimental.pallas import tpu as pltpu
from jax.sharding import PartitionSpec as P

DH = 128
F32, BF16 = jnp.float32, jnp.bfloat16
VMEM = pl.BlockSpec(memory_space=pltpu.VMEM)
SMEM = pl.BlockSpec(memory_space=pltpu.SMEM)
ANY = pl.BlockSpec(memory_space=pl.ANY)


def dot(a, b, ca, cb):
    return lax.dot_general(a, b, (((ca,), (cb,)), ((), ())), preferred_element_type=F32)


def call(kernel, vmem=16, **kw):
    hint = pl.CostEstimate(flops=1, bytes_accessed=1, transcendentals=0)
    params = pltpu.CompilerParams(vmem_limit_bytes=vmem * 2**20)
    return pl.pallas_call(kernel, cost_estimate=hint, compiler_params=params, **kw)


def states_kernel(par_ref, *refs):
    arrays, (keep_ref, send_ref, near_ref), bufs, sems = (
        refs[:4],
        refs[4:7],
        refs[7:11],
        refs[11],
    )
    heads = arrays[0].shape[1] // DH
    half = heads // 2

    def copy(j, hd):
        at = pl.ds(hd * DH, DH)
        return pltpu.make_async_copy(
            arrays[j].at[:, at], bufs[j].at[:, at], sems.at[j, hd]
        )

    for hd in range(heads):
        for j in range(4):
            copy(j, hd).start()
    for hd in range(heads):
        at = slice(hd * DH, (hd + 1) * DH)
        for j in range(4):
            copy(j, hd).wait()
        for kind, (a, b) in enumerate(((0, 3), (1, 2))):
            s = dot(bufs[a][:, at], bufs[b][:, at], 0, 0)
            own = par_ref[0] == hd // half

            @pl.when(own)
            def _():
                keep_ref[kind, hd % half] = s
                near_ref[kind, hd % half] = s.astype(BF16)

            @pl.when(jnp.logical_not(own))
            def _():
                send_ref[kind, hd % half] = s.astype(BF16)


def states(par, *arrays):
    n, cols = arrays[0].shape
    heads = cols // DH
    shape = (2, heads // 2, DH, DH)
    return call(
        states_kernel,
        vmem=60,
        in_specs=[SMEM] + [pl.BlockSpec(memory_space=pltpu.HBM)] * 4,
        out_specs=[VMEM] * 3,
        out_shape=[jax.ShapeDtypeStruct(shape, d) for d in (F32, BF16, BF16)],
        scratch_shapes=[pltpu.VMEM((n, cols), BF16)] * 4
        + [pltpu.SemaphoreType.DMA((4, heads))],
        name="states",
    )(par, *arrays)


def split_kernel(per, par_ref, x_ref, own_ref, theirs_ref, sems):
    width = own_ref.shape[2]
    for k in range(2):

        @pl.when(par_ref[0] == k)
        def _():
            copies = []
            for i in range(per):
                for j, out_ref in enumerate((own_ref, theirs_ref)):
                    at = (2 * i + (k ^ j)) * width
                    if width % 128:
                        out_ref[i] = x_ref[:, at : at + width]
                    else:
                        src = x_ref.at[:, pl.ds(at, width)]
                        copies.append(
                            pltpu.make_async_copy(src, out_ref.at[i], sems.at[j, i])
                        )
            for c in copies:
                c.start()
            for c in copies:
                c.wait()


def split(par, x, per):
    width = x.shape[1] // (2 * per)
    out = jax.ShapeDtypeStruct((per, x.shape[0], width), x.dtype)
    place = VMEM if width % 128 else pl.BlockSpec(memory_space=pltpu.HBM)
    return call(
        functools.partial(split_kernel, per),
        in_specs=[SMEM, place],
        out_specs=[VMEM] * 2,
        out_shape=[out, out],
        scratch_shapes=[pltpu.SemaphoreType.DMA((2, per))],
        name="split",
    )(par, x)


def inside_kernel(*refs):
    arrays, out_ref, bufs, (made, sems, done) = refs[:3], refs[3], refs[4:7], refs[7:]
    n, cols = out_ref.shape
    heads = cols // DH

    def at(hd):
        return pl.ds(hd * DH, DH)

    def copy(j, hd):
        return pltpu.make_async_copy(
            arrays[j].at[:, at(hd)], bufs[j].at[:, at(hd)], sems.at[j, hd]
        )

    def give(hd):
        return pltpu.make_async_copy(
            made.at[:, at(hd)], out_ref.at[:, at(hd)], done.at[hd]
        )

    for hd in range(heads):
        for j in range(3):
            copy(j, hd).start()
    rows = lax.broadcasted_iota(jnp.int32, (n, n), 0)
    causal = rows >= lax.broadcasted_iota(jnp.int32, (n, n), 1)
    for hd in range(heads):
        for j in range(3):
            copy(j, hd).wait()
        q, k, g = (x[:, at(hd)] for x in bufs)
        scores = jnp.where(causal, dot(q, k, 1, 1), 0.0).astype(BF16)
        made[:, at(hd)] = dot(scores, g, 0, 0)
        give(hd).start()
    for hd in range(heads):
        give(hd).wait()


def inside(*arrays):
    n, cols = arrays[0].shape
    heads = cols // DH
    hbm = pl.BlockSpec(memory_space=pltpu.HBM)
    return call(
        inside_kernel,
        in_specs=[hbm] * 3,
        out_specs=hbm,
        out_shape=jax.ShapeDtypeStruct((n, cols), F32),
        scratch_shapes=[pltpu.VMEM((n, cols), BF16)] * 3
        + [
            pltpu.VMEM((n, cols), F32),
            pltpu.SemaphoreType.DMA((3, heads)),
            pltpu.SemaphoreType.DMA((heads,)),
        ],
        name="inside",
    )(*arrays)


def offer_kernel(pair_ref, keep_ref, got_ref, out_ref):
    sums = [(keep_ref[k] + got_ref[k].astype(F32)).astype(BF16) for k in range(2)]
    for p in range(out_ref.shape[0]):
        out_ref[p] = jnp.where(p < pair_ref[0], sums[0], sums[1])


def offer(pair, keep, got, pairs):
    return call(
        offer_kernel,
        in_specs=[SMEM, VMEM, VMEM],
        out_specs=VMEM,
        out_shape=jax.ShapeDtypeStruct((pairs, *keep.shape[1:]), BF16),
        name="offer",
    )(pair, keep, got)


def far_kernel(pair_ref, every_ref, near_ref, out_ref, send_ref):
    for kind in range(2):
        total = jnp.zeros(out_ref.shape[1:], F32)
        for p in range(every_ref.shape[0]):
            reached = p > pair_ref[0] if kind == 0 else p < pair_ref[0]
            total = total + jnp.where(reached, every_ref[p].astype(F32), 0.0)
        out_ref[kind] = total
        send_ref[0, kind] = total.astype(BF16)
        send_ref[1, kind] = near_ref[kind]


def far_states(pair, every, near):
    shape = (2, *every.shape[1:])
    return call(
        far_kernel,
        in_specs=[SMEM, VMEM, VMEM],
        out_specs=[VMEM] * 2,
        out_shape=[
            jax.ShapeDtypeStruct(shape, F32),
            jax.ShapeDtypeStruct((2, *shape), BF16),
        ],
        name="far",
    )(pair, every, near)


def entering(par, kind, hd, half, far, got, near):
    mine = par == hd // half
    i = hd % half
    outer = jnp.where(mine, far[kind, i], got[0, kind, i].astype(F32))
    close = jnp.where(mine, near[kind, i].astype(F32), got[1, kind, i].astype(F32))
    total = outer + jnp.where(par == kind, close, 0.0)
    hi = total.astype(BF16)
    return hi, (total - hi.astype(F32)).astype(BF16)


def value_kernel(factor, half, par_ref, k_any, vi_any, *refs):
    ends, out_ref, k_ref, vi_ref, sems = refs[:-4], *refs[-4:]

    def copies(hd):
        at = pl.ds(hd * DH, DH)
        return [
            pltpu.make_async_copy(src.at[:, at], dst.at[:, at], sems.at[j, hd])
            for j, (src, dst) in enumerate(((k_any, k_ref), (vi_any, vi_ref)))
        ]

    for hd in range(2 * half):
        for c in copies(hd):
            c.start()
    for hd in range(2 * half):
        at = slice(hd * DH, (hd + 1) * DH)
        hi, lo = entering(par_ref[0], 0, hd, half, *ends)
        for c in copies(hd):
            c.wait()
        k = k_ref[:, at]
        total = vi_ref[:, at] + (dot(k, hi, 1, 0) + dot(k, lo, 1, 0))
        out_ref[:, at] = (factor * total).astype(BF16)


def finish_value(factor, par, k, vi, ends):
    heads = k.shape[1] // DH
    return call(
        functools.partial(value_kernel, factor, heads // 2),
        in_specs=[SMEM]
        + [pl.BlockSpec(memory_space=pltpu.HBM)] * 2
        + [VMEM] * len(ends),
        out_specs=VMEM,
        out_shape=jax.ShapeDtypeStruct(k.shape, BF16),
        scratch_shapes=[
            pltpu.VMEM(k.shape, BF16),
            pltpu.VMEM(k.shape, F32),
            pltpu.SemaphoreType.DMA((2, heads)),
        ],
        name="finish_value",
    )(par, k, vi, *ends)


def others_kernel(factor, half, par_ref, q_ref, k_ref, v_ref, g_ref, *refs):
    ends, (qo_ref, ko_ref) = refs[:-2], refs[-2:]
    hd = pl.program_id(0)
    q, k, v, g = q_ref[...], k_ref[...], v_ref[...], g_ref[...]
    n = q.shape[0]
    rows = lax.broadcasted_iota(jnp.int32, (n, n), 0)
    cols = lax.broadcasted_iota(jnp.int32, (n, n), 1)
    scores = jnp.where(rows >= cols, dot(g, v, 1, 1), 0.0).astype(BF16)
    hi, lo = entering(par_ref[0], 1, hd, half, *ends)
    total = dot(scores, k, 1, 0) + (dot(g, hi, 1, 1) + dot(g, lo, 1, 1))
    qo_ref[...] = (factor * total).astype(BF16)
    hi, lo = entering(par_ref[0], 0, hd, half, *ends)
    total = dot(scores, q, 0, 0) + (dot(v, hi, 1, 1) + dot(v, lo, 1, 1))
    ko_ref[...] = (factor * total).astype(BF16)


def others(factor, par, q, k, v, g, ends):
    n, cols = q.shape
    spec = pl.BlockSpec((n, DH), lambda h: (0, h))
    held = [pl.BlockSpec(x.shape, lambda h, d=x.ndim: (0,) * d) for x in ends]
    out = jax.ShapeDtypeStruct(q.shape, BF16)
    return call(
        functools.partial(others_kernel, factor, cols // DH // 2),
        grid=(cols // DH,),
        in_specs=[SMEM] + [spec] * 4 + held,
        out_specs=[spec] * 2,
        out_shape=[out] * 2,
        name="others",
    )(par, q, k, v, g, *ends)


def piece_kernel(count, offs_ref, subs_ref, a_ref, b_ref, *refs):
    own, theirs = refs[:count], refs[count : 2 * count]
    outs, (x, y, at, bt, sems) = refs[2 * count : -5], refs[-5:]
    step, steps = pl.program_id(0), pl.num_programs(0)
    slot = lax.rem(step, 2)

    def fetch(k, to):
        for i in range(count):

            @pl.when(offs_ref[k] == i)
            def _():
                for j, (src, dst) in enumerate(((own, x), (theirs, y))):
                    pltpu.make_async_copy(
                        src[i].at[subs_ref[k]], dst.at[to], sems.at[j, to]
                    ).start()

    @pl.when(step == 0)
    def _():
        fetch(0, 0)

    @pl.when(step + 1 < steps)
    def _():
        fetch(step + 1, 1 - slot)

    @pl.when(step == 0)
    def _():
        at[...] = a_ref[...].T
        bt[...] = b_ref[...].T

    for j, (src, dst) in enumerate(((own, x), (theirs, y))):
        pltpu.make_async_copy(src[0].at[0], dst.at[slot], sems.at[j, slot]).wait()
    total = dot(at[...], x[slot], 1, 0) + dot(bt[...], y[slot], 1, 0)
    for i, out_ref in enumerate(outs):

        @pl.when(step == i)
        def _():
            out_ref[...] = total.astype(out_ref.dtype)


def pieces(dtype, offs, subs, a, b, own, theirs):
    steps = offs.shape[0]
    count = len(own)
    _, n, width = own[0].shape
    cols = a.shape[1]
    return call(
        functools.partial(piece_kernel, count),
        grid=(steps,),
        in_specs=[SMEM] * 2 + [VMEM] * 2 + [ANY] * (2 * count),
        out_specs=[VMEM] * steps,
        out_shape=[jax.ShapeDtypeStruct((cols, width), dtype)] * steps,
        scratch_shapes=[
            pltpu.VMEM((2, n, width), BF16),
            pltpu.VMEM((2, n, width), BF16),
            pltpu.VMEM((cols, n), BF16),
            pltpu.VMEM((cols, n), BF16),
            pltpu.SemaphoreType.DMA((2, 2)),
        ],
        name="pieces",
    )(offs, subs, a, b, *own, *theirs)


def weight_kernel(scale, moved_ref, own_ref, out_ref):
    out_ref[...] = (moved_ref[...].astype(F32) + own_ref[...]).T * scale


def finish_weight(scale, moved, own):
    return call(
        functools.partial(weight_kernel, scale),
        in_specs=[VMEM] * 2,
        out_specs=VMEM,
        out_shape=jax.ShapeDtypeStruct(moved.shape[::-1], F32),
        name="finish_weight",
    )(moved, own)


def add_kernel(moved_ref, own_ref, out_ref):
    out_ref[...] = (moved_ref[...].astype(F32) + own_ref[...]).astype(BF16)


def add_own(moved, own):
    return call(
        add_kernel,
        in_specs=[VMEM] * 2,
        out_specs=VMEM,
        out_shape=jax.ShapeDtypeStruct(moved.shape, BF16),
        name="add_own",
    )(moved, own)


def arrange_kernel(per, head_ref, which_ref, *refs):
    count = which_ref.shape[0]
    outs, sems = refs[-3:-1], refs[-1]
    rows = refs[0].shape[0]

    def copies(s):
        p = which_ref[s]
        at = (p // per // 2, pl.ds((p % per) * rows, rows))
        pair = [
            pltpu.make_async_copy(refs[j * count + s], outs[j].at[at], sems.at[j, s])
            for j in range(2)
        ]
        return pair, (p // per) % 2 == head_ref[0] % 2

    for act in ("start", "wait"):
        for s in range(count):
            pair, needed = copies(s)

            @pl.when(needed)
            def _():
                for c in pair:
                    getattr(c, act)()


def arrange(per, n_head, head, which, blocks, lent):
    rows, cols = blocks[0].shape
    count = len(blocks)
    out = jax.ShapeDtypeStruct((n_head // 2, per * rows, cols), BF16)
    return call(
        functools.partial(arrange_kernel, per),
        in_specs=[SMEM] * 2 + [ANY] * (2 * count),
        out_specs=[VMEM] * 2,
        out_shape=[out] * 2,
        scratch_shapes=[pltpu.SemaphoreType.DMA((2, count))],
        name="arrange",
    )(head, which, *blocks, *lent)


def block_product(at_ref, x_ref, y_ref, w_ref, wy_ref):
    at = at_ref[0] // 2
    return dot(x_ref[...], w_ref[at], 1, 1) + dot(y_ref[...], wy_ref[at], 1, 1)


def part_kernel(at_ref, x_ref, y_ref, w_ref, wy_ref, *refs):
    total = block_product(at_ref, x_ref, y_ref, w_ref, wy_ref)
    for got in refs[:-1]:
        total = total + got[...].astype(F32)
    refs[-1][...] = total.astype(BF16)


def head_part(at, x, y, w, wy, got=()):
    return call(
        part_kernel,
        in_specs=[SMEM] + [VMEM] * (4 + len(got)),
        out_specs=VMEM,
        out_shape=jax.ShapeDtypeStruct((x.shape[0], w.shape[1]), BF16),
        name="head_part",
    )(at, x, y, w, wy, *got)


def join_kernel(per, par_ref, at_ref, x_ref, y_ref, w_ref, wy_ref, *refs):
    total = block_product(at_ref, x_ref, y_ref, w_ref, wy_ref)
    for got in refs[:-2]:
        total = total + got[...].astype(F32)
    other_ref, out_ref = refs[-2:]
    rows = other_ref.shape[1] // per
    both = (total.astype(BF16), other_ref[...])
    for k in range(2):

        @pl.when(par_ref[0] == k)
        def _():
            for i in range(per):
                at = slice(i * rows, (i + 1) * rows)
                for j in range(2):
                    to = (2 * i + j) * rows
                    out_ref[:, to : to + rows] = both[j ^ k][:, at]


def join(par, at, per, x, y, w, wy, got, other):
    return call(
        functools.partial(join_kernel, per),
        in_specs=[SMEM] * 2 + [VMEM] * (5 + len(got)),
        out_specs=VMEM,
        out_shape=jax.ShapeDtypeStruct((x.shape[0], 2 * other.shape[1]), BF16),
        name="join",
    )(par, at, x, y, w, wy, *got, other)


def after(x, *earlier):
    return lax.optimization_barrier((x, *earlier))[0]


def local(queries, keys, values, out_grad, inputs, value_weight):
    length, cols = queries.shape
    n_ctx, n_head = lax.axis_size("ctx"), lax.axis_size("head")
    pairs = n_ctx // 2
    ctx, head = lax.axis_index("ctx"), lax.axis_index("head")
    parity, pair = ctx % 2, ctx // 2
    par = parity.astype(jnp.int32).reshape(1)
    factor = 1.0 / math.sqrt(DH * length * n_ctx)
    lines = [[2 * i + k for i in range(pairs)] for k in range(2)]
    def partner(x):
        return lax.ppermute(x, "ctx", [(i, i ^ 1) for i in range(n_ctx)])

    def across(x, bit):
        return lax.ppermute(x, "head", [(i, i ^ bit) for i in range(n_head)])

    order = list(range(0, pairs, 2)) + list(range(1, pairs, 2))[::-1]
    place = [order.index(i) for i in range(pairs)]
    moves = [
        (2 * order[i] + k, 2 * order[(i + 1) % pairs] + k)
        for i in range(pairs)
        for k in range(2)
    ]
    spot = jnp.asarray(place, jnp.int32)[pair]
    steps = jnp.arange(pairs, dtype=jnp.int32)

    def ring(x):
        return lax.ppermute(x, "ctx", moves)

    keep, send, near16 = states(par, queries, keys, values, out_grad)
    their_half = partner(send)
    line = pair.astype(jnp.int32).reshape(1)

    per = n_ctx // n_head // 2
    own, theirs = split(after(par, send), inputs, per)
    blocks = [value_weight, ring(after(value_weight, send))]
    own, theirs = [own], [partner(after(theirs, their_half))]

    vi = inside(after(queries, own[0]), keys, out_grad)
    offered = offer(line, after(keep, vi), their_half, pairs)
    every = lax.all_to_all(
        offered, "ctx", split_axis=0, concat_axis=0, axis_index_groups=lines
    )
    far, send_far = far_states(line, every, near16)
    ends = (far, partner(send_far), their_half)
    theirs = [after(theirs[0], send_far)]
    mine = finish_value(factor, par, keys, vi, ends)
    other = partner(mine)
    query_grad, key_grad = others(
        factor, par, queries, keys, after(values, mine), out_grad, ends
    )
    token = send_far
    for _ in range(2, pairs):
        blocks.append(ring(after(blocks[-1], token)))
        token = mine
    lent = [across(after(x, mine), 1) for x in blocks[:-1]]
    mine_too = across(mine, 1)

    offsets = [0]
    bit = n_head // 2
    while bit:
        own = own + [across(r, bit) for r in own]
        theirs = theirs + [across(r, bit) for r in theirs]
        offsets = offsets + [o ^ bit for o in offsets]
        bit //= 2
    own = [own[offsets.index(i)] for i in range(n_head)]
    theirs = [theirs[offsets.index(i)] for i in range(n_head)]

    which = jnp.asarray(order, jnp.int32)[(spot - 1 - steps) % pairs]
    offs, subs = (which // per) ^ head, which % per

    def piece(dtype, step, token):
        at = (offs[step : step + 1], subs[step : step + 1])
        return pieces(dtype, *at, after(mine, token), other, own, theirs)[0]

    total = piece(BF16, 0, query_grad)
    moved = ring(total)
    other_too = across(after(other, total, blocks[-1]), 1)
    lent.append(across(after(blocks[-1], total), 1))
    local_part = piece(F32, 1, other_too)

    here = head.astype(jnp.int32).reshape(1)
    held = jnp.asarray(order, jnp.int32)[(spot - steps) % pairs]

    def summed_parts(x, y):
        sent = [
            head_part(here ^ off, x, y, weight, borrowed)
            for off in range(2, n_head, 2)
        ]
        return sent[-1], [across(x, 2 * i + 2) for i, x in enumerate(sent)]

    total = add_own(moved, local_part)
    moved = ring(total)
    weight, borrowed = arrange(
        per, n_head, here, held, [after(blocks[0], total)] + blocks[1:], lent
    )
    token, got_other = summed_parts(other, other_too)
    token, got_mine = summed_parts(after(mine, token), mine_too)
    for step in range(2, pairs - 1):
        total = add_own(moved, piece(F32, step, token))
        moved = ring(total)
        token = total
    local_part = piece(F32, pairs - 1, token)
    part = head_part(
        here, after(other, local_part), other_too, weight, borrowed, got_other
    )
    swapped = partner(part)
    weight_grad = finish_weight(
        1.0 / math.sqrt(length * n_ctx), moved, after(local_part, part)
    )
    mine = after(mine, weight_grad)
    input_grad = join(
        par, here, per, mine, mine_too, weight, borrowed, got_mine, swapped
    )
    return (query_grad, key_grad, input_grad, weight_grad)


def solution(mesh):
    spec = P("ctx", "head")
    return jax.shard_map(
        local, mesh=mesh, in_specs=(spec,) * 6, out_specs=(spec,) * 4, check_vma=False
    )
```

```python
import functools
import math

import jax
import jax.numpy as jnp
from jax import lax
from jax.experimental import pallas as pl
from jax.experimental.pallas import tpu as pltpu
from jax.sharding import PartitionSpec as P

DH = 128
F32, BF16 = jnp.float32, jnp.bfloat16
VMEM = pl.BlockSpec(memory_space=pltpu.VMEM)
SMEM = pl.BlockSpec(memory_space=pltpu.SMEM)
ANY = pl.BlockSpec(memory_space=pl.ANY)


def dot(a, b, ca, cb):
    return lax.dot_general(a, b, (((ca,), (cb,)), ((), ())), preferred_element_type=F32)


def call(kernel, vmem=16, flops=1, **kw):
    hint = pl.CostEstimate(flops=flops, bytes_accessed=1, transcendentals=0)
    params = pltpu.CompilerParams(vmem_limit_bytes=vmem * 2**20)
    return pl.pallas_call(kernel, cost_estimate=hint, compiler_params=params, **kw)


def states_kernel(par_ref, *refs):
    arrays, (keep_ref, send_ref), bufs, sems = refs[:4], refs[4:6], refs[6:10], refs[10]
    heads = arrays[0].shape[1] // DH
    half = heads // 2

    def copy(j, hd):
        at = pl.ds(hd * DH, DH)
        return pltpu.make_async_copy(
            arrays[j].at[:, at], bufs[j].at[:, at], sems.at[j, hd]
        )

    for hd in range(heads):
        for j in range(4):
            copy(j, hd).start()
    for hd in range(heads):
        at = slice(hd * DH, (hd + 1) * DH)
        for j in range(4):
            copy(j, hd).wait()
        for kind, (a, b) in enumerate(((0, 3), (1, 2))):
            s = dot(bufs[a][:, at], bufs[b][:, at], 0, 0)
            own = par_ref[0] == hd // half

            @pl.when(own)
            def _():
                keep_ref[kind, hd % half] = s
                send_ref[1, kind, hd % half] = s.astype(BF16)

            @pl.when(jnp.logical_not(own))
            def _():
                send_ref[0, kind, hd % half] = s.astype(BF16)


def states(par, *arrays):
    n, cols = arrays[0].shape
    heads = cols // DH
    shape = (2, heads // 2, DH, DH)
    return call(
        states_kernel,
        vmem=60,
        in_specs=[SMEM] + [pl.BlockSpec(memory_space=pltpu.HBM)] * 4,
        out_specs=[VMEM] * 2,
        out_shape=[
            jax.ShapeDtypeStruct(shape, F32),
            jax.ShapeDtypeStruct((2, *shape), BF16),
        ],
        scratch_shapes=[pltpu.VMEM((n, cols), BF16)] * 4
        + [pltpu.SemaphoreType.DMA((4, heads))],
        name="states",
    )(par, *arrays)


def split_kernel(per, par_ref, x_ref, own_ref, theirs_ref, sems):
    width = own_ref.shape[2]
    for k in range(2):

        @pl.when(par_ref[0] == k)
        def _():
            copies = []
            for i in range(per):
                for j, out_ref in enumerate((own_ref, theirs_ref)):
                    at = (2 * i + (k ^ j)) * width
                    if width % 128:
                        out_ref[i] = x_ref[:, at : at + width]
                    else:
                        src = x_ref.at[:, pl.ds(at, width)]
                        copies.append(
                            pltpu.make_async_copy(src, out_ref.at[i], sems.at[j, i])
                        )
            for c in copies:
                c.start()
            for c in copies:
                c.wait()


def split(par, x, per):
    width = x.shape[1] // (2 * per)
    out = jax.ShapeDtypeStruct((per, x.shape[0], width), x.dtype)
    place = VMEM if width % 128 else pl.BlockSpec(memory_space=pltpu.HBM)
    return call(
        functools.partial(split_kernel, per),
        in_specs=[SMEM, place],
        out_specs=[VMEM] * 2,
        out_shape=[out, out],
        scratch_shapes=[pltpu.SemaphoreType.DMA((2, per))],
        name="split",
    )(par, x)


def inside_kernel(*refs):
    arrays, (out_ref, k_ref), bufs, sems = refs[:3], refs[3:5], refs[5:8], refs[8]
    n, cols = out_ref.shape
    heads = cols // DH

    def copy(j, hd):
        at = pl.ds(hd * DH, DH)
        return pltpu.make_async_copy(
            arrays[j].at[:, at], bufs[j].at[:, at], sems.at[j, hd]
        )

    for hd in range(heads):
        for j in range(3):
            copy(j, hd).start()
    rows = lax.broadcasted_iota(jnp.int32, (n, n), 0)
    causal = rows >= lax.broadcasted_iota(jnp.int32, (n, n), 1)
    for hd in range(heads):
        at = slice(hd * DH, (hd + 1) * DH)
        for j in range(3):
            copy(j, hd).wait()
        q, k, g = (x[:, at] for x in bufs)
        scores = jnp.where(causal, dot(q, k, 1, 1), 0.0).astype(BF16)
        out_ref[:, at] = dot(scores, g, 0, 0)
        k_ref[:, at] = k


def inside(*arrays):
    n, cols = arrays[0].shape
    return call(
        inside_kernel,
        in_specs=[pl.BlockSpec(memory_space=pltpu.HBM)] * 3,
        out_specs=[VMEM] * 2,
        out_shape=[jax.ShapeDtypeStruct((n, cols), d) for d in (F32, BF16)],
        scratch_shapes=[pltpu.VMEM((n, cols), BF16)] * 3
        + [pltpu.SemaphoreType.DMA((3, cols // DH))],
        name="inside",
    )(*arrays)


def offer_kernel(pair_ref, keep_ref, got_ref, out_ref):
    sums = [(keep_ref[k] + got_ref[0, k].astype(F32)).astype(BF16) for k in range(2)]
    for p in range(out_ref.shape[0]):
        out_ref[p] = jnp.where(p < pair_ref[0], sums[0], sums[1])


def offer(pair, keep, got, pairs):
    return call(
        offer_kernel,
        in_specs=[SMEM, VMEM, VMEM],
        out_specs=VMEM,
        out_shape=jax.ShapeDtypeStruct((pairs, *keep.shape[1:]), BF16),
        name="offer",
    )(pair, keep, got)


def far_kernel(pair_ref, every_ref, out_ref, send_ref):
    for kind in range(2):
        total = jnp.zeros(out_ref.shape[1:], F32)
        for p in range(every_ref.shape[0]):
            reached = p > pair_ref[0] if kind == 0 else p < pair_ref[0]
            total = total + jnp.where(reached, every_ref[p].astype(F32), 0.0)
        out_ref[kind] = total
        send_ref[kind] = total.astype(BF16)


def far_states(pair, every):
    shape = (2, *every.shape[1:])
    return call(
        far_kernel,
        in_specs=[SMEM, VMEM],
        out_specs=[VMEM] * 2,
        out_shape=[jax.ShapeDtypeStruct(shape, d) for d in (F32, BF16)],
        name="far",
    )(pair, every)


def entering(par, kind, hd, half, far, got, near):
    mine = par == hd // half
    i = hd % half
    outer = jnp.where(mine, far[kind, i], got[kind, i].astype(F32))
    close = jnp.where(mine, near[0, kind, i], near[1, kind, i]).astype(F32)
    total = outer + jnp.where(par == kind, close, 0.0)
    hi = total.astype(BF16)
    return hi, (total - hi.astype(F32)).astype(BF16)


def value_kernel(factor, half, par_ref, k_ref, vi_ref, *refs):
    ends, out_ref = refs[:-1], refs[-1]
    for hd in range(2 * half):
        at = slice(hd * DH, (hd + 1) * DH)
        hi, lo = entering(par_ref[0], 0, hd, half, *ends)
        k = k_ref[:, at]
        total = vi_ref[:, at] + (dot(k, hi, 1, 0) + dot(k, lo, 1, 0))
        out_ref[:, at] = (factor * total).astype(BF16)


def finish_value(factor, par, k, vi, ends):
    return call(
        functools.partial(value_kernel, factor, k.shape[1] // DH // 2),
        in_specs=[SMEM] + [VMEM] * (2 + len(ends)),
        out_specs=VMEM,
        out_shape=jax.ShapeDtypeStruct(k.shape, BF16),
        name="finish_value",
    )(par, k, vi, *ends)


def others_kernel(factor, half, par_ref, q_ref, k_ref, v_ref, g_ref, *refs):
    ends, (qo_ref, ko_ref) = refs[:-2], refs[-2:]
    hd = pl.program_id(0)
    q, k, v, g = q_ref[...], k_ref[...], v_ref[...], g_ref[...]
    n = q.shape[0]
    rows = lax.broadcasted_iota(jnp.int32, (n, n), 0)
    cols = lax.broadcasted_iota(jnp.int32, (n, n), 1)
    scores = jnp.where(rows >= cols, dot(g, v, 1, 1), 0.0).astype(BF16)
    hi, lo = entering(par_ref[0], 1, hd, half, *ends)
    total = dot(scores, k, 1, 0) + (dot(g, hi, 1, 1) + dot(g, lo, 1, 1))
    qo_ref[...] = (factor * total).astype(BF16)
    hi, lo = entering(par_ref[0], 0, hd, half, *ends)
    total = dot(scores, q, 0, 0) + (dot(v, hi, 1, 1) + dot(v, lo, 1, 1))
    ko_ref[...] = (factor * total).astype(BF16)


def others(factor, par, q, k, v, g, ends):
    n, cols = q.shape
    spec = pl.BlockSpec((n, DH), lambda h: (0, h))
    held = [pl.BlockSpec(x.shape, lambda h, d=x.ndim: (0,) * d) for x in ends]
    out = jax.ShapeDtypeStruct(q.shape, BF16)
    return call(
        functools.partial(others_kernel, factor, cols // DH // 2),
        grid=(cols // DH,),
        in_specs=[SMEM] + [spec] * 4 + held,
        out_specs=[spec] * 2,
        out_shape=[out] * 2,
        name="others",
    )(par, q, k, v, g, *ends)


def piece_kernel(count, offs_ref, subs_ref, a_ref, b_ref, *refs):
    own, theirs = refs[:count], refs[count : 2 * count]
    outs, (x, y, at, bt, sems) = refs[2 * count : -5], refs[-5:]
    step, steps = pl.program_id(0), pl.num_programs(0)
    slot = lax.rem(step, 2)

    def fetch(k, to):
        for i in range(count):

            @pl.when(offs_ref[k] == i)
            def _():
                for j, (src, dst) in enumerate(((own, x), (theirs, y))):
                    pltpu.make_async_copy(
                        src[i].at[subs_ref[k]], dst.at[to], sems.at[j, to]
                    ).start()

    @pl.when(step == 0)
    def _():
        fetch(0, 0)

    @pl.when(step + 1 < steps)
    def _():
        fetch(step + 1, 1 - slot)

    @pl.when(step == 0)
    def _():
        at[...] = a_ref[...].T
        bt[...] = b_ref[...].T

    for j, (src, dst) in enumerate(((own, x), (theirs, y))):
        pltpu.make_async_copy(src[0].at[0], dst.at[slot], sems.at[j, slot]).wait()
    total = dot(at[...], x[slot], 1, 0) + dot(bt[...], y[slot], 1, 0)
    span = outs[0].shape[0]
    for i, out_ref in enumerate(outs):
        out_ref[...] = total[i * span : (i + 1) * span].astype(out_ref.dtype)


def pieces(dtype, chains, flops, offs, subs, a, b, own, theirs):
    steps = offs.shape[0]
    count = len(own)
    _, n, width = own[0].shape
    cols = a.shape[1]
    return call(
        functools.partial(piece_kernel, count),
        grid=(steps,),
        in_specs=[SMEM] * 2 + [VMEM] * 2 + [ANY] * (2 * count),
        flops=flops,
        out_specs=[VMEM] * chains,
        out_shape=[jax.ShapeDtypeStruct((cols // chains, width), dtype)] * chains,
        scratch_shapes=[
            pltpu.VMEM((2, n, width), BF16),
            pltpu.VMEM((2, n, width), BF16),
            pltpu.VMEM((cols, n), BF16),
            pltpu.VMEM((cols, n), BF16),
            pltpu.SemaphoreType.DMA((2, 2)),
        ],
        name="pieces",
    )(offs, subs, a, b, *own, *theirs)


def weight_kernel(scale, *refs):
    count, out_ref = len(refs) // 2, refs[-1]
    span = refs[0].shape[0]
    for i in range(count):
        total = refs[i][...].astype(F32) + refs[count + i][...]
        out_ref[:, i * span : (i + 1) * span] = total.T * scale


def finish_weight(scale, moved, own):
    span, width = moved[0].shape
    count = len(moved)
    return call(
        functools.partial(weight_kernel, scale),
        in_specs=[VMEM] * (2 * count),
        out_specs=VMEM,
        out_shape=jax.ShapeDtypeStruct((width, span * count), F32),
        name="finish_weight",
    )(*moved, *own)


def add_kernel(moved_ref, own_ref, out_ref):
    out_ref[...] = (moved_ref[...].astype(F32) + own_ref[...]).astype(BF16)


def add_own(moved, own):
    return call(
        add_kernel,
        in_specs=[VMEM] * 2,
        out_specs=VMEM,
        out_shape=jax.ShapeDtypeStruct(moved.shape, BF16),
        name="add_own",
    )(moved, own)


def arrange_kernel(per, head_ref, which_ref, *refs):
    count = which_ref.shape[0]
    outs, sems = refs[-3:-1], refs[-1]
    rows = refs[0].shape[0]

    def copies(s):
        p = which_ref[s]
        at = (p // per // 2, pl.ds((p % per) * rows, rows))
        pair = [
            pltpu.make_async_copy(refs[j * count + s], outs[j].at[at], sems.at[j, s])
            for j in range(2)
        ]
        return pair, (p // per) % 2 == head_ref[0] % 2

    for act in ("start", "wait"):
        for s in range(count):
            pair, needed = copies(s)

            @pl.when(needed)
            def _():
                for c in pair:
                    getattr(c, act)()


def arrange(per, n_head, head, which, blocks, lent):
    rows, cols = blocks[0].shape
    count = len(blocks)
    out = jax.ShapeDtypeStruct((n_head // 2, per * rows, cols), BF16)
    return call(
        functools.partial(arrange_kernel, per),
        in_specs=[SMEM] * 2 + [ANY] * (2 * count),
        out_specs=[VMEM] * 2,
        out_shape=[out] * 2,
        scratch_shapes=[pltpu.SemaphoreType.DMA((2, count))],
        name="arrange",
    )(head, which, *blocks, *lent)


def block_product(at_ref, x_ref, y_ref, w_ref, wy_ref):
    at = at_ref[0] // 2
    return dot(x_ref[...], w_ref[at], 1, 1) + dot(y_ref[...], wy_ref[at], 1, 1)


def part_kernel(at_ref, x_ref, y_ref, w_ref, wy_ref, *refs):
    total = block_product(at_ref, x_ref, y_ref, w_ref, wy_ref)
    for got in refs[:-1]:
        total = total + got[...].astype(F32)
    refs[-1][...] = total.astype(BF16)


def head_part(at, x, y, w, wy, got=()):
    return call(
        part_kernel,
        in_specs=[SMEM] + [VMEM] * (4 + len(got)),
        out_specs=VMEM,
        out_shape=jax.ShapeDtypeStruct((x.shape[0], w.shape[1]), BF16),
        name="head_part",
    )(at, x, y, w, wy, *got)


def join_kernel(per, par_ref, at_ref, x_ref, y_ref, w_ref, wy_ref, *refs):
    total = block_product(at_ref, x_ref, y_ref, w_ref, wy_ref)
    for got in refs[:-2]:
        total = total + got[...].astype(F32)
    other_ref, out_ref = refs[-2:]
    rows = other_ref.shape[1] // per
    both = (total.astype(BF16), other_ref[...])
    for k in range(2):

        @pl.when(par_ref[0] == k)
        def _():
            for i in range(per):
                at = slice(i * rows, (i + 1) * rows)
                for j in range(2):
                    to = (2 * i + j) * rows
                    out_ref[:, to : to + rows] = both[j ^ k][:, at]


def join(par, at, per, x, y, w, wy, got, other):
    return call(
        functools.partial(join_kernel, per),
        in_specs=[SMEM] * 2 + [VMEM] * (5 + len(got)),
        out_specs=VMEM,
        out_shape=jax.ShapeDtypeStruct((x.shape[0], 2 * other.shape[1]), BF16),
        name="join",
    )(par, at, x, y, w, wy, *got, other)


def after(x, *earlier):
    return lax.optimization_barrier((x, *earlier))[0]


def local(queries, keys, values, out_grad, inputs, value_weight):
    length, cols = queries.shape
    n_ctx, n_head = lax.axis_size("ctx"), lax.axis_size("head")
    pairs = n_ctx // 2
    ctx, head = lax.axis_index("ctx"), lax.axis_index("head")
    parity, pair = ctx % 2, ctx // 2
    par = parity.astype(jnp.int32).reshape(1)
    factor = 1.0 / math.sqrt(DH * length * n_ctx)
    lines = [[2 * i + k for i in range(pairs)] for k in range(2)]
    def partner(x):
        return lax.ppermute(x, "ctx", [(i, i ^ 1) for i in range(n_ctx)])

    def across(x, bit):
        return lax.ppermute(x, "head", [(i, i ^ bit) for i in range(n_head)])

    order = list(range(0, pairs, 2)) + list(range(1, pairs, 2))[::-1]
    place = [order.index(i) for i in range(pairs)]
    moves = [
        (2 * order[i] + k, 2 * order[(i + 1) % pairs] + k)
        for i in range(pairs)
        for k in range(2)
    ]
    spot = jnp.asarray(place, jnp.int32)[pair]
    steps = jnp.arange(pairs, dtype=jnp.int32)

    def ring(x):
        return lax.ppermute(x, "ctx", moves)

    keep, send = states(par, queries, keys, values, out_grad)
    near = partner(send)
    line = pair.astype(jnp.int32).reshape(1)

    per = n_ctx // n_head // 2
    width = value_weight.shape[0]
    own, theirs = split(after(par, send), inputs, per)
    blocks = [value_weight, ring(after(value_weight, send))]
    own, theirs = [own], [partner(after(theirs, near))]

    offered = offer(line, keep, near, pairs)
    every = lax.all_to_all(
        offered, "ctx", split_axis=0, concat_axis=0, axis_index_groups=lines
    )
    far, send_far = far_states(line, every)
    ends = (far, partner(send_far), near)
    vi, keys_too = inside(after(queries, send_far), keys, out_grad)
    theirs = [after(theirs[0], send_far)]
    mine = finish_value(factor, par, keys_too, vi, ends)
    other = partner(mine)
    query_grad, key_grad = others(
        factor, par, queries, keys, after(values, mine), out_grad, ends
    )
    token = send_far
    for _ in range(2, pairs):
        blocks.append(ring(after(blocks[-1], token)))
        token = mine
    lent = [across(after(x, mine), 1) for x in blocks[:-1]]
    mine_too = across(mine, 1)

    offsets = [0]
    bit = n_head // 2
    while bit:
        own = own + [across(r, bit) for r in own]
        theirs = theirs + [across(r, bit) for r in theirs]
        offsets = offsets + [o ^ bit for o in offsets]
        bit //= 2
    own = [own[offsets.index(i)] for i in range(n_head)]
    theirs = [theirs[offsets.index(i)] for i in range(n_head)]

    which = jnp.asarray(order, jnp.int32)[(spot - 1 - steps) % pairs]
    offs, subs = (which // per) ^ head, which % per

    chains = 2

    def piece(dtype, step, token, flops=1):
        at = (offs[step : step + 1], subs[step : step + 1])
        vals = (after(mine, token), other, own, theirs)
        return pieces(dtype, chains, flops, *at, *vals)

    total = piece(BF16, 0, query_grad, 4 * length * cols * width)
    moved = [ring(x) for x in total]
    other_too = across(other, 1)
    lent.append(across(after(blocks[-1], total[0]), 1))
    local_part = piece(F32, 1, total[0])

    here = head.astype(jnp.int32).reshape(1)
    held = jnp.asarray(order, jnp.int32)[(spot - steps) % pairs]

    def summed_parts(x, y):
        sent = [
            head_part(here ^ off, x, y, weight, borrowed)
            for off in range(2, n_head, 2)
        ]
        return sent[-1], [across(x, 2 * i + 2) for i, x in enumerate(sent)]

    weight, borrowed = arrange(
        per, n_head, here, held, [after(blocks[0], local_part[0])] + blocks[1:], lent
    )
    token, got_other = summed_parts(other, other_too)
    token, got_mine = summed_parts(after(mine, token), mine_too)
    for step in range(1, pairs - 1):
        for i in range(chains):
            token = add_own(moved[i], after(local_part[i], token))
            moved[i] = ring(token)
        local_part = piece(F32, step + 1, token)
        token = local_part[0]
    part = head_part(
        here, after(other, token), other_too, weight, borrowed, got_other
    )
    swapped = partner(part)
    weight_grad = finish_weight(
        1.0 / math.sqrt(length * n_ctx),
        moved,
        [after(local_part[0], part), *local_part[1:]],
    )
    mine = after(mine, weight_grad)
    input_grad = join(
        par, here, per, mine, mine_too, weight, borrowed, got_mine, swapped
    )
    return (query_grad, key_grad, input_grad, weight_grad)


def solution(mesh):
    spec = P("ctx", "head")
    return jax.shard_map(
        local, mesh=mesh, in_specs=(spec,) * 6, out_specs=(spec,) * 4, check_vma=False
    )
```

```python
import functools
import math

import jax
import jax.numpy as jnp
from jax import lax
from jax.experimental import pallas as pl
from jax.experimental.pallas import tpu as pltpu
from jax.sharding import PartitionSpec as P

DH = 128
F32, BF16 = jnp.float32, jnp.bfloat16
VMEM = pl.BlockSpec(memory_space=pltpu.VMEM)
SMEM = pl.BlockSpec(memory_space=pltpu.SMEM)
ANY = pl.BlockSpec(memory_space=pl.ANY)


def dot(a, b, ca, cb):
    return lax.dot_general(a, b, (((ca,), (cb,)), ((), ())), preferred_element_type=F32)


def call(kernel, vmem=16, flops=1, **kw):
    hint = pl.CostEstimate(flops=flops, bytes_accessed=1, transcendentals=0)
    params = pltpu.CompilerParams(vmem_limit_bytes=vmem * 2**20)
    return pl.pallas_call(kernel, cost_estimate=hint, compiler_params=params, **kw)


def states_kernel(par_ref, *refs):
    arrays, (keep_ref, send_ref), bufs, sems = refs[:4], refs[4:6], refs[6:10], refs[10]
    heads = arrays[0].shape[1] // DH
    half = heads // 2

    def copy(j, hd):
        at = pl.ds(hd * DH, DH)
        return pltpu.make_async_copy(
            arrays[j].at[:, at], bufs[j].at[:, at], sems.at[j, hd]
        )

    for hd in range(heads):
        for j in range(4):
            copy(j, hd).start()
    for hd in range(heads):
        at = slice(hd * DH, (hd + 1) * DH)
        for j in range(4):
            copy(j, hd).wait()
        for kind, (a, b) in enumerate(((0, 3), (1, 2))):
            s = dot(bufs[a][:, at], bufs[b][:, at], 0, 0)
            own = par_ref[0] == hd // half

            @pl.when(own)
            def _():
                keep_ref[kind, hd % half] = s

            @pl.when(own & (par_ref[0] != kind))
            def _():
                send_ref[2, hd % half] = s.astype(BF16)

            @pl.when(jnp.logical_not(own))
            def _():
                send_ref[kind, hd % half] = s.astype(BF16)


def states(par, *arrays):
    n, cols = arrays[0].shape
    heads = cols // DH
    shape = (2, heads // 2, DH, DH)
    return call(
        states_kernel,
        vmem=60,
        in_specs=[SMEM] + [pl.BlockSpec(memory_space=pltpu.HBM)] * 4,
        out_specs=[VMEM] * 2,
        out_shape=[
            jax.ShapeDtypeStruct(shape, F32),
            jax.ShapeDtypeStruct((3, *shape[1:]), BF16),
        ],
        scratch_shapes=[pltpu.VMEM((n, cols), BF16)] * 4
        + [pltpu.SemaphoreType.DMA((4, heads))],
        name="states",
    )(par, *arrays)


def split_kernel(per, par_ref, x_ref, own_ref, theirs_ref, sems):
    width = own_ref.shape[2]
    for k in range(2):

        @pl.when(par_ref[0] == k)
        def _():
            copies = []
            for i in range(per):
                for j, out_ref in enumerate((own_ref, theirs_ref)):
                    at = (2 * i + (k ^ j)) * width
                    if width % 128:
                        out_ref[i] = x_ref[:, at : at + width]
                    else:
                        src = x_ref.at[:, pl.ds(at, width)]
                        copies.append(
                            pltpu.make_async_copy(src, out_ref.at[i], sems.at[j, i])
                        )
            for c in copies:
                c.start()
            for c in copies:
                c.wait()


def split(par, x, per):
    width = x.shape[1] // (2 * per)
    out = jax.ShapeDtypeStruct((per, x.shape[0], width), x.dtype)
    place = VMEM if width % 128 else pl.BlockSpec(memory_space=pltpu.HBM)
    return call(
        functools.partial(split_kernel, per),
        in_specs=[SMEM, place],
        out_specs=[VMEM] * 2,
        out_shape=[out, out],
        scratch_shapes=[pltpu.SemaphoreType.DMA((2, per))],
        name="split",
    )(par, x)


def inside_kernel(*refs):
    arrays, (out_ref, k_ref), bufs, sems = refs[:3], refs[3:5], refs[5:8], refs[8]
    n, cols = out_ref.shape
    heads = cols // DH

    def copy(j, hd):
        at = pl.ds(hd * DH, DH)
        return pltpu.make_async_copy(
            arrays[j].at[:, at], bufs[j].at[:, at], sems.at[j, hd]
        )

    for hd in range(heads):
        for j in range(3):
            copy(j, hd).start()
    rows = lax.broadcasted_iota(jnp.int32, (n, n), 0)
    causal = rows >= lax.broadcasted_iota(jnp.int32, (n, n), 1)
    for hd in range(heads):
        at = slice(hd * DH, (hd + 1) * DH)
        for j in range(3):
            copy(j, hd).wait()
        q, k, g = (x[:, at] for x in bufs)
        scores = jnp.where(causal, dot(q, k, 1, 1), 0.0).astype(BF16)
        out_ref[:, at] = dot(scores, g, 0, 0)
        k_ref[:, at] = k


def inside(*arrays):
    n, cols = arrays[0].shape
    return call(
        inside_kernel,
        in_specs=[pl.BlockSpec(memory_space=pltpu.HBM)] * 3,
        out_specs=[VMEM] * 2,
        out_shape=[jax.ShapeDtypeStruct((n, cols), d) for d in (F32, BF16)],
        scratch_shapes=[pltpu.VMEM((n, cols), BF16)] * 3
        + [pltpu.SemaphoreType.DMA((3, cols // DH))],
        name="inside",
    )(*arrays)


def offer_kernel(pair_ref, keep_ref, got_ref, out_ref):
    sums = [(keep_ref[k] + got_ref[k].astype(F32)).astype(BF16) for k in range(2)]
    for p in range(out_ref.shape[0]):
        out_ref[p] = jnp.where(p < pair_ref[0], sums[0], sums[1])


def offer(pair, keep, got, pairs):
    return call(
        offer_kernel,
        in_specs=[SMEM, VMEM, VMEM],
        out_specs=VMEM,
        out_shape=jax.ShapeDtypeStruct((pairs, *keep.shape[1:]), BF16),
        name="offer",
    )(pair, keep, got)


def far_kernel(pair_ref, every_ref, out_ref, send_ref):
    for kind in range(2):
        total = jnp.zeros(out_ref.shape[1:], F32)
        for p in range(every_ref.shape[0]):
            reached = p > pair_ref[0] if kind == 0 else p < pair_ref[0]
            total = total + jnp.where(reached, every_ref[p].astype(F32), 0.0)
        out_ref[kind] = total
        send_ref[kind] = total.astype(BF16)


def far_states(pair, every):
    shape = (2, *every.shape[1:])
    return call(
        far_kernel,
        in_specs=[SMEM, VMEM],
        out_specs=[VMEM] * 2,
        out_shape=[jax.ShapeDtypeStruct(shape, d) for d in (F32, BF16)],
        name="far",
    )(pair, every)


def entering(par, kind, hd, half, far, got, near):
    mine = par == hd // half
    i = hd % half
    outer = jnp.where(mine, far[kind, i], got[kind, i].astype(F32))
    close = jnp.where(mine, near[kind, i], near[2, i]).astype(F32)
    total = outer + jnp.where(par == kind, close, 0.0)
    hi = total.astype(BF16)
    return hi, (total - hi.astype(F32)).astype(BF16)


def value_kernel(factor, half, par_ref, k_ref, vi_ref, *refs):
    ends, out_ref = refs[:-1], refs[-1]
    for hd in range(2 * half):
        at = slice(hd * DH, (hd + 1) * DH)
        hi, lo = entering(par_ref[0], 0, hd, half, *ends)
        k = k_ref[:, at]
        total = vi_ref[:, at] + (dot(k, hi, 1, 0) + dot(k, lo, 1, 0))
        out_ref[:, at] = (factor * total).astype(BF16)


def finish_value(factor, par, k, vi, ends):
    return call(
        functools.partial(value_kernel, factor, k.shape[1] // DH // 2),
        in_specs=[SMEM] + [VMEM] * (2 + len(ends)),
        out_specs=VMEM,
        out_shape=jax.ShapeDtypeStruct(k.shape, BF16),
        name="finish_value",
    )(par, k, vi, *ends)


def others_kernel(factor, half, par_ref, q_ref, k_ref, v_ref, g_ref, *refs):
    ends, (qo_ref, ko_ref) = refs[:-2], refs[-2:]
    hd = pl.program_id(0)
    q, k, v, g = q_ref[...], k_ref[...], v_ref[...], g_ref[...]
    n = q.shape[0]
    rows = lax.broadcasted_iota(jnp.int32, (n, n), 0)
    cols = lax.broadcasted_iota(jnp.int32, (n, n), 1)
    scores = jnp.where(rows >= cols, dot(g, v, 1, 1), 0.0).astype(BF16)
    hi, lo = entering(par_ref[0], 1, hd, half, *ends)
    total = dot(scores, k, 1, 0) + (dot(g, hi, 1, 1) + dot(g, lo, 1, 1))
    qo_ref[...] = (factor * total).astype(BF16)
    hi, lo = entering(par_ref[0], 0, hd, half, *ends)
    total = dot(scores, q, 0, 0) + (dot(v, hi, 1, 1) + dot(v, lo, 1, 1))
    ko_ref[...] = (factor * total).astype(BF16)


def others(factor, par, q, k, v, g, ends):
    n, cols = q.shape
    spec = pl.BlockSpec((n, DH), lambda h: (0, h))
    held = [pl.BlockSpec(x.shape, lambda h, d=x.ndim: (0,) * d) for x in ends]
    out = jax.ShapeDtypeStruct(q.shape, BF16)
    return call(
        functools.partial(others_kernel, factor, cols // DH // 2),
        grid=(cols // DH,),
        in_specs=[SMEM] + [spec] * 4 + held,
        out_specs=[spec] * 2,
        out_shape=[out] * 2,
        name="others",
    )(par, q, k, v, g, *ends)


def line_at(order, place):
    place = lax.rem(place + 2 * len(order), len(order))
    line = jnp.int32(order[0])
    for i, p in enumerate(order[1:], 1):
        line = jnp.where(place == i, p, line)
    return line


def piece_kernel(order, per, step, count, spot_ref, head_ref, a_ref, b_ref, *refs):
    own, theirs = refs[:count], refs[count : 2 * count]
    outs, (x, y, at, bt, sems) = refs[2 * count : -5], refs[-5:]
    line = line_at(order, spot_ref[0] - 1 - step)
    off, sub = lax.div(line, per) ^ head_ref[0], lax.rem(line, per)

    for i in range(count):

        @pl.when(off == i)
        def _():
            for j, (src, dst) in enumerate(((own, x), (theirs, y))):
                pltpu.make_async_copy(src[i].at[sub], dst, sems.at[j]).start()

    at[...] = a_ref[...].T
    bt[...] = b_ref[...].T
    for j, (src, dst) in enumerate(((own, x), (theirs, y))):
        pltpu.make_async_copy(src[0].at[0], dst, sems.at[j]).wait()
    total = dot(at[...], x[...], 1, 0) + dot(bt[...], y[...], 1, 0)
    span = outs[0].shape[0]
    for i, out_ref in enumerate(outs):
        out_ref[...] = total[i * span : (i + 1) * span].astype(out_ref.dtype)


def pieces(dtype, chains, flops, order, per, step, spot, head, a, b, own, theirs):
    count = len(own)
    _, n, width = own[0].shape
    cols = a.shape[1]
    return call(
        functools.partial(piece_kernel, order, per, step, count),
        flops=flops,
        in_specs=[SMEM] * 2 + [VMEM] * 2 + [ANY] * (2 * count),
        out_specs=[VMEM] * chains,
        out_shape=[jax.ShapeDtypeStruct((cols // chains, width), dtype)] * chains,
        scratch_shapes=[pltpu.VMEM((n, width), BF16)] * 2
        + [pltpu.VMEM((cols, n), BF16)] * 2
        + [pltpu.SemaphoreType.DMA((2,))],
        name="pieces",
    )(spot, head, a, b, *own, *theirs)


def weight_kernel(scale, *refs):
    count, out_ref = len(refs) // 2, refs[-1]
    span = refs[0].shape[0]
    for i in range(count):
        total = refs[i][...].astype(F32) + refs[count + i][...]
        out_ref[:, i * span : (i + 1) * span] = total.T * scale


def finish_weight(scale, moved, own):
    span, width = moved[0].shape
    count = len(moved)
    return call(
        functools.partial(weight_kernel, scale),
        in_specs=[VMEM] * (2 * count),
        out_specs=VMEM,
        out_shape=jax.ShapeDtypeStruct((width, span * count), F32),
        name="finish_weight",
    )(*moved, *own)


def add_kernel(moved_ref, own_ref, out_ref):
    out_ref[...] = (moved_ref[...].astype(F32) + own_ref[...]).astype(BF16)


def add_own(moved, own):
    return call(
        add_kernel,
        in_specs=[VMEM] * 2,
        out_specs=VMEM,
        out_shape=jax.ShapeDtypeStruct(moved.shape, BF16),
        name="add_own",
    )(moved, own)


def arrange_kernel(order, per, head_ref, spot_ref, *refs):
    count = len(order)
    outs, sems = refs[-3:-1], refs[-1]
    rows = refs[0].shape[0]

    def copies(s):
        p = line_at(order, spot_ref[0] - s)
        head, sub = lax.div(p, per), lax.rem(p, per)
        at = (lax.div(head, 2), pl.ds(sub * rows, rows))
        pair = [
            pltpu.make_async_copy(refs[j * count + s], outs[j].at[at], sems.at[j, s])
            for j in range(2)
        ]
        return pair, lax.rem(head, 2) == lax.rem(head_ref[0], 2)

    for act in ("start", "wait"):
        for s in range(count):
            pair, needed = copies(s)

            @pl.when(needed)
            def _():
                for c in pair:
                    getattr(c, act)()


def arrange(order, per, n_head, head, spot, blocks, lent):
    rows, cols = blocks[0].shape
    count = len(blocks)
    out = jax.ShapeDtypeStruct((n_head // 2, per * rows, cols), BF16)
    return call(
        functools.partial(arrange_kernel, order, per),
        in_specs=[SMEM] * 2 + [ANY] * (2 * count),
        out_specs=[VMEM] * 2,
        out_shape=[out] * 2,
        scratch_shapes=[pltpu.SemaphoreType.DMA((2, count))],
        name="arrange",
    )(head, spot, *blocks, *lent)


def block_product(at_ref, x_ref, y_ref, w_ref, wy_ref):
    at = at_ref[0] // 2
    return dot(x_ref[...], w_ref[at], 1, 1) + dot(y_ref[...], wy_ref[at], 1, 1)


def part_kernel(at_ref, x_ref, y_ref, w_ref, wy_ref, *refs):
    total = block_product(at_ref, x_ref, y_ref, w_ref, wy_ref)
    for got in refs[:-1]:
        total = total + got[...].astype(F32)
    refs[-1][...] = total.astype(BF16)


def head_part(at, x, y, w, wy, got=()):
    return call(
        part_kernel,
        in_specs=[SMEM] + [VMEM] * (4 + len(got)),
        out_specs=VMEM,
        out_shape=jax.ShapeDtypeStruct((x.shape[0], w.shape[1]), BF16),
        name="head_part",
    )(at, x, y, w, wy, *got)


def join_kernel(per, par_ref, at_ref, x_ref, y_ref, w_ref, wy_ref, *refs):
    total = block_product(at_ref, x_ref, y_ref, w_ref, wy_ref)
    for got in refs[:-2]:
        total = total + got[...].astype(F32)
    other_ref, out_ref = refs[-2:]
    rows = other_ref.shape[1] // per
    both = (total.astype(BF16), other_ref[...])
    for k in range(2):

        @pl.when(par_ref[0] == k)
        def _():
            for i in range(per):
                at = slice(i * rows, (i + 1) * rows)
                for j in range(2):
                    to = (2 * i + j) * rows
                    out_ref[:, to : to + rows] = both[j ^ k][:, at]


def join(par, at, per, x, y, w, wy, got, other):
    return call(
        functools.partial(join_kernel, per),
        in_specs=[SMEM] * 2 + [VMEM] * (5 + len(got)),
        out_specs=VMEM,
        out_shape=jax.ShapeDtypeStruct((x.shape[0], 2 * other.shape[1]), BF16),
        name="join",
    )(par, at, x, y, w, wy, *got, other)


def after(x, *earlier):
    return lax.optimization_barrier((x, *earlier))[0]


def local(queries, keys, values, out_grad, inputs, value_weight):
    length, cols = queries.shape
    n_ctx, n_head = lax.axis_size("ctx"), lax.axis_size("head")
    pairs = n_ctx // 2
    ctx, head = lax.axis_index("ctx"), lax.axis_index("head")
    parity, pair = ctx % 2, ctx // 2
    par = parity.astype(jnp.int32).reshape(1)
    factor = 1.0 / math.sqrt(DH * length * n_ctx)
    lines = [[2 * i + k for i in range(pairs)] for k in range(2)]
    def partner(x):
        return lax.ppermute(x, "ctx", [(i, i ^ 1) for i in range(n_ctx)])

    def across(x, bit):
        return lax.ppermute(x, "head", [(i, i ^ bit) for i in range(n_head)])

    order = list(range(0, pairs, 2)) + list(range(1, pairs, 2))[::-1]
    place = [order.index(i) for i in range(pairs)]
    moves = [
        (2 * order[i] + k, 2 * order[(i + 1) % pairs] + k)
        for i in range(pairs)
        for k in range(2)
    ]
    here = head.astype(jnp.int32).reshape(1)
    spot = line_at(place, pair.astype(jnp.int32)).reshape(1)

    def ring(x):
        return lax.ppermute(x, "ctx", moves)

    keep, send = states(par, queries, keys, values, out_grad)
    near = partner(send)
    line = pair.astype(jnp.int32).reshape(1)

    per = n_ctx // n_head // 2
    width = value_weight.shape[0]
    own, theirs = split(after(par, send), inputs, per)
    blocks = [value_weight, ring(after(value_weight, send))]
    own, theirs = [own], [partner(after(theirs, near))]

    offered = offer(line, keep, near, pairs)
    every = lax.all_to_all(
        offered, "ctx", split_axis=0, concat_axis=0, axis_index_groups=lines
    )
    far, send_far = far_states(line, every)
    ends = (far, partner(send_far), near)
    vi, keys_too = inside(after(queries, send_far), keys, out_grad)
    theirs = [after(theirs[0], send_far)]
    mine = finish_value(factor, par, keys_too, vi, ends)
    other = partner(mine)
    query_grad, key_grad = others(
        factor, par, queries, keys, after(values, mine), out_grad, ends
    )
    token = send_far
    for _ in range(2, pairs):
        blocks.append(ring(after(blocks[-1], token)))
        token = mine
    lent = [across(after(x, mine), 1) for x in blocks[:-1]]
    mine_too = across(mine, 1)

    offsets = [0]
    bit = n_head // 2
    while bit:
        own = own + [across(r, bit) for r in own]
        theirs = theirs + [across(r, bit) for r in theirs]
        offsets = offsets + [o ^ bit for o in offsets]
        bit //= 2
    own = [own[offsets.index(i)] for i in range(n_head)]
    theirs = [theirs[offsets.index(i)] for i in range(n_head)]


    chains = 2

    def piece(dtype, step, token, flops=1):
        vals = (spot, here, after(mine, token), other, own, theirs)
        return pieces(dtype, chains, flops, order, per, step, *vals)

    total = piece(BF16, 0, query_grad, 4 * length * cols * width)
    moved = [ring(x) for x in total]
    other_too = across(other, 1)
    lent.append(across(after(blocks[-1], total[0]), 1))
    local_part = piece(F32, 1, total[0])


    def summed_parts(x, y):
        sent = [
            head_part(here ^ off, x, y, weight, borrowed)
            for off in range(2, n_head, 2)
        ]
        return sent[-1], [across(x, 2 * i + 2) for i, x in enumerate(sent)]

    held = [after(blocks[0], local_part[0])] + blocks[1:]
    weight, borrowed = arrange(order, per, n_head, here, spot, held, lent)
    token, got_other = summed_parts(other, other_too)
    token, got_mine = summed_parts(after(mine, token), mine_too)
    part = None
    for step in range(1, pairs - 1):
        if step == pairs - 2:
            last = piece(F32, pairs - 1, token)
            token = last[0]
        for i in range(chains):
            if step == pairs - 2 and i == chains - 1:
                lead = (here, after(other, token), other_too, weight, borrowed)
                token = part = head_part(*lead, got_other)
            token = add_own(moved[i], after(local_part[i], token))
            moved[i] = ring(token)
        if step < pairs - 2:
            local_part = piece(F32, step + 1, token)
            token = local_part[0]
    swapped = partner(part)
    weight_grad = finish_weight(1.0 / math.sqrt(length * n_ctx), moved, last)
    mine = after(mine, weight_grad)
    input_grad = join(
        par, here, per, mine, mine_too, weight, borrowed, got_mine, swapped
    )
    return (query_grad, key_grad, input_grad, weight_grad)


def solution(mesh):
    spec = P("ctx", "head")
    return jax.shard_map(
        local, mesh=mesh, in_specs=(spec,) * 6, out_specs=(spec,) * 4, check_vma=False
    )
```

```python
import functools
import math

import jax
import jax.numpy as jnp
from jax import lax
from jax.experimental import pallas as pl
from jax.experimental.pallas import tpu as pltpu
from jax.sharding import PartitionSpec as P

DH = 128
F32, BF16 = jnp.float32, jnp.bfloat16
VMEM = pl.BlockSpec(memory_space=pltpu.VMEM)
SMEM = pl.BlockSpec(memory_space=pltpu.SMEM)
ANY = pl.BlockSpec(memory_space=pl.ANY)


def dot(a, b, ca, cb):
    return lax.dot_general(a, b, (((ca,), (cb,)), ((), ())), preferred_element_type=F32)


def call(kernel, vmem=16, flops=1, **kw):
    hint = pl.CostEstimate(flops=flops, bytes_accessed=1, transcendentals=0)
    params = pltpu.CompilerParams(vmem_limit_bytes=vmem * 2**20)
    return pl.pallas_call(kernel, cost_estimate=hint, compiler_params=params, **kw)


def states_kernel(par_ref, *refs):
    arrays, (keep_ref, send_ref), bufs, sems = refs[:4], refs[4:6], refs[6:10], refs[10]
    heads = arrays[0].shape[1] // DH
    half = heads // 2

    def copy(j, hd):
        at = pl.ds(hd * DH, DH)
        return pltpu.make_async_copy(
            arrays[j].at[:, at], bufs[j].at[:, at], sems.at[j, hd]
        )

    for hd in range(heads):
        for j in range(4):
            copy(j, hd).start()
    for hd in range(heads):
        at = slice(hd * DH, (hd + 1) * DH)
        for j in range(4):
            copy(j, hd).wait()
        for kind, (a, b) in enumerate(((0, 3), (1, 2))):
            s = dot(bufs[a][:, at], bufs[b][:, at], 0, 0)
            own = par_ref[0] == hd // half

            @pl.when(own)
            def _():
                keep_ref[kind, hd % half] = s

            @pl.when(own & (par_ref[0] != kind))
            def _():
                send_ref[2, hd % half] = s.astype(BF16)

            @pl.when(jnp.logical_not(own))
            def _():
                send_ref[kind, hd % half] = s.astype(BF16)


def states(par, *arrays):
    n, cols = arrays[0].shape
    heads = cols // DH
    shape = (2, heads // 2, DH, DH)
    return call(
        states_kernel,
        vmem=60,
        in_specs=[SMEM] + [pl.BlockSpec(memory_space=pltpu.HBM)] * 4,
        out_specs=[VMEM] * 2,
        out_shape=[
            jax.ShapeDtypeStruct(shape, F32),
            jax.ShapeDtypeStruct((3, *shape[1:]), BF16),
        ],
        scratch_shapes=[pltpu.VMEM((n, cols), BF16)] * 4
        + [pltpu.SemaphoreType.DMA((4, heads))],
        name="states",
    )(par, *arrays)


def split_kernel(per, par_ref, x_ref, own_ref, theirs_ref, sems):
    width = own_ref.shape[2]
    for k in range(2):

        @pl.when(par_ref[0] == k)
        def _():
            copies = []
            for i in range(per):
                for j, out_ref in enumerate((own_ref, theirs_ref)):
                    at = (2 * i + (k ^ j)) * width
                    if width % 128:
                        out_ref[i] = x_ref[:, at : at + width]
                    else:
                        src = x_ref.at[:, pl.ds(at, width)]
                        copies.append(
                            pltpu.make_async_copy(src, out_ref.at[i], sems.at[j, i])
                        )
            for c in copies:
                c.start()
            for c in copies:
                c.wait()


def split(par, x, per):
    width = x.shape[1] // (2 * per)
    out = jax.ShapeDtypeStruct((per, x.shape[0], width), x.dtype)
    place = VMEM if width % 128 else pl.BlockSpec(memory_space=pltpu.HBM)
    return call(
        functools.partial(split_kernel, per),
        in_specs=[SMEM, place],
        out_specs=[VMEM] * 2,
        out_shape=[out, out],
        scratch_shapes=[pltpu.SemaphoreType.DMA((2, per))],
        name="split",
    )(par, x)


def inside_kernel(*refs):
    arrays, (out_ref, k_ref), bufs, sems = refs[:3], refs[3:5], refs[5:8], refs[8]
    n, cols = out_ref.shape
    heads = cols // DH

    def copy(j, hd):
        at = pl.ds(hd * DH, DH)
        return pltpu.make_async_copy(
            arrays[j].at[:, at], bufs[j].at[:, at], sems.at[j, hd]
        )

    for hd in range(heads):
        for j in range(3):
            copy(j, hd).start()
    rows = lax.broadcasted_iota(jnp.int32, (n, n), 0)
    causal = rows >= lax.broadcasted_iota(jnp.int32, (n, n), 1)
    for hd in range(heads):
        at = slice(hd * DH, (hd + 1) * DH)
        for j in range(3):
            copy(j, hd).wait()
        q, k, g = (x[:, at] for x in bufs)
        scores = jnp.where(causal, dot(q, k, 1, 1), 0.0).astype(BF16)
        out_ref[:, at] = dot(scores, g, 0, 0)
        k_ref[:, at] = k


def inside(*arrays):
    n, cols = arrays[0].shape
    return call(
        inside_kernel,
        in_specs=[pl.BlockSpec(memory_space=pltpu.HBM)] * 3,
        out_specs=[VMEM] * 2,
        out_shape=[jax.ShapeDtypeStruct((n, cols), d) for d in (F32, BF16)],
        scratch_shapes=[pltpu.VMEM((n, cols), BF16)] * 3
        + [pltpu.SemaphoreType.DMA((3, cols // DH))],
        name="inside",
    )(*arrays)


def offer_kernel(pair_ref, keep_ref, got_ref, out_ref):
    sums = [(keep_ref[k] + got_ref[k].astype(F32)).astype(BF16) for k in range(2)]
    for p in range(out_ref.shape[0]):
        out_ref[p] = jnp.where(p < pair_ref[0], sums[0], sums[1])


def offer(pair, keep, got, pairs):
    return call(
        offer_kernel,
        in_specs=[SMEM, VMEM, VMEM],
        out_specs=VMEM,
        out_shape=jax.ShapeDtypeStruct((pairs, *keep.shape[1:]), BF16),
        name="offer",
    )(pair, keep, got)


def far_kernel(pair_ref, every_ref, out_ref, send_ref):
    for kind in range(2):
        total = jnp.zeros(out_ref.shape[1:], F32)
        for p in range(every_ref.shape[0]):
            reached = p > pair_ref[0] if kind == 0 else p < pair_ref[0]
            total = total + jnp.where(reached, every_ref[p].astype(F32), 0.0)
        out_ref[kind] = total
        send_ref[kind] = total.astype(BF16)


def far_states(pair, every):
    shape = (2, *every.shape[1:])
    return call(
        far_kernel,
        in_specs=[SMEM, VMEM],
        out_specs=[VMEM] * 2,
        out_shape=[jax.ShapeDtypeStruct(shape, d) for d in (F32, BF16)],
        name="far",
    )(pair, every)


def entering(par, kind, hd, half, far, got, near):
    mine = par == hd // half
    i = hd % half
    outer = jnp.where(mine, far[kind, i], got[kind, i].astype(F32))
    close = jnp.where(mine, near[kind, i], near[2, i]).astype(F32)
    total = outer + jnp.where(par == kind, close, 0.0)
    hi = total.astype(BF16)
    return hi, (total - hi.astype(F32)).astype(BF16)


def value_kernel(factor, half, par_ref, k_ref, vi_ref, *refs):
    ends, out_ref = refs[:-1], refs[-1]
    for hd in range(2 * half):
        at = slice(hd * DH, (hd + 1) * DH)
        hi, lo = entering(par_ref[0], 0, hd, half, *ends)
        k = k_ref[:, at]
        total = vi_ref[:, at] + (dot(k, hi, 1, 0) + dot(k, lo, 1, 0))
        out_ref[:, at] = (factor * total).astype(BF16)


def finish_value(factor, par, k, vi, ends):
    return call(
        functools.partial(value_kernel, factor, k.shape[1] // DH // 2),
        in_specs=[SMEM] + [VMEM] * (2 + len(ends)),
        out_specs=VMEM,
        out_shape=jax.ShapeDtypeStruct(k.shape, BF16),
        name="finish_value",
    )(par, k, vi, *ends)


def others_kernel(factor, half, par_ref, q_ref, k_ref, v_ref, g_ref, *refs):
    ends, (qo_ref, ko_ref) = refs[:-2], refs[-2:]
    hd = pl.program_id(0)
    q, k, v, g = q_ref[...], k_ref[...], v_ref[...], g_ref[...]
    n = q.shape[0]
    rows = lax.broadcasted_iota(jnp.int32, (n, n), 0)
    cols = lax.broadcasted_iota(jnp.int32, (n, n), 1)
    scores = jnp.where(rows >= cols, dot(g, v, 1, 1), 0.0).astype(BF16)
    hi, lo = entering(par_ref[0], 1, hd, half, *ends)
    total = dot(scores, k, 1, 0) + (dot(g, hi, 1, 1) + dot(g, lo, 1, 1))
    qo_ref[...] = (factor * total).astype(BF16)
    hi, lo = entering(par_ref[0], 0, hd, half, *ends)
    total = dot(scores, q, 0, 0) + (dot(v, hi, 1, 1) + dot(v, lo, 1, 1))
    ko_ref[...] = (factor * total).astype(BF16)


def others(factor, par, q, k, v, g, ends):
    n, cols = q.shape
    spec = pl.BlockSpec((n, DH), lambda h: (0, h))
    held = [pl.BlockSpec(x.shape, lambda h, d=x.ndim: (0,) * d) for x in ends]
    out = jax.ShapeDtypeStruct(q.shape, BF16)
    return call(
        functools.partial(others_kernel, factor, cols // DH // 2),
        grid=(cols // DH,),
        in_specs=[SMEM] + [spec] * 4 + held,
        out_specs=[spec] * 2,
        out_shape=[out] * 2,
        name="others",
    )(par, q, k, v, g, *ends)


def line_at(order, place):
    place = lax.rem(place + 2 * len(order), len(order))
    line = jnp.int32(order[0])
    for i, p in enumerate(order[1:], 1):
        line = jnp.where(place == i, p, line)
    return line


def piece_kernel(order, per, step, count, spot_ref, head_ref, a_ref, b_ref, *refs):
    own, theirs = refs[:count], refs[count : 2 * count]
    outs, (x, y, at, bt, sems) = refs[2 * count : -5], refs[-5:]
    line = line_at(order, spot_ref[0] - 1 - step)
    off, sub = lax.div(line, per) ^ head_ref[0], lax.rem(line, per)

    for i in range(count):

        @pl.when(off == i)
        def _():
            for j, (src, dst) in enumerate(((own, x), (theirs, y))):
                pltpu.make_async_copy(src[i].at[sub], dst, sems.at[j]).start()

    at[...] = a_ref[...].T
    bt[...] = b_ref[...].T
    for j, (src, dst) in enumerate(((own, x), (theirs, y))):
        pltpu.make_async_copy(src[0].at[0], dst, sems.at[j]).wait()
    total = dot(at[...], x[...], 1, 0) + dot(bt[...], y[...], 1, 0)
    span = outs[0].shape[0]
    for i, out_ref in enumerate(outs):
        out_ref[...] = total[i * span : (i + 1) * span].astype(out_ref.dtype)


def pieces(dtype, chains, flops, order, per, step, spot, head, a, b, own, theirs):
    count = len(own)
    _, n, width = own[0].shape
    cols = a.shape[1]
    return call(
        functools.partial(piece_kernel, order, per, step, count),
        flops=flops,
        in_specs=[SMEM] * 2 + [VMEM] * 2 + [ANY] * (2 * count),
        out_specs=[VMEM] * chains,
        out_shape=[jax.ShapeDtypeStruct((cols // chains, width), dtype)] * chains,
        scratch_shapes=[pltpu.VMEM((n, width), BF16)] * 2
        + [pltpu.VMEM((cols, n), BF16)] * 2
        + [pltpu.SemaphoreType.DMA((2,))],
        name="pieces",
    )(spot, head, a, b, *own, *theirs)


def weight_kernel(scale, *refs):
    count, out_ref = len(refs) // 2, refs[-1]
    span = refs[0].shape[0]
    for i in range(count):
        total = refs[i][...].astype(F32) + refs[count + i][...]
        out_ref[:, i * span : (i + 1) * span] = total.T * scale


def finish_weight(scale, moved, own):
    span, width = moved[0].shape
    count = len(moved)
    return call(
        functools.partial(weight_kernel, scale),
        in_specs=[VMEM] * (2 * count),
        out_specs=VMEM,
        out_shape=jax.ShapeDtypeStruct((width, span * count), F32),
        name="finish_weight",
    )(*moved, *own)


def add_kernel(moved_ref, own_ref, out_ref):
    out_ref[...] = (moved_ref[...].astype(F32) + own_ref[...]).astype(BF16)


def add_own(moved, own):
    return call(
        add_kernel,
        in_specs=[VMEM] * 2,
        out_specs=VMEM,
        out_shape=jax.ShapeDtypeStruct(moved.shape, BF16),
        name="add_own",
    )(moved, own)


def arrange_kernel(order, per, head_ref, spot_ref, *refs):
    count = len(order)
    outs, sems = refs[-3:-1], refs[-1]
    rows = refs[0].shape[0]

    def copies(s):
        p = line_at(order, spot_ref[0] - s)
        head, sub = lax.div(p, per), lax.rem(p, per)
        at = (lax.div(head, 2), pl.ds(sub * rows, rows))
        pair = [
            pltpu.make_async_copy(refs[j * count + s], outs[j].at[at], sems.at[j, s])
            for j in range(2)
        ]
        return pair, lax.rem(head, 2) == lax.rem(head_ref[0], 2)

    for act in ("start", "wait"):
        for s in range(count):
            pair, needed = copies(s)

            @pl.when(needed)
            def _():
                for c in pair:
                    getattr(c, act)()


def arrange(order, per, n_head, head, spot, blocks, lent):
    rows, cols = blocks[0].shape
    count = len(blocks)
    out = jax.ShapeDtypeStruct((n_head // 2, per * rows, cols), BF16)
    return call(
        functools.partial(arrange_kernel, order, per),
        in_specs=[SMEM] * 2 + [ANY] * (2 * count),
        out_specs=[VMEM] * 2,
        out_shape=[out] * 2,
        scratch_shapes=[pltpu.SemaphoreType.DMA((2, count))],
        name="arrange",
    )(head, spot, *blocks, *lent)


def block_product(at_ref, x_ref, y_ref, w_ref, wy_ref):
    at = at_ref[0] // 2
    return dot(x_ref[...], w_ref[at], 1, 1) + dot(y_ref[...], wy_ref[at], 1, 1)


def part_kernel(at_ref, x_ref, y_ref, w_ref, wy_ref, *refs):
    total = block_product(at_ref, x_ref, y_ref, w_ref, wy_ref)
    for got in refs[:-1]:
        total = total + got[...].astype(F32)
    refs[-1][...] = total.astype(BF16)


def head_part(at, x, y, w, wy, got=()):
    return call(
        part_kernel,
        in_specs=[SMEM] + [VMEM] * (4 + len(got)),
        out_specs=VMEM,
        out_shape=jax.ShapeDtypeStruct((x.shape[0], w.shape[1]), BF16),
        name="head_part",
    )(at, x, y, w, wy, *got)


def join_kernel(per, par_ref, at_ref, x_ref, y_ref, w_ref, wy_ref, *refs):
    total = block_product(at_ref, x_ref, y_ref, w_ref, wy_ref)
    for got in refs[:-2]:
        total = total + got[...].astype(F32)
    other_ref, out_ref = refs[-2:]
    rows = other_ref.shape[1] // per
    both = (total.astype(BF16), other_ref[...])
    for k in range(2):

        @pl.when(par_ref[0] == k)
        def _():
            for i in range(per):
                at = slice(i * rows, (i + 1) * rows)
                for j in range(2):
                    to = (2 * i + j) * rows
                    out_ref[:, to : to + rows] = both[j ^ k][:, at]


def join(par, at, per, x, y, w, wy, got, other):
    return call(
        functools.partial(join_kernel, per),
        in_specs=[SMEM] * 2 + [VMEM] * (5 + len(got)),
        out_specs=VMEM,
        out_shape=jax.ShapeDtypeStruct((x.shape[0], 2 * other.shape[1]), BF16),
        name="join",
    )(par, at, x, y, w, wy, *got, other)


def after(x, *earlier):
    return lax.optimization_barrier((x, *earlier))[0]


def local(queries, keys, values, out_grad, inputs, value_weight):
    length, cols = queries.shape
    n_ctx, n_head = lax.axis_size("ctx"), lax.axis_size("head")
    pairs = n_ctx // 2
    ctx, head = lax.axis_index("ctx"), lax.axis_index("head")
    parity, pair = ctx % 2, ctx // 2
    par = parity.astype(jnp.int32).reshape(1)
    factor = 1.0 / math.sqrt(DH * length * n_ctx)
    lines = [[2 * i + k for i in range(pairs)] for k in range(2)]
    def partner(x):
        return lax.ppermute(x, "ctx", [(i, i ^ 1) for i in range(n_ctx)])

    def across(x, bit):
        return lax.ppermute(x, "head", [(i, i ^ bit) for i in range(n_head)])

    order = list(range(0, pairs, 2)) + list(range(1, pairs, 2))[::-1]
    place = [order.index(i) for i in range(pairs)]
    moves = [
        (2 * order[i] + k, 2 * order[(i + 1) % pairs] + k)
        for i in range(pairs)
        for k in range(2)
    ]
    here = head.astype(jnp.int32).reshape(1)
    spot = line_at(place, pair.astype(jnp.int32)).reshape(1)

    def ring(x):
        return lax.ppermute(x, "ctx", moves)

    keep, send = states(par, queries, keys, values, out_grad)
    near = partner(send)
    line = pair.astype(jnp.int32).reshape(1)

    per = n_ctx // n_head // 2
    width = value_weight.shape[0]
    own, theirs = split(after(par, send), inputs, per)
    blocks = [value_weight, ring(after(value_weight, send))]
    own, theirs = [own], [partner(after(theirs, near))]

    offered = offer(line, keep, near, pairs)
    every = lax.all_to_all(
        offered, "ctx", split_axis=0, concat_axis=0, axis_index_groups=lines
    )
    far, send_far = far_states(line, every)
    ends = (far, partner(send_far), near)
    vi, keys_too = inside(after(queries, send_far), keys, out_grad)
    theirs = [after(theirs[0], send_far)]
    mine = finish_value(factor, par, keys_too, vi, ends)
    other = partner(mine)
    query_grad, key_grad = others(
        factor, par, queries, keys, after(values, mine), out_grad, ends
    )
    token = send_far
    for _ in range(2, pairs):
        blocks.append(ring(after(blocks[-1], token)))
        token = mine
    lent = [across(after(x, mine), 1) for x in blocks[:-1]]
    mine_too = across(mine, 1)

    offsets = [0]
    bit = n_head // 2
    while bit:
        own = own + [across(after(r, mine) if len(own) > 1 else r, bit) for r in own]
        theirs = theirs + [across(r, bit) for r in theirs]
        offsets = offsets + [o ^ bit for o in offsets]
        bit //= 2
    own = [own[offsets.index(i)] for i in range(n_head)]
    theirs = [theirs[offsets.index(i)] for i in range(n_head)]


    chains = 2

    def piece(dtype, step, token, flops=1):
        vals = (spot, here, after(mine, token), other, own, theirs)
        return pieces(dtype, chains, flops, order, per, step, *vals)

    total = piece(BF16, 0, query_grad, 4 * length * cols * width)
    moved = [ring(x) for x in total]
    other_too = across(after(other, total[0]), 1)
    local_part = piece(F32, 1, other_too)
    lent.append(across(after(blocks[-1], local_part[0]), 1))


    def summed_parts(x, y):
        sent = [
            head_part(here ^ off, x, y, weight, borrowed)
            for off in range(2, n_head, 2)
        ]
        return sent[-1], [across(x, 2 * i + 2) for i, x in enumerate(sent)]

    token = part = None
    for step in range(1, pairs - 1):
        if step == pairs - 2:
            last = piece(F32, pairs - 1, token)
            token = last[0]
        for i in range(chains):
            if step == pairs - 2 and i == chains - 1:
                lead = (here, after(other, token), other_too, weight, borrowed)
                token = part = head_part(*lead, got_other)
            own_part = local_part[i] if token is None else after(local_part[i], token)
            token = add_own(moved[i], own_part)
            moved[i] = ring(token)
            if step == 1 and i == 0:
                held = [after(blocks[0], token)] + blocks[1:]
                weight, borrowed = arrange(order, per, n_head, here, spot, held, lent)
                token, got_other = summed_parts(other, other_too)
            elif step == 1 and i == chains - 1:
                token, got_mine = summed_parts(after(mine, token), mine_too)
        if step < pairs - 2:
            local_part = piece(F32, step + 1, token)
            token = local_part[0]
    swapped = partner(part)
    weight_grad = finish_weight(1.0 / math.sqrt(length * n_ctx), moved, last)
    mine = after(mine, weight_grad)
    input_grad = join(
        par, here, per, mine, mine_too, weight, borrowed, got_mine, swapped
    )
    return (query_grad, key_grad, input_grad, weight_grad)


def solution(mesh):
    spec = P("ctx", "head")
    return jax.shard_map(
        local, mesh=mesh, in_specs=(spec,) * 6, out_specs=(spec,) * 4, check_vma=False
    )
```

```python
import functools
import math

import jax
import jax.numpy as jnp
from jax import lax
from jax.experimental import pallas as pl
from jax.experimental.pallas import tpu as pltpu
from jax.sharding import PartitionSpec as P

DH = 128
F32, BF16 = jnp.float32, jnp.bfloat16
VMEM = pl.BlockSpec(memory_space=pltpu.VMEM)
SMEM = pl.BlockSpec(memory_space=pltpu.SMEM)
ANY = pl.BlockSpec(memory_space=pl.ANY)


def dot(a, b, ca, cb):
    return lax.dot_general(a, b, (((ca,), (cb,)), ((), ())), preferred_element_type=F32)


def call(kernel, vmem=16, flops=1, **kw):
    hint = pl.CostEstimate(flops=flops, bytes_accessed=1, transcendentals=0)
    params = pltpu.CompilerParams(vmem_limit_bytes=vmem * 2**20)
    return pl.pallas_call(kernel, cost_estimate=hint, compiler_params=params, **kw)


def states_kernel(par_ref, *refs):
    arrays, (keep_ref, send_ref), bufs, sems = refs[:4], refs[4:6], refs[6:10], refs[10]
    heads = arrays[0].shape[1] // DH
    half = heads // 2

    def copy(j, hd):
        at = pl.ds(hd * DH, DH)
        return pltpu.make_async_copy(
            arrays[j].at[:, at], bufs[j].at[:, at], sems.at[j, hd]
        )

    for hd in range(heads):
        for j in range(4):
            copy(j, hd).start()
    for hd in range(heads):
        at = slice(hd * DH, (hd + 1) * DH)
        for j in range(4):
            copy(j, hd).wait()
        for kind, (a, b) in enumerate(((0, 3), (1, 2))):
            s = dot(bufs[a][:, at], bufs[b][:, at], 0, 0)
            own = par_ref[0] == hd // half

            @pl.when(own)
            def _():
                keep_ref[kind, hd % half] = s

            @pl.when(own & (par_ref[0] != kind))
            def _():
                send_ref[2, hd % half] = s.astype(BF16)

            @pl.when(jnp.logical_not(own))
            def _():
                send_ref[kind, hd % half] = s.astype(BF16)


def states(par, *arrays):
    n, cols = arrays[0].shape
    heads = cols // DH
    shape = (2, heads // 2, DH, DH)
    return call(
        states_kernel,
        vmem=60,
        in_specs=[SMEM] + [pl.BlockSpec(memory_space=pltpu.HBM)] * 4,
        out_specs=[VMEM] * 2,
        out_shape=[
            jax.ShapeDtypeStruct(shape, F32),
            jax.ShapeDtypeStruct((3, *shape[1:]), BF16),
        ],
        scratch_shapes=[pltpu.VMEM((n, cols), BF16)] * 4
        + [pltpu.SemaphoreType.DMA((4, heads))],
        name="states",
    )(par, *arrays)


def split_kernel(per, par_ref, x_ref, own_ref, theirs_ref, sems):
    width = own_ref.shape[2]
    for k in range(2):

        @pl.when(par_ref[0] == k)
        def _():
            copies = []
            for i in range(per):
                for j, out_ref in enumerate((own_ref, theirs_ref)):
                    at = (2 * i + (k ^ j)) * width
                    if width % 128:
                        out_ref[i] = x_ref[:, at : at + width]
                    else:
                        src = x_ref.at[:, pl.ds(at, width)]
                        copies.append(
                            pltpu.make_async_copy(src, out_ref.at[i], sems.at[j, i])
                        )
            for c in copies:
                c.start()
            for c in copies:
                c.wait()


def split(par, x, per):
    width = x.shape[1] // (2 * per)
    out = jax.ShapeDtypeStruct((per, x.shape[0], width), x.dtype)
    place = VMEM if width % 128 else pl.BlockSpec(memory_space=pltpu.HBM)
    return call(
        functools.partial(split_kernel, per),
        in_specs=[SMEM, place],
        out_specs=[VMEM] * 2,
        out_shape=[out, out],
        scratch_shapes=[pltpu.SemaphoreType.DMA((2, per))],
        name="split",
    )(par, x)


def inside_kernel(*refs):
    arrays, (out_ref, k_ref), bufs, sems = refs[:3], refs[3:5], refs[5:8], refs[8]
    n, cols = out_ref.shape
    heads = cols // DH

    def copy(j, hd):
        at = pl.ds(hd * DH, DH)
        return pltpu.make_async_copy(
            arrays[j].at[:, at], bufs[j].at[:, at], sems.at[j, hd]
        )

    for hd in range(heads):
        for j in range(3):
            copy(j, hd).start()
    rows = lax.broadcasted_iota(jnp.int32, (n, n), 0)
    causal = rows >= lax.broadcasted_iota(jnp.int32, (n, n), 1)
    for hd in range(heads):
        at = slice(hd * DH, (hd + 1) * DH)
        for j in range(3):
            copy(j, hd).wait()
        q, k, g = (x[:, at] for x in bufs)
        scores = jnp.where(causal, dot(q, k, 1, 1), 0.0).astype(BF16)
        out_ref[:, at] = dot(scores, g, 0, 0)
        k_ref[:, at] = k


def inside(*arrays):
    n, cols = arrays[0].shape
    return call(
        inside_kernel,
        in_specs=[pl.BlockSpec(memory_space=pltpu.HBM)] * 3,
        out_specs=[VMEM] * 2,
        out_shape=[jax.ShapeDtypeStruct((n, cols), d) for d in (F32, BF16)],
        scratch_shapes=[pltpu.VMEM((n, cols), BF16)] * 3
        + [pltpu.SemaphoreType.DMA((3, cols // DH))],
        name="inside",
    )(*arrays)


def offer_kernel(pair_ref, keep_ref, got_ref, out_ref):
    sums = [(keep_ref[k] + got_ref[k].astype(F32)).astype(BF16) for k in range(2)]
    for p in range(out_ref.shape[0]):
        out_ref[p] = jnp.where(p < pair_ref[0], sums[0], sums[1])


def offer(pair, keep, got, pairs):
    return call(
        offer_kernel,
        in_specs=[SMEM, VMEM, VMEM],
        out_specs=VMEM,
        out_shape=jax.ShapeDtypeStruct((pairs, *keep.shape[1:]), BF16),
        name="offer",
    )(pair, keep, got)


def far_kernel(pair_ref, every_ref, out_ref, send_ref):
    for kind in range(2):
        total = jnp.zeros(out_ref.shape[1:], F32)
        for p in range(every_ref.shape[0]):
            reached = p > pair_ref[0] if kind == 0 else p < pair_ref[0]
            total = total + jnp.where(reached, every_ref[p].astype(F32), 0.0)
        out_ref[kind] = total
        send_ref[kind] = total.astype(BF16)


def far_states(pair, every):
    shape = (2, *every.shape[1:])
    return call(
        far_kernel,
        in_specs=[SMEM, VMEM],
        out_specs=[VMEM] * 2,
        out_shape=[jax.ShapeDtypeStruct(shape, d) for d in (F32, BF16)],
        name="far",
    )(pair, every)


def entering(par, kind, hd, half, far, got, near):
    mine = par == hd // half
    i = hd % half
    outer = jnp.where(mine, far[kind, i], got[kind, i].astype(F32))
    close = jnp.where(mine, near[kind, i], near[2, i]).astype(F32)
    total = outer + jnp.where(par == kind, close, 0.0)
    hi = total.astype(BF16)
    return hi, (total - hi.astype(F32)).astype(BF16)


def value_kernel(factor, half, par_ref, k_ref, vi_ref, *refs):
    ends, out_ref = refs[:-1], refs[-1]
    for hd in range(2 * half):
        at = slice(hd * DH, (hd + 1) * DH)
        hi, lo = entering(par_ref[0], 0, hd, half, *ends)
        k = k_ref[:, at]
        total = vi_ref[:, at] + (dot(k, hi, 1, 0) + dot(k, lo, 1, 0))
        out_ref[:, at] = (factor * total).astype(BF16)


def finish_value(factor, par, k, vi, ends):
    return call(
        functools.partial(value_kernel, factor, k.shape[1] // DH // 2),
        in_specs=[SMEM] + [VMEM] * (2 + len(ends)),
        out_specs=VMEM,
        out_shape=jax.ShapeDtypeStruct(k.shape, BF16),
        name="finish_value",
    )(par, k, vi, *ends)


def others_kernel(factor, half, par_ref, q_ref, k_ref, v_ref, g_ref, *refs):
    ends, (qo_ref, ko_ref) = refs[:-2], refs[-2:]
    hd = pl.program_id(0)
    q, k, v, g = q_ref[...], k_ref[...], v_ref[...], g_ref[...]
    n = q.shape[0]
    rows = lax.broadcasted_iota(jnp.int32, (n, n), 0)
    cols = lax.broadcasted_iota(jnp.int32, (n, n), 1)
    scores = jnp.where(rows >= cols, dot(g, v, 1, 1), 0.0).astype(BF16)
    hi, lo = entering(par_ref[0], 1, hd, half, *ends)
    total = dot(scores, k, 1, 0) + (dot(g, hi, 1, 1) + dot(g, lo, 1, 1))
    qo_ref[...] = (factor * total).astype(BF16)
    hi, lo = entering(par_ref[0], 0, hd, half, *ends)
    total = dot(scores, q, 0, 0) + (dot(v, hi, 1, 1) + dot(v, lo, 1, 1))
    ko_ref[...] = (factor * total).astype(BF16)


def others(factor, par, q, k, v, g, ends):
    n, cols = q.shape
    spec = pl.BlockSpec((n, DH), lambda h: (0, h))
    held = [pl.BlockSpec(x.shape, lambda h, d=x.ndim: (0,) * d) for x in ends]
    out = jax.ShapeDtypeStruct(q.shape, BF16)
    return call(
        functools.partial(others_kernel, factor, cols // DH // 2),
        grid=(cols // DH,),
        in_specs=[SMEM] + [spec] * 4 + held,
        out_specs=[spec] * 2,
        out_shape=[out] * 2,
        name="others",
    )(par, q, k, v, g, *ends)


def line_at(order, place):
    place = lax.rem(place + 2 * len(order), len(order))
    line = jnp.int32(order[0])
    for i, p in enumerate(order[1:], 1):
        line = jnp.where(place == i, p, line)
    return line


def piece_kernel(order, per, step, count, spot_ref, head_ref, a_ref, b_ref, *refs):
    own, theirs = refs[:count], refs[count : 2 * count]
    outs, (x, y, at, bt, sems) = refs[2 * count : -5], refs[-5:]
    line = line_at(order, spot_ref[0] - 1 - step)
    off, sub = lax.div(line, per) ^ head_ref[0], lax.rem(line, per)

    for i in range(count):

        @pl.when(off == i)
        def _():
            for j, (src, dst) in enumerate(((own, x), (theirs, y))):
                pltpu.make_async_copy(src[i].at[sub], dst, sems.at[j]).start()

    at[...] = a_ref[...].T
    bt[...] = b_ref[...].T
    for j, (src, dst) in enumerate(((own, x), (theirs, y))):
        pltpu.make_async_copy(src[0].at[0], dst, sems.at[j]).wait()
    total = dot(at[...], x[...], 1, 0) + dot(bt[...], y[...], 1, 0)
    span = outs[0].shape[0]
    for i, out_ref in enumerate(outs):
        out_ref[...] = total[i * span : (i + 1) * span].astype(out_ref.dtype)


def pieces(dtype, chains, flops, order, per, step, spot, head, a, b, own, theirs):
    count = len(own)
    _, n, width = own[0].shape
    cols = a.shape[1]
    return call(
        functools.partial(piece_kernel, order, per, step, count),
        flops=flops,
        in_specs=[SMEM] * 2 + [VMEM] * 2 + [ANY] * (2 * count),
        out_specs=[VMEM] * chains,
        out_shape=[jax.ShapeDtypeStruct((cols // chains, width), dtype)] * chains,
        scratch_shapes=[pltpu.VMEM((n, width), BF16)] * 2
        + [pltpu.VMEM((cols, n), BF16)] * 2
        + [pltpu.SemaphoreType.DMA((2,))],
        name="pieces",
    )(spot, head, a, b, *own, *theirs)


def weight_kernel(scale, *refs):
    count, out_ref = len(refs) // 2, refs[-1]
    span = refs[0].shape[0]
    for i in range(count):
        total = refs[i][...].astype(F32) + refs[count + i][...]
        out_ref[:, i * span : (i + 1) * span] = total.T * scale


def finish_weight(scale, moved, own):
    span, width = moved[0].shape
    count = len(moved)
    return call(
        functools.partial(weight_kernel, scale),
        in_specs=[VMEM] * (2 * count),
        out_specs=VMEM,
        out_shape=jax.ShapeDtypeStruct((width, span * count), F32),
        name="finish_weight",
    )(*moved, *own)


def add_kernel(moved_ref, own_ref, out_ref):
    out_ref[...] = (moved_ref[...].astype(F32) + own_ref[...]).astype(BF16)


def add_own(moved, part, own):
    return call(
        add_kernel,
        grid=(1,),
        in_specs=[
            pl.BlockSpec(own.shape, lambda s: (part, 0)),
            pl.BlockSpec(own.shape, lambda s: (0, 0)),
        ],
        out_specs=pl.BlockSpec(own.shape, lambda s: (0, 0)),
        out_shape=jax.ShapeDtypeStruct(own.shape, BF16),
        name="add_own",
    )(moved, own)


def arrange_kernel(order, per, head_ref, spot_ref, *refs):
    count = len(order)
    outs, sems = refs[-3:-1], refs[-1]
    rows = refs[0].shape[0]

    def copies(s):
        p = line_at(order, spot_ref[0] - s)
        head, sub = lax.div(p, per), lax.rem(p, per)
        at = (lax.div(head, 2), pl.ds(sub * rows, rows))
        pair = [
            pltpu.make_async_copy(refs[j * count + s], outs[j].at[at], sems.at[j, s])
            for j in range(2)
        ]
        return pair, lax.rem(head, 2) == lax.rem(head_ref[0], 2)

    for act in ("start", "wait"):
        for s in range(count):
            pair, needed = copies(s)

            @pl.when(needed)
            def _():
                for c in pair:
                    getattr(c, act)()


def arrange(order, per, n_head, head, spot, blocks, lent):
    rows, cols = blocks[0].shape
    count = len(blocks)
    out = jax.ShapeDtypeStruct((n_head // 2, per * rows, cols), BF16)
    return call(
        functools.partial(arrange_kernel, order, per),
        in_specs=[SMEM] * 2 + [ANY] * (2 * count),
        out_specs=[VMEM] * 2,
        out_shape=[out] * 2,
        scratch_shapes=[pltpu.SemaphoreType.DMA((2, count))],
        name="arrange",
    )(head, spot, *blocks, *lent)


def block_product(at_ref, x_ref, y_ref, w_ref, wy_ref):
    at = at_ref[0] // 2
    return dot(x_ref[...], w_ref[at], 1, 1) + dot(y_ref[...], wy_ref[at], 1, 1)


def part_kernel(at_ref, x_ref, y_ref, w_ref, wy_ref, *refs):
    total = block_product(at_ref, x_ref, y_ref, w_ref, wy_ref)
    for got in refs[:-1]:
        total = total + got[...].astype(F32)
    refs[-1][...] = total.astype(BF16)


def head_part(at, x, y, w, wy, got=()):
    return call(
        part_kernel,
        in_specs=[SMEM] + [VMEM] * (4 + len(got)),
        out_specs=VMEM,
        out_shape=jax.ShapeDtypeStruct((x.shape[0], w.shape[1]), BF16),
        name="head_part",
    )(at, x, y, w, wy, *got)


def join_kernel(per, par_ref, at_ref, x_ref, y_ref, w_ref, wy_ref, *refs):
    total = block_product(at_ref, x_ref, y_ref, w_ref, wy_ref)
    for got in refs[:-2]:
        total = total + got[...].astype(F32)
    other_ref, out_ref = refs[-2:]
    rows = other_ref.shape[1] // per
    both = (total.astype(BF16), other_ref[...])
    for k in range(2):

        @pl.when(par_ref[0] == k)
        def _():
            for i in range(per):
                at = slice(i * rows, (i + 1) * rows)
                for j in range(2):
                    to = (2 * i + j) * rows
                    out_ref[:, to : to + rows] = both[j ^ k][:, at]


def join(par, at, per, x, y, w, wy, got, other):
    return call(
        functools.partial(join_kernel, per),
        in_specs=[SMEM] * 2 + [VMEM] * (5 + len(got)),
        out_specs=VMEM,
        out_shape=jax.ShapeDtypeStruct((x.shape[0], 2 * other.shape[1]), BF16),
        name="join",
    )(par, at, x, y, w, wy, *got, other)


def after(x, *earlier):
    return lax.optimization_barrier((x, *earlier))[0]


def local(queries, keys, values, out_grad, inputs, value_weight):
    length, cols = queries.shape
    n_ctx, n_head = lax.axis_size("ctx"), lax.axis_size("head")
    pairs = n_ctx // 2
    ctx, head = lax.axis_index("ctx"), lax.axis_index("head")
    parity, pair = ctx % 2, ctx // 2
    par = parity.astype(jnp.int32).reshape(1)
    factor = 1.0 / math.sqrt(DH * length * n_ctx)
    lines = [[2 * i + k for i in range(pairs)] for k in range(2)]
    def partner(x):
        return lax.ppermute(x, "ctx", [(i, i ^ 1) for i in range(n_ctx)])

    def across(x, bit):
        return lax.ppermute(x, "head", [(i, i ^ bit) for i in range(n_head)])

    order = list(range(0, pairs, 2)) + list(range(1, pairs, 2))[::-1]
    place = [order.index(i) for i in range(pairs)]
    moves = [
        (2 * order[i] + k, 2 * order[(i + 1) % pairs] + k)
        for i in range(pairs)
        for k in range(2)
    ]
    here = head.astype(jnp.int32).reshape(1)
    spot = line_at(place, pair.astype(jnp.int32)).reshape(1)

    def ring(x):
        return lax.ppermute(x, "ctx", moves)

    keep, send = states(par, queries, keys, values, out_grad)
    near = partner(send)
    line = pair.astype(jnp.int32).reshape(1)

    per = n_ctx // n_head // 2
    width = value_weight.shape[0]
    own, theirs = split(after(par, send), inputs, per)
    blocks = [value_weight, ring(after(value_weight, send))]
    own, theirs = [own], [partner(after(theirs, near))]

    offered = offer(line, keep, near, pairs)
    every = lax.all_to_all(
        offered, "ctx", split_axis=0, concat_axis=0, axis_index_groups=lines
    )
    far, send_far = far_states(line, every)
    ends = (far, partner(send_far), near)
    vi, keys_too = inside(after(queries, send_far), keys, out_grad)
    theirs = [after(theirs[0], send_far)]
    mine = finish_value(factor, par, keys_too, vi, ends)
    other = partner(mine)
    query_grad, key_grad = others(
        factor, par, queries, keys, after(values, mine), out_grad, ends
    )
    token = send_far
    for _ in range(2, pairs):
        blocks.append(ring(after(blocks[-1], token)))
        token = mine
    lent = [across(after(x, mine), 1) for x in blocks[:-1]]
    mine_too = across(mine, 1)

    offsets = [0]
    bit = n_head // 2
    while bit:
        own = own + [across(after(r, mine) if len(own) > 1 else r, bit) for r in own]
        theirs = theirs + [across(r, bit) for r in theirs]
        offsets = offsets + [o ^ bit for o in offsets]
        bit //= 2
    own = [own[offsets.index(i)] for i in range(n_head)]
    theirs = [theirs[offsets.index(i)] for i in range(n_head)]


    chains = 2

    def piece(dtype, step, token, chains=chains, flops=1):
        vals = (spot, here, after(mine, token), other, own, theirs)
        return pieces(dtype, chains, flops, order, per, step, *vals)

    total = piece(BF16, 0, query_grad, 1, 4 * length * cols * width)
    moved = [ring(total[0])] * chains
    other_too = across(other, 1)
    lent.append(across(after(blocks[-1], total[0]), 1))
    local_part = piece(F32, 1, total[0])


    def summed_parts(x, y):
        sent = [
            head_part(here ^ off, x, y, weight, borrowed)
            for off in range(2, n_head, 2)
        ]
        return sent[-1], [across(x, 2 * i + 2) for i, x in enumerate(sent)]

    held = [after(blocks[0], local_part[0])] + blocks[1:]
    weight, borrowed = arrange(order, per, n_head, here, spot, held, lent)
    token, got_other = summed_parts(other, other_too)
    token, got_mine = summed_parts(after(mine, token), mine_too)
    part = None
    for step in range(1, pairs - 1):
        if step == pairs - 2:
            last = piece(F32, pairs - 1, token)
            token = last[0]
        for i in range(chains):
            if step == pairs - 2 and i == chains - 1:
                lead = (here, after(other, token), other_too, weight, borrowed)
                token = part = head_part(*lead, got_other)
            at = i if step == 1 else 0
            token = add_own(moved[i], at, after(local_part[i], token))
            moved[i] = ring(token)
        if step < pairs - 2:
            local_part = piece(F32, step + 1, token)
            token = local_part[0]
    swapped = partner(part)
    weight_grad = finish_weight(1.0 / math.sqrt(length * n_ctx), moved, last)
    mine = after(mine, weight_grad)
    input_grad = join(
        par, here, per, mine, mine_too, weight, borrowed, got_mine, swapped
    )
    return (query_grad, key_grad, input_grad, weight_grad)


def solution(mesh):
    spec = P("ctx", "head")
    return jax.shard_map(
        local, mesh=mesh, in_specs=(spec,) * 6, out_specs=(spec,) * 4, check_vma=False
    )
```

```python
import functools
import math

import jax
import jax.numpy as jnp
from jax import lax
from jax.experimental import pallas as pl
from jax.experimental.pallas import tpu as pltpu
from jax.sharding import PartitionSpec as P

DH = 128
F32, BF16 = jnp.float32, jnp.bfloat16
VMEM = pl.BlockSpec(memory_space=pltpu.VMEM)
SMEM = pl.BlockSpec(memory_space=pltpu.SMEM)
ANY = pl.BlockSpec(memory_space=pl.ANY)


def dot(a, b, ca, cb):
    return lax.dot_general(a, b, (((ca,), (cb,)), ((), ())), preferred_element_type=F32)


def call(kernel, vmem=16, flops=1, **kw):
    hint = pl.CostEstimate(flops=flops, bytes_accessed=1, transcendentals=0)
    params = pltpu.CompilerParams(vmem_limit_bytes=vmem * 2**20)
    return pl.pallas_call(kernel, cost_estimate=hint, compiler_params=params, **kw)


def states_kernel(par_ref, *refs):
    arrays, (keep_ref, send_ref), bufs, sems = refs[:4], refs[4:6], refs[6:10], refs[10]
    heads = arrays[0].shape[1] // DH
    half = heads // 2

    def copy(j, hd):
        at = pl.ds(hd * DH, DH)
        return pltpu.make_async_copy(
            arrays[j].at[:, at], bufs[j].at[:, at], sems.at[j, hd]
        )

    for hd in range(heads):
        for j in range(4):
            copy(j, hd).start()
    for hd in range(heads):
        at = slice(hd * DH, (hd + 1) * DH)
        for j in range(4):
            copy(j, hd).wait()
        for kind, (a, b) in enumerate(((0, 3), (1, 2))):
            s = dot(bufs[a][:, at], bufs[b][:, at], 0, 0)
            own = par_ref[0] == hd // half

            @pl.when(own)
            def _():
                keep_ref[kind, hd % half] = s

            @pl.when(own & (par_ref[0] != kind))
            def _():
                send_ref[2, hd % half] = s.astype(BF16)

            @pl.when(jnp.logical_not(own))
            def _():
                send_ref[kind, hd % half] = s.astype(BF16)


def states(par, *arrays):
    n, cols = arrays[0].shape
    heads = cols // DH
    shape = (2, heads // 2, DH, DH)
    return call(
        states_kernel,
        vmem=60,
        in_specs=[SMEM] + [pl.BlockSpec(memory_space=pltpu.HBM)] * 4,
        out_specs=[VMEM] * 2,
        out_shape=[
            jax.ShapeDtypeStruct(shape, F32),
            jax.ShapeDtypeStruct((3, *shape[1:]), BF16),
        ],
        scratch_shapes=[pltpu.VMEM((n, cols), BF16)] * 4
        + [pltpu.SemaphoreType.DMA((4, heads))],
        name="states",
    )(par, *arrays)


def split_kernel(per, par_ref, x_ref, own_ref, theirs_ref, sems):
    width = own_ref.shape[2]
    for k in range(2):

        @pl.when(par_ref[0] == k)
        def _():
            copies = []
            for i in range(per):
                for j, out_ref in enumerate((own_ref, theirs_ref)):
                    at = (2 * i + (k ^ j)) * width
                    if width % 128:
                        out_ref[i] = x_ref[:, at : at + width]
                    else:
                        src = x_ref.at[:, pl.ds(at, width)]
                        copies.append(
                            pltpu.make_async_copy(src, out_ref.at[i], sems.at[j, i])
                        )
            for c in copies:
                c.start()
            for c in copies:
                c.wait()


def split(par, x, per):
    width = x.shape[1] // (2 * per)
    out = jax.ShapeDtypeStruct((per, x.shape[0], width), x.dtype)
    place = VMEM if width % 128 else pl.BlockSpec(memory_space=pltpu.HBM)
    return call(
        functools.partial(split_kernel, per),
        in_specs=[SMEM, place],
        out_specs=[VMEM] * 2,
        out_shape=[out, out],
        scratch_shapes=[pltpu.SemaphoreType.DMA((2, per))],
        name="split",
    )(par, x)


def inside_kernel(*refs):
    arrays, (out_ref, k_ref), bufs, sems = refs[:3], refs[3:5], refs[5:8], refs[8]
    n, cols = out_ref.shape
    heads = cols // DH

    def copy(j, hd):
        at = pl.ds(hd * DH, DH)
        return pltpu.make_async_copy(
            arrays[j].at[:, at], bufs[j].at[:, at], sems.at[j, hd]
        )

    for hd in range(heads):
        for j in range(3):
            copy(j, hd).start()
    rows = lax.broadcasted_iota(jnp.int32, (n, n), 0)
    causal = rows >= lax.broadcasted_iota(jnp.int32, (n, n), 1)
    for hd in range(heads):
        at = slice(hd * DH, (hd + 1) * DH)
        for j in range(3):
            copy(j, hd).wait()
        q, k, g = (x[:, at] for x in bufs)
        scores = jnp.where(causal, dot(q, k, 1, 1), 0.0).astype(BF16)
        out_ref[:, at] = dot(scores, g, 0, 0)
        k_ref[:, at] = k


def inside(*arrays):
    n, cols = arrays[0].shape
    return call(
        inside_kernel,
        in_specs=[pl.BlockSpec(memory_space=pltpu.HBM)] * 3,
        out_specs=[VMEM] * 2,
        out_shape=[jax.ShapeDtypeStruct((n, cols), d) for d in (F32, BF16)],
        scratch_shapes=[pltpu.VMEM((n, cols), BF16)] * 3
        + [pltpu.SemaphoreType.DMA((3, cols // DH))],
        name="inside",
    )(*arrays)


def offer_kernel(pair_ref, keep_ref, got_ref, out_ref):
    sums = [(keep_ref[k] + got_ref[k].astype(F32)).astype(BF16) for k in range(2)]
    for p in range(out_ref.shape[0]):
        out_ref[p] = jnp.where(p < pair_ref[0], sums[0], sums[1])


def offer(pair, keep, got, pairs):
    return call(
        offer_kernel,
        in_specs=[SMEM, VMEM, VMEM],
        out_specs=VMEM,
        out_shape=jax.ShapeDtypeStruct((pairs, *keep.shape[1:]), BF16),
        name="offer",
    )(pair, keep, got)


def far_kernel(pair_ref, every_ref, out_ref, send_ref):
    for kind in range(2):
        total = jnp.zeros(out_ref.shape[1:], F32)
        for p in range(every_ref.shape[0]):
            reached = p > pair_ref[0] if kind == 0 else p < pair_ref[0]
            total = total + jnp.where(reached, every_ref[p].astype(F32), 0.0)
        out_ref[kind] = total
        send_ref[kind] = total.astype(BF16)


def far_states(pair, every):
    shape = (2, *every.shape[1:])
    return call(
        far_kernel,
        in_specs=[SMEM, VMEM],
        out_specs=[VMEM] * 2,
        out_shape=[jax.ShapeDtypeStruct(shape, d) for d in (F32, BF16)],
        name="far",
    )(pair, every)


def entering(par, kind, hd, half, far, got, near):
    mine = par == hd // half
    i = hd % half
    outer = jnp.where(mine, far[kind, i], got[kind, i].astype(F32))
    close = jnp.where(mine, near[kind, i], near[2, i]).astype(F32)
    total = outer + jnp.where(par == kind, close, 0.0)
    hi = total.astype(BF16)
    return hi, (total - hi.astype(F32)).astype(BF16)


def value_kernel(factor, half, par_ref, k_ref, vi_ref, *refs):
    ends, out_ref = refs[:-1], refs[-1]
    for hd in range(2 * half):
        at = slice(hd * DH, (hd + 1) * DH)
        hi, lo = entering(par_ref[0], 0, hd, half, *ends)
        k = k_ref[:, at]
        total = vi_ref[:, at] + (dot(k, hi, 1, 0) + dot(k, lo, 1, 0))
        out_ref[:, at] = (factor * total).astype(BF16)


def finish_value(factor, par, k, vi, ends):
    return call(
        functools.partial(value_kernel, factor, k.shape[1] // DH // 2),
        in_specs=[SMEM] + [VMEM] * (2 + len(ends)),
        out_specs=VMEM,
        out_shape=jax.ShapeDtypeStruct(k.shape, BF16),
        name="finish_value",
    )(par, k, vi, *ends)


def others_kernel(factor, half, par_ref, q_ref, k_ref, v_ref, g_ref, *refs):
    ends, (qo_ref, ko_ref) = refs[:-2], refs[-2:]
    hd = pl.program_id(0)
    q, k, v, g = q_ref[...], k_ref[...], v_ref[...], g_ref[...]
    n = q.shape[0]
    rows = lax.broadcasted_iota(jnp.int32, (n, n), 0)
    cols = lax.broadcasted_iota(jnp.int32, (n, n), 1)
    scores = jnp.where(rows >= cols, dot(g, v, 1, 1), 0.0).astype(BF16)
    hi, lo = entering(par_ref[0], 1, hd, half, *ends)
    total = dot(scores, k, 1, 0) + (dot(g, hi, 1, 1) + dot(g, lo, 1, 1))
    qo_ref[...] = (factor * total).astype(BF16)
    hi, lo = entering(par_ref[0], 0, hd, half, *ends)
    total = dot(scores, q, 0, 0) + (dot(v, hi, 1, 1) + dot(v, lo, 1, 1))
    ko_ref[...] = (factor * total).astype(BF16)


def others(factor, par, q, k, v, g, ends):
    n, cols = q.shape
    spec = pl.BlockSpec((n, DH), lambda h: (0, h))
    held = [pl.BlockSpec(x.shape, lambda h, d=x.ndim: (0,) * d) for x in ends]
    out = jax.ShapeDtypeStruct(q.shape, BF16)
    return call(
        functools.partial(others_kernel, factor, cols // DH // 2),
        grid=(cols // DH,),
        in_specs=[SMEM] + [spec] * 4 + held,
        out_specs=[spec] * 2,
        out_shape=[out] * 2,
        name="others",
    )(par, q, k, v, g, *ends)


def line_at(order, place):
    place = lax.rem(place + 2 * len(order), len(order))
    line = jnp.int32(order[0])
    for i, p in enumerate(order[1:], 1):
        line = jnp.where(place == i, p, line)
    return line


def piece_kernel(order, per, step, count, spot_ref, head_ref, a_ref, b_ref, *refs):
    own, theirs = refs[:count], refs[count : 2 * count]
    outs, (x, y, at, bt, sems) = refs[2 * count : -5], refs[-5:]
    line = line_at(order, spot_ref[0] - 1 - step)
    off, sub = lax.div(line, per) ^ head_ref[0], lax.rem(line, per)

    for i in range(count):

        @pl.when(off == i)
        def _():
            for j, (src, dst) in enumerate(((own, x), (theirs, y))):
                pltpu.make_async_copy(src[i].at[sub], dst, sems.at[j]).start()

    at[...] = a_ref[...].T
    bt[...] = b_ref[...].T
    for j, (src, dst) in enumerate(((own, x), (theirs, y))):
        pltpu.make_async_copy(src[0].at[0], dst, sems.at[j]).wait()
    total = dot(at[...], x[...], 1, 0) + dot(bt[...], y[...], 1, 0)
    span = outs[0].shape[0]
    for i, out_ref in enumerate(outs):
        out_ref[...] = total[i * span : (i + 1) * span].astype(out_ref.dtype)


def pieces(dtype, chains, flops, order, per, step, spot, head, a, b, own, theirs):
    count = len(own)
    _, n, width = own[0].shape
    cols = a.shape[1]
    return call(
        functools.partial(piece_kernel, order, per, step, count),
        flops=flops,
        in_specs=[SMEM] * 2 + [VMEM] * 2 + [ANY] * (2 * count),
        out_specs=[VMEM] * chains,
        out_shape=[jax.ShapeDtypeStruct((cols // chains, width), dtype)] * chains,
        scratch_shapes=[pltpu.VMEM((n, width), BF16)] * 2
        + [pltpu.VMEM((cols, n), BF16)] * 2
        + [pltpu.SemaphoreType.DMA((2,))],
        name="pieces",
    )(spot, head, a, b, *own, *theirs)


def weight_kernel(scale, *refs):
    count, out_ref = len(refs) // 2, refs[-1]
    span = refs[0].shape[0]
    for i in range(count):
        total = refs[i][...].astype(F32) + refs[count + i][...]
        out_ref[:, i * span : (i + 1) * span] = total.T * scale


def finish_weight(scale, moved, own):
    span, width = moved[0].shape
    count = len(moved)
    return call(
        functools.partial(weight_kernel, scale),
        in_specs=[VMEM] * (2 * count),
        out_specs=VMEM,
        out_shape=jax.ShapeDtypeStruct((width, span * count), F32),
        name="finish_weight",
    )(*moved, *own)


def add_kernel(moved_ref, own_ref, out_ref):
    out_ref[...] = (moved_ref[...].astype(F32) + own_ref[...]).astype(BF16)


def add_own(moved, own):
    return call(
        add_kernel,
        in_specs=[VMEM] * 2,
        out_specs=VMEM,
        out_shape=jax.ShapeDtypeStruct(moved.shape, BF16),
        name="add_own",
    )(moved, own)


def arrange_kernel(order, per, head_ref, spot_ref, *refs):
    count = len(order)
    outs, sems = refs[-3:-1], refs[-1]
    rows = refs[0].shape[0]

    def copies(s):
        p = line_at(order, spot_ref[0] - s)
        head, sub = lax.div(p, per), lax.rem(p, per)
        at = (lax.div(head, 2), pl.ds(sub * rows, rows))
        pair = [
            pltpu.make_async_copy(refs[j * count + s], outs[j].at[at], sems.at[j, s])
            for j in range(2)
        ]
        return pair, lax.rem(head, 2) == lax.rem(head_ref[0], 2)

    for act in ("start", "wait"):
        for s in range(count):
            pair, needed = copies(s)

            @pl.when(needed)
            def _():
                for c in pair:
                    getattr(c, act)()


def arrange(order, per, n_head, head, spot, blocks, lent):
    rows, cols = blocks[0].shape
    count = len(blocks)
    out = jax.ShapeDtypeStruct((n_head // 2, per * rows, cols), BF16)
    return call(
        functools.partial(arrange_kernel, order, per),
        in_specs=[SMEM] * 2 + [ANY] * (2 * count),
        out_specs=[VMEM] * 2,
        out_shape=[out] * 2,
        scratch_shapes=[pltpu.SemaphoreType.DMA((2, count))],
        name="arrange",
    )(head, spot, *blocks, *lent)


def block_product(at_ref, x_ref, y_ref, w_ref, wy_ref):
    at = at_ref[0] // 2
    return dot(x_ref[...], w_ref[at], 1, 1) + dot(y_ref[...], wy_ref[at], 1, 1)


def part_kernel(at_ref, x_ref, y_ref, w_ref, wy_ref, *refs):
    total = block_product(at_ref, x_ref, y_ref, w_ref, wy_ref)
    for got in refs[:-1]:
        total = total + got[...].astype(F32)
    refs[-1][...] = total.astype(BF16)


def head_part(at, x, y, w, wy, got=()):
    return call(
        part_kernel,
        in_specs=[SMEM] + [VMEM] * (4 + len(got)),
        out_specs=VMEM,
        out_shape=jax.ShapeDtypeStruct((x.shape[0], w.shape[1]), BF16),
        name="head_part",
    )(at, x, y, w, wy, *got)


def join_kernel(per, par_ref, at_ref, x_ref, y_ref, w_ref, wy_ref, *refs):
    total = block_product(at_ref, x_ref, y_ref, w_ref, wy_ref)
    for got in refs[:-2]:
        total = total + got[...].astype(F32)
    other_ref, out_ref = refs[-2:]
    rows = other_ref.shape[1] // per
    both = (total.astype(BF16), other_ref[...])
    for k in range(2):

        @pl.when(par_ref[0] == k)
        def _():
            for i in range(per):
                at = slice(i * rows, (i + 1) * rows)
                for j in range(2):
                    to = (2 * i + j) * rows
                    out_ref[:, to : to + rows] = both[j ^ k][:, at]


def join(par, at, per, x, y, w, wy, got, other):
    return call(
        functools.partial(join_kernel, per),
        in_specs=[SMEM] * 2 + [VMEM] * (5 + len(got)),
        out_specs=VMEM,
        out_shape=jax.ShapeDtypeStruct((x.shape[0], 2 * other.shape[1]), BF16),
        name="join",
    )(par, at, x, y, w, wy, *got, other)


def after(x, *earlier):
    return lax.optimization_barrier((x, *earlier))[0]


def local(queries, keys, values, out_grad, inputs, value_weight):
    length, cols = queries.shape
    n_ctx, n_head = lax.axis_size("ctx"), lax.axis_size("head")
    pairs = n_ctx // 2
    ctx, head = lax.axis_index("ctx"), lax.axis_index("head")
    parity, pair = ctx % 2, ctx // 2
    par = parity.astype(jnp.int32).reshape(1)
    factor = 1.0 / math.sqrt(DH * length * n_ctx)
    lines = [[2 * i + k for i in range(pairs)] for k in range(2)]
    def partner(x):
        return lax.ppermute(x, "ctx", [(i, i ^ 1) for i in range(n_ctx)])

    def across(x, bit):
        return lax.ppermute(x, "head", [(i, i ^ bit) for i in range(n_head)])

    order = list(range(0, pairs, 2)) + list(range(1, pairs, 2))[::-1]
    place = [order.index(i) for i in range(pairs)]
    moves = [
        (2 * order[i] + k, 2 * order[(i + 1) % pairs] + k)
        for i in range(pairs)
        for k in range(2)
    ]
    here = head.astype(jnp.int32).reshape(1)
    spot = line_at(place, pair.astype(jnp.int32)).reshape(1)

    def ring(x):
        return lax.ppermute(x, "ctx", moves)

    def back(x):
        return lax.ppermute(x, "ctx", [(b, a) for a, b in moves])

    keep, send = states(par, queries, keys, values, out_grad)
    near = partner(send)
    line = pair.astype(jnp.int32).reshape(1)

    per = n_ctx // n_head // 2
    width = value_weight.shape[0]
    own, theirs = split(after(par, send), inputs, per)
    blocks = [value_weight, ring(after(value_weight, send))]
    own, theirs = [own], [partner(after(theirs, near))]

    offered = offer(line, keep, near, pairs)
    every = lax.all_to_all(
        offered, "ctx", split_axis=0, concat_axis=0, axis_index_groups=lines
    )
    far, send_far = far_states(line, every)
    ends = (far, partner(send_far), near)
    vi, keys_too = inside(after(queries, send_far), keys, out_grad)
    theirs = [after(theirs[0], send_far)]
    mine = finish_value(factor, par, keys_too, vi, ends)
    other = partner(mine)
    query_grad, key_grad = others(
        factor, par, queries, keys, after(values, mine), out_grad, ends
    )
    token = send_far
    for _ in range(2, pairs // 2 + 1):
        blocks.append(ring(after(blocks[-1], token)))
        token = mine
    ahead = [value_weight]
    for _ in range(pairs // 2 + 1, pairs):
        ahead.append(back(after(ahead[-1], mine)))
    blocks = blocks + ahead[:0:-1]
    early = pairs // 2
    lent = [across(after(x, mine), 1) for x in blocks[:early]]
    mine_too = across(mine, 1)

    offsets = [0]
    bit = n_head // 2
    while bit:
        own = own + [across(after(r, mine) if len(own) > 1 else r, bit) for r in own]
        theirs = theirs + [across(r, bit) for r in theirs]
        offsets = offsets + [o ^ bit for o in offsets]
        bit //= 2
    own = [own[offsets.index(i)] for i in range(n_head)]
    theirs = [theirs[offsets.index(i)] for i in range(n_head)]


    chains = 2

    def piece(dtype, step, token, flops=1):
        vals = (spot, here, after(mine, token), other, own, theirs)
        return pieces(dtype, chains, flops, order, per, step, *vals)

    total = piece(BF16, 0, query_grad, 4 * length * cols * width)
    moved = [ring(x) for x in total]
    other_too = across(other, 1)
    lent = lent + [across(after(x, total[0]), 1) for x in blocks[early:]]
    local_part = piece(F32, 1, total[0])


    def summed_parts(x, y):
        sent = [
            head_part(here ^ off, x, y, weight, borrowed)
            for off in range(2, n_head, 2)
        ]
        return sent[-1], [across(x, 2 * i + 2) for i, x in enumerate(sent)]

    held = [after(blocks[0], local_part[0])] + blocks[1:]
    weight, borrowed = arrange(order, per, n_head, here, spot, held, lent)
    token, got_other = summed_parts(other, other_too)
    token, got_mine = summed_parts(after(mine, token), mine_too)
    part = None
    for step in range(1, pairs - 1):
        if step == pairs - 2:
            last = piece(F32, pairs - 1, token)
            token = last[0]
        for i in range(chains):
            if step == pairs - 2 and i == chains - 1:
                lead = (here, after(other, token), other_too, weight, borrowed)
                token = part = head_part(*lead, got_other)
            token = add_own(moved[i], after(local_part[i], token))
            moved[i] = ring(token)
        if step < pairs - 2:
            local_part = piece(F32, step + 1, token)
            token = local_part[0]
    swapped = partner(part)
    weight_grad = finish_weight(1.0 / math.sqrt(length * n_ctx), moved, last)
    mine = after(mine, weight_grad)
    input_grad = join(
        par, here, per, mine, mine_too, weight, borrowed, got_mine, swapped
    )
    return (query_grad, key_grad, input_grad, weight_grad)


def solution(mesh):
    spec = P("ctx", "head")
    return jax.shard_map(
        local, mesh=mesh, in_specs=(spec,) * 6, out_specs=(spec,) * 4, check_vma=False
    )
```

```python
import functools
import math

import jax
import jax.numpy as jnp
from jax import lax
from jax.experimental import pallas as pl
from jax.experimental.pallas import tpu as pltpu
from jax.sharding import PartitionSpec as P

DH = 128
F32, BF16 = jnp.float32, jnp.bfloat16
VMEM = pl.BlockSpec(memory_space=pltpu.VMEM)
SMEM = pl.BlockSpec(memory_space=pltpu.SMEM)
ANY = pl.BlockSpec(memory_space=pl.ANY)


def dot(a, b, ca, cb):
    return lax.dot_general(a, b, (((ca,), (cb,)), ((), ())), preferred_element_type=F32)


def call(kernel, vmem=16, flops=1, **kw):
    hint = pl.CostEstimate(flops=flops, bytes_accessed=1, transcendentals=0)
    params = pltpu.CompilerParams(vmem_limit_bytes=vmem * 2**20)
    return pl.pallas_call(kernel, cost_estimate=hint, compiler_params=params, **kw)


def states_kernel(par_ref, *refs):
    arrays, (keep_ref, send_ref), bufs, sems = refs[:4], refs[4:6], refs[6:10], refs[10]
    heads = arrays[0].shape[1] // DH
    half = heads // 2

    def copy(j, hd):
        at = pl.ds(hd * DH, DH)
        return pltpu.make_async_copy(
            arrays[j].at[:, at], bufs[j].at[:, at], sems.at[j, hd]
        )

    for hd in range(heads):
        for j in range(4):
            copy(j, hd).start()
    for hd in range(heads):
        at = slice(hd * DH, (hd + 1) * DH)
        for j in range(4):
            copy(j, hd).wait()
        for kind, (a, b) in enumerate(((0, 3), (1, 2))):
            s = dot(bufs[a][:, at], bufs[b][:, at], 0, 0)
            own = par_ref[0] == hd // half

            @pl.when(own)
            def _():
                keep_ref[kind, hd % half] = s

            @pl.when(own & (par_ref[0] != kind))
            def _():
                send_ref[2, hd % half] = s.astype(BF16)

            @pl.when(jnp.logical_not(own))
            def _():
                send_ref[kind, hd % half] = s.astype(BF16)


def states(par, *arrays):
    n, cols = arrays[0].shape
    heads = cols // DH
    shape = (2, heads // 2, DH, DH)
    return call(
        states_kernel,
        vmem=60,
        in_specs=[SMEM] + [pl.BlockSpec(memory_space=pltpu.HBM)] * 4,
        out_specs=[VMEM] * 2,
        out_shape=[
            jax.ShapeDtypeStruct(shape, F32),
            jax.ShapeDtypeStruct((3, *shape[1:]), BF16),
        ],
        scratch_shapes=[pltpu.VMEM((n, cols), BF16)] * 4
        + [pltpu.SemaphoreType.DMA((4, heads))],
        name="states",
    )(par, *arrays)


def split_kernel(per, par_ref, x_ref, own_ref, theirs_ref, sems):
    width = own_ref.shape[2]
    for k in range(2):

        @pl.when(par_ref[0] == k)
        def _():
            copies = []
            for i in range(per):
                for j, out_ref in enumerate((own_ref, theirs_ref)):
                    at = (2 * i + (k ^ j)) * width
                    if width % 128:
                        out_ref[i] = x_ref[:, at : at + width]
                    else:
                        src = x_ref.at[:, pl.ds(at, width)]
                        copies.append(
                            pltpu.make_async_copy(src, out_ref.at[i], sems.at[j, i])
                        )
            for c in copies:
                c.start()
            for c in copies:
                c.wait()


def split(par, x, per):
    width = x.shape[1] // (2 * per)
    out = jax.ShapeDtypeStruct((per, x.shape[0], width), x.dtype)
    place = VMEM if width % 128 else pl.BlockSpec(memory_space=pltpu.HBM)
    return call(
        functools.partial(split_kernel, per),
        in_specs=[SMEM, place],
        out_specs=[VMEM] * 2,
        out_shape=[out, out],
        scratch_shapes=[pltpu.SemaphoreType.DMA((2, per))],
        name="split",
    )(par, x)


def inside_kernel(*refs):
    arrays, (out_ref, k_ref), bufs, sems = refs[:3], refs[3:5], refs[5:8], refs[8]
    n, cols = out_ref.shape
    heads = cols // DH

    def copy(j, hd):
        at = pl.ds(hd * DH, DH)
        return pltpu.make_async_copy(
            arrays[j].at[:, at], bufs[j].at[:, at], sems.at[j, hd]
        )

    for hd in range(heads):
        for j in range(3):
            copy(j, hd).start()
    rows = lax.broadcasted_iota(jnp.int32, (n, n), 0)
    causal = rows >= lax.broadcasted_iota(jnp.int32, (n, n), 1)
    for hd in range(heads):
        at = slice(hd * DH, (hd + 1) * DH)
        for j in range(3):
            copy(j, hd).wait()
        q, k, g = (x[:, at] for x in bufs)
        scores = jnp.where(causal, dot(q, k, 1, 1), 0.0).astype(BF16)
        out_ref[:, at] = dot(scores, g, 0, 0)
        k_ref[:, at] = k


def inside(*arrays):
    n, cols = arrays[0].shape
    return call(
        inside_kernel,
        in_specs=[pl.BlockSpec(memory_space=pltpu.HBM)] * 3,
        out_specs=[VMEM] * 2,
        out_shape=[jax.ShapeDtypeStruct((n, cols), d) for d in (F32, BF16)],
        scratch_shapes=[pltpu.VMEM((n, cols), BF16)] * 3
        + [pltpu.SemaphoreType.DMA((3, cols // DH))],
        name="inside",
    )(*arrays)


def offer_kernel(pair_ref, keep_ref, got_ref, out_ref):
    sums = [(keep_ref[k] + got_ref[k].astype(F32)).astype(BF16) for k in range(2)]
    for p in range(out_ref.shape[0]):
        out_ref[p] = jnp.where(p < pair_ref[0], sums[0], sums[1])


def offer(pair, keep, got, pairs):
    return call(
        offer_kernel,
        in_specs=[SMEM, VMEM, VMEM],
        out_specs=VMEM,
        out_shape=jax.ShapeDtypeStruct((pairs, *keep.shape[1:]), BF16),
        name="offer",
    )(pair, keep, got)


def far_kernel(pair_ref, every_ref, out_ref, send_ref):
    for kind in range(2):
        total = jnp.zeros(out_ref.shape[1:], F32)
        for p in range(every_ref.shape[0]):
            reached = p > pair_ref[0] if kind == 0 else p < pair_ref[0]
            total = total + jnp.where(reached, every_ref[p].astype(F32), 0.0)
        out_ref[kind] = total
        send_ref[kind] = total.astype(BF16)


def far_states(pair, every):
    shape = (2, *every.shape[1:])
    return call(
        far_kernel,
        in_specs=[SMEM, VMEM],
        out_specs=[VMEM] * 2,
        out_shape=[jax.ShapeDtypeStruct(shape, d) for d in (F32, BF16)],
        name="far",
    )(pair, every)


def entering(par, kind, hd, half, far, got, near):
    mine = par == hd // half
    i = hd % half
    outer = jnp.where(mine, far[kind, i], got[kind, i].astype(F32))
    close = jnp.where(mine, near[kind, i], near[2, i]).astype(F32)
    total = outer + jnp.where(par == kind, close, 0.0)
    hi = total.astype(BF16)
    return hi, (total - hi.astype(F32)).astype(BF16)


def value_kernel(factor, half, par_ref, k_ref, vi_ref, *refs):
    ends, out_ref = refs[:-1], refs[-1]
    for hd in range(2 * half):
        at = slice(hd * DH, (hd + 1) * DH)
        hi, lo = entering(par_ref[0], 0, hd, half, *ends)
        k = k_ref[:, at]
        total = vi_ref[:, at] + (dot(k, hi, 1, 0) + dot(k, lo, 1, 0))
        out_ref[:, at] = (factor * total).astype(BF16)


def finish_value(factor, par, k, vi, ends):
    return call(
        functools.partial(value_kernel, factor, k.shape[1] // DH // 2),
        in_specs=[SMEM] + [VMEM] * (2 + len(ends)),
        out_specs=VMEM,
        out_shape=jax.ShapeDtypeStruct(k.shape, BF16),
        name="finish_value",
    )(par, k, vi, *ends)


def others_kernel(factor, half, par_ref, q_ref, k_ref, v_ref, g_ref, *refs):
    ends, (qo_ref, ko_ref) = refs[:-2], refs[-2:]
    hd = pl.program_id(0)
    q, k, v, g = q_ref[...], k_ref[...], v_ref[...], g_ref[...]
    n = q.shape[0]
    rows = lax.broadcasted_iota(jnp.int32, (n, n), 0)
    cols = lax.broadcasted_iota(jnp.int32, (n, n), 1)
    scores = jnp.where(rows >= cols, dot(g, v, 1, 1), 0.0).astype(BF16)
    hi, lo = entering(par_ref[0], 1, hd, half, *ends)
    total = dot(scores, k, 1, 0) + (dot(g, hi, 1, 1) + dot(g, lo, 1, 1))
    qo_ref[...] = (factor * total).astype(BF16)
    hi, lo = entering(par_ref[0], 0, hd, half, *ends)
    total = dot(scores, q, 0, 0) + (dot(v, hi, 1, 1) + dot(v, lo, 1, 1))
    ko_ref[...] = (factor * total).astype(BF16)


def others(factor, par, q, k, v, g, ends):
    n, cols = q.shape
    spec = pl.BlockSpec((n, DH), lambda h: (0, h))
    held = [pl.BlockSpec(x.shape, lambda h, d=x.ndim: (0,) * d) for x in ends]
    out = jax.ShapeDtypeStruct(q.shape, BF16)
    return call(
        functools.partial(others_kernel, factor, cols // DH // 2),
        grid=(cols // DH,),
        in_specs=[SMEM] + [spec] * 4 + held,
        out_specs=[spec] * 2,
        out_shape=[out] * 2,
        name="others",
    )(par, q, k, v, g, *ends)


def line_at(order, place):
    place = lax.rem(place + 2 * len(order), len(order))
    line = jnp.int32(order[0])
    for i, p in enumerate(order[1:], 1):
        line = jnp.where(place == i, p, line)
    return line


def piece_kernel(order, per, step, count, spot_ref, head_ref, a_ref, b_ref, *refs):
    own, theirs = refs[:count], refs[count : 2 * count]
    outs, (x, y, at, bt, sems) = refs[2 * count : -5], refs[-5:]
    line = line_at(order, spot_ref[0] - 1 - step)
    off, sub = lax.div(line, per) ^ head_ref[0], lax.rem(line, per)

    for i in range(count):

        @pl.when(off == i)
        def _():
            for j, (src, dst) in enumerate(((own, x), (theirs, y))):
                pltpu.make_async_copy(src[i].at[sub], dst, sems.at[j]).start()

    at[...] = a_ref[...].T
    bt[...] = b_ref[...].T
    for j, (src, dst) in enumerate(((own, x), (theirs, y))):
        pltpu.make_async_copy(src[0].at[0], dst, sems.at[j]).wait()
    total = dot(at[...], x[...], 1, 0) + dot(bt[...], y[...], 1, 0)
    span = outs[0].shape[0]
    for i, out_ref in enumerate(outs):
        out_ref[...] = total[i * span : (i + 1) * span].astype(out_ref.dtype)


def pieces(dtype, chains, flops, order, per, step, spot, head, a, b, own, theirs):
    count = len(own)
    _, n, width = own[0].shape
    cols = a.shape[1]
    return call(
        functools.partial(piece_kernel, order, per, step, count),
        flops=flops,
        in_specs=[SMEM] * 2 + [VMEM] * 2 + [ANY] * (2 * count),
        out_specs=[VMEM] * chains,
        out_shape=[jax.ShapeDtypeStruct((cols // chains, width), dtype)] * chains,
        scratch_shapes=[pltpu.VMEM((n, width), BF16)] * 2
        + [pltpu.VMEM((cols, n), BF16)] * 2
        + [pltpu.SemaphoreType.DMA((2,))],
        name="pieces",
    )(spot, head, a, b, *own, *theirs)


def weight_kernel(scale, *refs):
    count, out_ref = len(refs) // 2, refs[-1]
    span = refs[0].shape[0]
    for i in range(count):
        total = refs[i][...].astype(F32) + refs[count + i][...]
        out_ref[:, i * span : (i + 1) * span] = total.T * scale


def finish_weight(scale, moved, own):
    span, width = moved[0].shape
    count = len(moved)
    return call(
        functools.partial(weight_kernel, scale),
        in_specs=[VMEM] * (2 * count),
        out_specs=VMEM,
        out_shape=jax.ShapeDtypeStruct((width, span * count), F32),
        name="finish_weight",
    )(*moved, *own)


def add_kernel(moved_ref, own_ref, out_ref):
    out_ref[...] = (moved_ref[...].astype(F32) + own_ref[...]).astype(BF16)


def add_own(moved, own):
    return call(
        add_kernel,
        in_specs=[VMEM] * 2,
        out_specs=VMEM,
        out_shape=jax.ShapeDtypeStruct(moved.shape, BF16),
        name="add_own",
    )(moved, own)


def arrange_kernel(order, per, head_ref, spot_ref, *refs):
    count = len(order)
    outs, sems = refs[-3:-1], refs[-1]
    rows = refs[0].shape[0]

    def copies(s):
        p = line_at(order, spot_ref[0] - s)
        head, sub = lax.div(p, per), lax.rem(p, per)
        at = (lax.div(head, 2), pl.ds(sub * rows, rows))
        pair = [
            pltpu.make_async_copy(refs[j * count + s], outs[j].at[at], sems.at[j, s])
            for j in range(2)
        ]
        return pair, lax.rem(head, 2) == lax.rem(head_ref[0], 2)

    for act in ("start", "wait"):
        for s in range(count):
            pair, needed = copies(s)

            @pl.when(needed)
            def _():
                for c in pair:
                    getattr(c, act)()


def arrange(order, per, n_head, head, spot, blocks, lent):
    rows, cols = blocks[0].shape
    count = len(blocks)
    out = jax.ShapeDtypeStruct((n_head // 2, per * rows, cols), BF16)
    return call(
        functools.partial(arrange_kernel, order, per),
        in_specs=[SMEM] * 2 + [ANY] * (2 * count),
        out_specs=[VMEM] * 2,
        out_shape=[out] * 2,
        scratch_shapes=[pltpu.SemaphoreType.DMA((2, count))],
        name="arrange",
    )(head, spot, *blocks, *lent)


def block_product(at_ref, x_ref, y_ref, w_ref, wy_ref):
    at = at_ref[0] // 2
    return dot(x_ref[...], w_ref[at], 1, 1) + dot(y_ref[...], wy_ref[at], 1, 1)


def part_kernel(at_ref, x_ref, y_ref, w_ref, wy_ref, *refs):
    total = block_product(at_ref, x_ref, y_ref, w_ref, wy_ref)
    for got in refs[:-1]:
        total = total + got[...].astype(F32)
    refs[-1][...] = total.astype(BF16)


def head_part(at, x, y, w, wy, got=()):
    return call(
        part_kernel,
        in_specs=[SMEM] + [VMEM] * (4 + len(got)),
        out_specs=VMEM,
        out_shape=jax.ShapeDtypeStruct((x.shape[0], w.shape[1]), BF16),
        name="head_part",
    )(at, x, y, w, wy, *got)


def join_kernel(per, par_ref, at_ref, x_ref, y_ref, w_ref, wy_ref, *refs):
    total = block_product(at_ref, x_ref, y_ref, w_ref, wy_ref)
    for got in refs[:-2]:
        total = total + got[...].astype(F32)
    other_ref, out_ref = refs[-2:]
    rows = other_ref.shape[1] // per
    both = (total.astype(BF16), other_ref[...])
    for k in range(2):

        @pl.when(par_ref[0] == k)
        def _():
            for i in range(per):
                at = slice(i * rows, (i + 1) * rows)
                for j in range(2):
                    to = (2 * i + j) * rows
                    out_ref[:, to : to + rows] = both[j ^ k][:, at]


def join(par, at, per, x, y, w, wy, got, other):
    return call(
        functools.partial(join_kernel, per),
        in_specs=[SMEM] * 2 + [VMEM] * (5 + len(got)),
        out_specs=VMEM,
        out_shape=jax.ShapeDtypeStruct((x.shape[0], 2 * other.shape[1]), BF16),
        name="join",
    )(par, at, x, y, w, wy, *got, other)


def after(x, *earlier):
    return lax.optimization_barrier((x, *earlier))[0]


def local(queries, keys, values, out_grad, inputs, value_weight):
    length, cols = queries.shape
    n_ctx, n_head = lax.axis_size("ctx"), lax.axis_size("head")
    pairs = n_ctx // 2
    ctx, head = lax.axis_index("ctx"), lax.axis_index("head")
    parity, pair = ctx % 2, ctx // 2
    par = parity.astype(jnp.int32).reshape(1)
    factor = 1.0 / math.sqrt(DH * length * n_ctx)
    lines = [[2 * i + k for i in range(pairs)] for k in range(2)]
    def partner(x):
        return lax.ppermute(x, "ctx", [(i, i ^ 1) for i in range(n_ctx)])

    def across(x, bit):
        return lax.ppermute(x, "head", [(i, i ^ bit) for i in range(n_head)])

    order = list(range(0, pairs, 2)) + list(range(1, pairs, 2))[::-1]
    place = [order.index(i) for i in range(pairs)]
    moves = [
        (2 * order[i] + k, 2 * order[(i + 1) % pairs] + k)
        for i in range(pairs)
        for k in range(2)
    ]
    here = head.astype(jnp.int32).reshape(1)
    spot = line_at(place, pair.astype(jnp.int32)).reshape(1)

    def ring(x):
        return lax.ppermute(x, "ctx", moves)

    def back(x):
        return lax.ppermute(x, "ctx", [(b, a) for a, b in moves])

    keep, send = states(par, queries, keys, values, out_grad)
    near = partner(send)
    line = pair.astype(jnp.int32).reshape(1)

    per = n_ctx // n_head // 2
    width = value_weight.shape[0]
    own, theirs = split(after(par, send), inputs, per)
    blocks = [value_weight, ring(after(value_weight, send))]
    own, theirs = [own], [partner(after(theirs, near))]

    offered = offer(line, keep, near, pairs)
    every = lax.all_to_all(
        offered, "ctx", split_axis=0, concat_axis=0, axis_index_groups=lines
    )
    far, send_far = far_states(line, after(every, blocks[1]))
    ends = (far, partner(send_far), near)
    vi, keys_too = inside(after(queries, send_far), keys, out_grad)
    theirs = [after(theirs[0], send_far)]
    mine = finish_value(factor, par, keys_too, vi, ends)
    other = partner(mine)
    query_grad, key_grad = others(
        factor, par, queries, keys, after(values, mine), out_grad, ends
    )
    token = send_far
    for _ in range(2, pairs // 2 + 1):
        blocks.append(ring(after(blocks[-1], token)))
        token = mine
    ahead = [value_weight]
    for _ in range(pairs // 2 + 1, pairs):
        ahead.append(back(after(ahead[-1], mine)))
    blocks = blocks + ahead[:0:-1]
    early = pairs // 2
    lent = [across(after(x, mine), 1) for x in blocks[:early]]
    mine_too = across(mine, 1)

    offsets = [0]
    bit = n_head // 2
    while bit:
        own = own + [across(after(r, mine) if len(own) > 1 else r, bit) for r in own]
        last = len(theirs) > 1
        theirs = theirs + [
            across(after(r, blocks[2]) if last and i else r, bit)
            for i, r in enumerate(theirs)
        ]
        offsets = offsets + [o ^ bit for o in offsets]
        bit //= 2
    own = [own[offsets.index(i)] for i in range(n_head)]
    theirs = [theirs[offsets.index(i)] for i in range(n_head)]


    chains = 2

    def piece(dtype, step, token, flops=1):
        vals = (spot, here, after(mine, token), other, own, theirs)
        return pieces(dtype, chains, flops, order, per, step, *vals)

    token = after(query_grad, blocks[-1])
    total = piece(BF16, 0, token, 4 * length * cols * width)
    moved = [ring(x) for x in total]
    other_too = across(other, 1)
    lent = lent + [across(after(x, total[0]), 1) for x in blocks[early:]]
    local_part = piece(F32, 1, total[0])


    def summed_parts(x, y):
        sent = [
            head_part(here ^ off, x, y, weight, borrowed)
            for off in range(2, n_head, 2)
        ]
        return sent[-1], [across(x, 2 * i + 2) for i, x in enumerate(sent)]

    held = [after(blocks[0], local_part[0])] + blocks[1:]
    weight, borrowed = arrange(order, per, n_head, here, spot, held, lent)
    token, got_other = summed_parts(other, other_too)
    token, got_mine = summed_parts(after(mine, token), mine_too)
    part = None
    for step in range(1, pairs - 1):
        if step == pairs - 2:
            last = piece(F32, pairs - 1, token)
            token = last[0]
        for i in range(chains):
            if step == pairs - 2 and i == chains - 1:
                lead = (here, after(other, token), other_too, weight, borrowed)
                token = part = head_part(*lead, got_other)
            token = add_own(moved[i], after(local_part[i], token))
            moved[i] = ring(token)
        if step < pairs - 2:
            local_part = piece(F32, step + 1, token)
            token = local_part[0]
    swapped = partner(part)
    weight_grad = finish_weight(1.0 / math.sqrt(length * n_ctx), moved, last)
    mine = after(mine, weight_grad)
    input_grad = join(
        par, here, per, mine, mine_too, weight, borrowed, got_mine, swapped
    )
    return (query_grad, key_grad, input_grad, weight_grad)


def solution(mesh):
    spec = P("ctx", "head")
    return jax.shard_map(
        local, mesh=mesh, in_specs=(spec,) * 6, out_specs=(spec,) * 4, check_vma=False
    )
```

```python
import functools
import math

import jax
import jax.numpy as jnp
from jax import lax
from jax.experimental import pallas as pl
from jax.experimental.pallas import tpu as pltpu
from jax.sharding import PartitionSpec as P

DH = 128
F32, BF16 = jnp.float32, jnp.bfloat16
VMEM = pl.BlockSpec(memory_space=pltpu.VMEM)
SMEM = pl.BlockSpec(memory_space=pltpu.SMEM)
ANY = pl.BlockSpec(memory_space=pl.ANY)


def dot(a, b, ca, cb):
    return lax.dot_general(a, b, (((ca,), (cb,)), ((), ())), preferred_element_type=F32)


def call(kernel, vmem=16, flops=1, **kw):
    hint = pl.CostEstimate(flops=flops, bytes_accessed=1, transcendentals=0)
    params = pltpu.CompilerParams(vmem_limit_bytes=vmem * 2**20)
    return pl.pallas_call(kernel, cost_estimate=hint, compiler_params=params, **kw)


def states_kernel(par_ref, *refs):
    arrays, (keep_ref, send_ref), bufs, sems = refs[:4], refs[4:6], refs[6:10], refs[10]
    heads = arrays[0].shape[1] // DH
    half = heads // 2

    def copy(j, hd):
        at = pl.ds(hd * DH, DH)
        return pltpu.make_async_copy(
            arrays[j].at[:, at], bufs[j].at[:, at], sems.at[j, hd]
        )

    for hd in range(heads):
        for j in range(4):
            copy(j, hd).start()
    for hd in range(heads):
        at = slice(hd * DH, (hd + 1) * DH)
        for j in range(4):
            copy(j, hd).wait()
        for kind, (a, b) in enumerate(((0, 3), (1, 2))):
            s = dot(bufs[a][:, at], bufs[b][:, at], 0, 0)
            own = par_ref[0] == hd // half

            @pl.when(own)
            def _():
                keep_ref[kind, hd % half] = s

            @pl.when(own & (par_ref[0] != kind))
            def _():
                send_ref[2, hd % half] = s.astype(BF16)

            @pl.when(jnp.logical_not(own))
            def _():
                send_ref[kind, hd % half] = s.astype(BF16)


def states(par, *arrays):
    n, cols = arrays[0].shape
    heads = cols // DH
    shape = (2, heads // 2, DH, DH)
    return call(
        states_kernel,
        vmem=60,
        in_specs=[SMEM] + [pl.BlockSpec(memory_space=pltpu.HBM)] * 4,
        out_specs=[VMEM] * 2,
        out_shape=[
            jax.ShapeDtypeStruct(shape, F32),
            jax.ShapeDtypeStruct((3, *shape[1:]), BF16),
        ],
        scratch_shapes=[pltpu.VMEM((n, cols), BF16)] * 4
        + [pltpu.SemaphoreType.DMA((4, heads))],
        name="states",
    )(par, *arrays)


def split_kernel(per, par_ref, x_ref, own_ref, theirs_ref, sems):
    width = own_ref.shape[2]
    for k in range(2):

        @pl.when(par_ref[0] == k)
        def _():
            copies = []
            for i in range(per):
                for j, out_ref in enumerate((own_ref, theirs_ref)):
                    at = (2 * i + (k ^ j)) * width
                    if width % 128:
                        out_ref[i] = x_ref[:, at : at + width]
                    else:
                        src = x_ref.at[:, pl.ds(at, width)]
                        copies.append(
                            pltpu.make_async_copy(src, out_ref.at[i], sems.at[j, i])
                        )
            for c in copies:
                c.start()
            for c in copies:
                c.wait()


def split(par, x, per):
    width = x.shape[1] // (2 * per)
    out = jax.ShapeDtypeStruct((per, x.shape[0], width), x.dtype)
    place = VMEM if width % 128 else pl.BlockSpec(memory_space=pltpu.HBM)
    return call(
        functools.partial(split_kernel, per),
        in_specs=[SMEM, place],
        out_specs=[VMEM] * 2,
        out_shape=[out, out],
        scratch_shapes=[pltpu.SemaphoreType.DMA((2, per))],
        name="split",
    )(par, x)


def inside_kernel(*refs):
    arrays, (out_ref, k_ref), bufs, sems = refs[:3], refs[3:5], refs[5:8], refs[8]
    n, cols = out_ref.shape
    heads = cols // DH

    def copy(j, hd):
        at = pl.ds(hd * DH, DH)
        return pltpu.make_async_copy(
            arrays[j].at[:, at], bufs[j].at[:, at], sems.at[j, hd]
        )

    for hd in range(heads):
        for j in range(3):
            copy(j, hd).start()
    rows = lax.broadcasted_iota(jnp.int32, (n, n), 0)
    causal = rows >= lax.broadcasted_iota(jnp.int32, (n, n), 1)
    for hd in range(heads):
        at = slice(hd * DH, (hd + 1) * DH)
        for j in range(3):
            copy(j, hd).wait()
        q, k, g = (x[:, at] for x in bufs)
        scores = jnp.where(causal, dot(q, k, 1, 1), 0.0).astype(BF16)
        out_ref[:, at] = dot(scores, g, 0, 0)
        k_ref[:, at] = k


def inside(*arrays):
    n, cols = arrays[0].shape
    return call(
        inside_kernel,
        in_specs=[pl.BlockSpec(memory_space=pltpu.HBM)] * 3,
        out_specs=[VMEM] * 2,
        out_shape=[jax.ShapeDtypeStruct((n, cols), d) for d in (F32, BF16)],
        scratch_shapes=[pltpu.VMEM((n, cols), BF16)] * 3
        + [pltpu.SemaphoreType.DMA((3, cols // DH))],
        name="inside",
    )(*arrays)


def offer_kernel(pair_ref, keep_ref, got_ref, out_ref):
    sums = [(keep_ref[k] + got_ref[k].astype(F32)).astype(BF16) for k in range(2)]
    for p in range(out_ref.shape[0]):
        out_ref[p] = jnp.where(p < pair_ref[0], sums[0], sums[1])


def offer(pair, keep, got, pairs):
    return call(
        offer_kernel,
        in_specs=[SMEM, VMEM, VMEM],
        out_specs=VMEM,
        out_shape=jax.ShapeDtypeStruct((pairs, *keep.shape[1:]), BF16),
        name="offer",
    )(pair, keep, got)


def far_kernel(pair_ref, every_ref, out_ref, send_ref):
    for kind in range(2):
        total = jnp.zeros(out_ref.shape[1:], F32)
        for p in range(every_ref.shape[0]):
            reached = p > pair_ref[0] if kind == 0 else p < pair_ref[0]
            total = total + jnp.where(reached, every_ref[p].astype(F32), 0.0)
        out_ref[kind] = total
        send_ref[kind] = total.astype(BF16)


def far_states(pair, every):
    shape = (2, *every.shape[1:])
    return call(
        far_kernel,
        in_specs=[SMEM, VMEM],
        out_specs=[VMEM] * 2,
        out_shape=[jax.ShapeDtypeStruct(shape, d) for d in (F32, BF16)],
        name="far",
    )(pair, every)


def entering(par, kind, hd, half, far, got, near):
    mine = par == hd // half
    i = hd % half
    outer = jnp.where(mine, far[kind, i], got[kind, i].astype(F32))
    close = jnp.where(mine, near[kind, i], near[2, i]).astype(F32)
    total = outer + jnp.where(par == kind, close, 0.0)
    hi = total.astype(BF16)
    return hi, (total - hi.astype(F32)).astype(BF16)


def value_kernel(factor, half, par_ref, k_ref, vi_ref, *refs):
    ends, out_ref = refs[:-1], refs[-1]
    for hd in range(2 * half):
        at = slice(hd * DH, (hd + 1) * DH)
        hi, lo = entering(par_ref[0], 0, hd, half, *ends)
        k = k_ref[:, at]
        total = vi_ref[:, at] + (dot(k, hi, 1, 0) + dot(k, lo, 1, 0))
        out_ref[:, at] = (factor * total).astype(BF16)


def finish_value(factor, par, k, vi, ends):
    return call(
        functools.partial(value_kernel, factor, k.shape[1] // DH // 2),
        in_specs=[SMEM] + [VMEM] * (2 + len(ends)),
        out_specs=VMEM,
        out_shape=jax.ShapeDtypeStruct(k.shape, BF16),
        name="finish_value",
    )(par, k, vi, *ends)


def others_kernel(factor, half, par_ref, q_ref, k_ref, v_ref, g_ref, *refs):
    ends, (qo_ref, ko_ref) = refs[:-2], refs[-2:]
    hd = pl.program_id(0)
    q, k, v, g = q_ref[...], k_ref[...], v_ref[...], g_ref[...]
    n = q.shape[0]
    rows = lax.broadcasted_iota(jnp.int32, (n, n), 0)
    cols = lax.broadcasted_iota(jnp.int32, (n, n), 1)
    scores = jnp.where(rows >= cols, dot(g, v, 1, 1), 0.0).astype(BF16)
    hi, lo = entering(par_ref[0], 1, hd, half, *ends)
    total = dot(scores, k, 1, 0) + (dot(g, hi, 1, 1) + dot(g, lo, 1, 1))
    qo_ref[...] = (factor * total).astype(BF16)
    hi, lo = entering(par_ref[0], 0, hd, half, *ends)
    total = dot(scores, q, 0, 0) + (dot(v, hi, 1, 1) + dot(v, lo, 1, 1))
    ko_ref[...] = (factor * total).astype(BF16)


def others(factor, par, q, k, v, g, ends):
    n, cols = q.shape
    spec = pl.BlockSpec((n, DH), lambda h: (0, h))
    held = [pl.BlockSpec(x.shape, lambda h, d=x.ndim: (0,) * d) for x in ends]
    out = jax.ShapeDtypeStruct(q.shape, BF16)
    return call(
        functools.partial(others_kernel, factor, cols // DH // 2),
        grid=(cols // DH,),
        in_specs=[SMEM] + [spec] * 4 + held,
        out_specs=[spec] * 2,
        out_shape=[out] * 2,
        name="others",
    )(par, q, k, v, g, *ends)


def line_at(order, place):
    place = lax.rem(place + 2 * len(order), len(order))
    line = jnp.int32(order[0])
    for i, p in enumerate(order[1:], 1):
        line = jnp.where(place == i, p, line)
    return line


def piece_kernel(order, per, step, count, spot_ref, head_ref, a_ref, b_ref, *refs):
    own, theirs = refs[:count], refs[count : 2 * count]
    outs, (x, y, at, bt, sems) = refs[2 * count : -5], refs[-5:]
    line = line_at(order, spot_ref[0] - 1 - step)
    off, sub = lax.div(line, per) ^ head_ref[0], lax.rem(line, per)

    for i in range(count):

        @pl.when(off == i)
        def _():
            for j, (src, dst) in enumerate(((own, x), (theirs, y))):
                pltpu.make_async_copy(src[i].at[sub], dst, sems.at[j]).start()

    at[...] = a_ref[...].T
    bt[...] = b_ref[...].T
    for j, (src, dst) in enumerate(((own, x), (theirs, y))):
        pltpu.make_async_copy(src[0].at[0], dst, sems.at[j]).wait()
    total = dot(at[...], x[...], 1, 0) + dot(bt[...], y[...], 1, 0)
    span = outs[0].shape[0]
    for i, out_ref in enumerate(outs):
        out_ref[...] = total[i * span : (i + 1) * span].astype(out_ref.dtype)


def pieces(dtype, chains, flops, order, per, step, spot, head, a, b, own, theirs):
    count = len(own)
    _, n, width = own[0].shape
    cols = a.shape[1]
    return call(
        functools.partial(piece_kernel, order, per, step, count),
        flops=flops,
        in_specs=[SMEM] * 2 + [VMEM] * 2 + [ANY] * (2 * count),
        out_specs=[VMEM] * chains,
        out_shape=[jax.ShapeDtypeStruct((cols // chains, width), dtype)] * chains,
        scratch_shapes=[pltpu.VMEM((n, width), BF16)] * 2
        + [pltpu.VMEM((cols, n), BF16)] * 2
        + [pltpu.SemaphoreType.DMA((2,))],
        name="pieces",
    )(spot, head, a, b, *own, *theirs)


def weight_kernel(scale, *refs):
    count, out_ref = len(refs) // 2, refs[-1]
    span = refs[0].shape[0]
    for i in range(count):
        total = refs[i][...].astype(F32) + refs[count + i][...]
        out_ref[:, i * span : (i + 1) * span] = total.T * scale


def finish_weight(scale, moved, own):
    span, width = moved[0].shape
    count = len(moved)
    return call(
        functools.partial(weight_kernel, scale),
        in_specs=[VMEM] * (2 * count),
        out_specs=VMEM,
        out_shape=jax.ShapeDtypeStruct((width, span * count), F32),
        name="finish_weight",
    )(*moved, *own)


def add_kernel(moved_ref, own_ref, out_ref):
    out_ref[...] = (moved_ref[...].astype(F32) + own_ref[...]).astype(BF16)


def add_own(moved, own):
    return call(
        add_kernel,
        in_specs=[VMEM] * 2,
        out_specs=VMEM,
        out_shape=jax.ShapeDtypeStruct(moved.shape, BF16),
        name="add_own",
    )(moved, own)


def arrange_kernel(order, per, head_ref, spot_ref, *refs):
    count = len(order)
    outs, sems = refs[-3:-1], refs[-1]
    rows = refs[0].shape[0]

    def copies(s):
        p = line_at(order, spot_ref[0] - s)
        head, sub = lax.div(p, per), lax.rem(p, per)
        at = (lax.div(head, 2), pl.ds(sub * rows, rows))
        pair = [
            pltpu.make_async_copy(refs[j * count + s], outs[j].at[at], sems.at[j, s])
            for j in range(2)
        ]
        return pair, lax.rem(head, 2) == lax.rem(head_ref[0], 2)

    for act in ("start", "wait"):
        for s in range(count):
            pair, needed = copies(s)

            @pl.when(needed)
            def _():
                for c in pair:
                    getattr(c, act)()


def arrange(order, per, n_head, head, spot, blocks, lent):
    rows, cols = blocks[0].shape
    count = len(blocks)
    out = jax.ShapeDtypeStruct((n_head // 2, per * rows, cols), BF16)
    return call(
        functools.partial(arrange_kernel, order, per),
        in_specs=[SMEM] * 2 + [ANY] * (2 * count),
        out_specs=[VMEM] * 2,
        out_shape=[out] * 2,
        scratch_shapes=[pltpu.SemaphoreType.DMA((2, count))],
        name="arrange",
    )(head, spot, *blocks, *lent)


def block_product(at_ref, x_ref, y_ref, w_ref, wy_ref):
    at = at_ref[0] // 2
    return dot(x_ref[...], w_ref[at], 1, 1) + dot(y_ref[...], wy_ref[at], 1, 1)


def part_kernel(at_ref, x_ref, y_ref, w_ref, wy_ref, *refs):
    total = block_product(at_ref, x_ref, y_ref, w_ref, wy_ref)
    for got in refs[:-1]:
        total = total + got[...].astype(F32)
    refs[-1][...] = total.astype(BF16)


def head_part(at, x, y, w, wy, got=()):
    return call(
        part_kernel,
        in_specs=[SMEM] + [VMEM] * (4 + len(got)),
        out_specs=VMEM,
        out_shape=jax.ShapeDtypeStruct((x.shape[0], w.shape[1]), BF16),
        name="head_part",
    )(at, x, y, w, wy, *got)


def join_kernel(per, par_ref, at_ref, x_ref, y_ref, w_ref, wy_ref, *refs):
    total = block_product(at_ref, x_ref, y_ref, w_ref, wy_ref)
    for got in refs[:-2]:
        total = total + got[...].astype(F32)
    other_ref, out_ref = refs[-2:]
    rows = other_ref.shape[1] // per
    both = (total.astype(BF16), other_ref[...])
    for k in range(2):

        @pl.when(par_ref[0] == k)
        def _():
            for i in range(per):
                at = slice(i * rows, (i + 1) * rows)
                for j in range(2):
                    to = (2 * i + j) * rows
                    out_ref[:, to : to + rows] = both[j ^ k][:, at]


def join(par, at, per, x, y, w, wy, got, other):
    return call(
        functools.partial(join_kernel, per),
        in_specs=[SMEM] * 2 + [VMEM] * (5 + len(got)),
        out_specs=VMEM,
        out_shape=jax.ShapeDtypeStruct((x.shape[0], 2 * other.shape[1]), BF16),
        name="join",
    )(par, at, x, y, w, wy, *got, other)


def after(x, *earlier):
    return lax.optimization_barrier((x, *earlier))[0]


def local(queries, keys, values, out_grad, inputs, value_weight):
    length, cols = queries.shape
    n_ctx, n_head = lax.axis_size("ctx"), lax.axis_size("head")
    pairs = n_ctx // 2
    ctx, head = lax.axis_index("ctx"), lax.axis_index("head")
    parity, pair = ctx % 2, ctx // 2
    par = parity.astype(jnp.int32).reshape(1)
    factor = 1.0 / math.sqrt(DH * length * n_ctx)
    lines = [[2 * i + k for i in range(pairs)] for k in range(2)]
    def partner(x):
        return lax.ppermute(x, "ctx", [(i, i ^ 1) for i in range(n_ctx)])

    def across(x, bit):
        return lax.ppermute(x, "head", [(i, i ^ bit) for i in range(n_head)])

    order = list(range(0, pairs, 2)) + list(range(1, pairs, 2))[::-1]
    place = [order.index(i) for i in range(pairs)]
    moves = [
        (2 * order[i] + k, 2 * order[(i + 1) % pairs] + k)
        for i in range(pairs)
        for k in range(2)
    ]
    here = head.astype(jnp.int32).reshape(1)
    spot = line_at(place, pair.astype(jnp.int32)).reshape(1)

    def ring(x):
        return lax.ppermute(x, "ctx", moves)

    def back(x):
        return lax.ppermute(x, "ctx", [(b, a) for a, b in moves])

    keep, send = states(par, queries, keys, values, out_grad)
    near = partner(send)
    line = pair.astype(jnp.int32).reshape(1)

    per = n_ctx // n_head // 2
    width = value_weight.shape[0]
    own, theirs = split(after(par, send), inputs, per)
    blocks = [value_weight, ring(after(value_weight, send))]
    own, theirs = [own], [partner(after(theirs, near))]

    offered = offer(line, keep, near, pairs)
    every = lax.all_to_all(
        offered, "ctx", split_axis=0, concat_axis=0, axis_index_groups=lines
    )
    far, send_far = far_states(line, after(every, blocks[1]))
    ends = (far, partner(send_far), near)
    vi, keys_too = inside(after(queries, send_far), keys, out_grad)
    theirs = [after(theirs[0], send_far)]
    mine = finish_value(factor, par, keys_too, vi, ends)
    other = partner(mine)
    query_grad, key_grad = others(
        factor, par, queries, keys, after(values, mine), out_grad, ends
    )
    token = send_far
    for _ in range(2, pairs // 2 + 1):
        blocks.append(ring(after(blocks[-1], token)))
        token = mine
    ahead = [value_weight]
    for _ in range(pairs // 2 + 1, pairs):
        ahead.append(back(after(ahead[-1], mine)))
    blocks = blocks + ahead[:0:-1]
    early = pairs // 2
    lent = [across(after(x, mine), 1) for x in blocks[:early]]
    mine_too = across(mine, 1)

    offsets = [0]
    bit = n_head // 2
    while bit:
        own = own + [across(after(r, mine) if len(own) > 1 else r, bit) for r in own]
        last = len(theirs) > 1
        theirs = theirs + [
            across(after(r, blocks[2]) if last and i else r, bit)
            for i, r in enumerate(theirs)
        ]
        offsets = offsets + [o ^ bit for o in offsets]
        bit //= 2
    own = [own[offsets.index(i)] for i in range(n_head)]
    theirs = [theirs[offsets.index(i)] for i in range(n_head)]


    chains = 2

    def piece(dtype, step, token, flops=1):
        vals = (spot, here, after(mine, token), other, own, theirs)
        return pieces(dtype, chains, flops, order, per, step, *vals)

    token = after(query_grad, blocks[-1])
    total = piece(BF16, 0, token, 4 * length * cols * width)
    moved = [ring(x) for x in total]
    other_too = across(other, 1)
    lent = lent + [across(after(x, total[0]), 1) for x in blocks[early:]]
    local_part = piece(F32, 1, total[0])


    def summed_parts(x, y):
        sent = [
            head_part(here ^ off, x, y, weight, borrowed)
            for off in range(2, n_head, 2)
        ]
        return sent[-1], [across(x, 2 * i + 2) for i, x in enumerate(sent)]

    held = [after(blocks[0], local_part[0])] + blocks[1:]
    weight, borrowed = arrange(order, per, n_head, here, spot, held, lent)
    token, got_other = summed_parts(other, other_too)
    token, got_mine = summed_parts(after(mine, token), mine_too)
    part = None
    for step in range(1, pairs - 1):
        if step == pairs - 2:
            last = piece(F32, pairs - 1, token)
            token = last[0]
        for i in range(chains):
            if step == pairs - 2 and i == chains - 1:
                lead = (here, after(other, token), other_too, weight, borrowed)
                token = part = head_part(*lead, got_other)
            ready = [token] + (moved[i + 1 :] if step == 1 else [])
            own_part = after(local_part[i], *ready)
            token = add_own(moved[i], own_part)
            moved[i] = ring(token)
        if step < pairs - 2:
            local_part = piece(F32, step + 1, token)
            token = local_part[0]
    swapped = partner(part)
    input_grad = join(
        par, here, per, mine, mine_too, weight, borrowed, got_mine, swapped
    )
    last = [after(last[0], input_grad), *last[1:]]
    weight_grad = finish_weight(1.0 / math.sqrt(length * n_ctx), moved, last)
    return (query_grad, key_grad, input_grad, weight_grad)


def solution(mesh):
    spec = P("ctx", "head")
    return jax.shard_map(
        local, mesh=mesh, in_specs=(spec,) * 6, out_specs=(spec,) * 4, check_vma=False
    )
```

```python
import functools
import math

import jax
import jax.numpy as jnp
from jax import lax
from jax.experimental import pallas as pl
from jax.experimental.pallas import tpu as pltpu
from jax.sharding import PartitionSpec as P

DH = 128
F32, BF16 = jnp.float32, jnp.bfloat16
VMEM = pl.BlockSpec(memory_space=pltpu.VMEM)
SMEM = pl.BlockSpec(memory_space=pltpu.SMEM)
ANY = pl.BlockSpec(memory_space=pl.ANY)


def dot(a, b, ca, cb):
    return lax.dot_general(a, b, (((ca,), (cb,)), ((), ())), preferred_element_type=F32)


def call(kernel, vmem=16, flops=1, **kw):
    hint = pl.CostEstimate(flops=flops, bytes_accessed=1, transcendentals=0)
    params = pltpu.CompilerParams(vmem_limit_bytes=vmem * 2**20)
    return pl.pallas_call(kernel, cost_estimate=hint, compiler_params=params, **kw)


def states_kernel(par_ref, *refs):
    arrays, (keep_ref, send_ref), bufs, sems = refs[:4], refs[4:6], refs[6:10], refs[10]
    heads = arrays[0].shape[1] // DH
    half = heads // 2

    def copy(j, hd):
        at = pl.ds(hd * DH, DH)
        return pltpu.make_async_copy(
            arrays[j].at[:, at], bufs[j].at[:, at], sems.at[j, hd]
        )

    for hd in range(heads):
        for j in range(4):
            copy(j, hd).start()
    for hd in range(heads):
        at = slice(hd * DH, (hd + 1) * DH)
        for j in range(4):
            copy(j, hd).wait()
        for kind, (a, b) in enumerate(((0, 3), (1, 2))):
            s = dot(bufs[a][:, at], bufs[b][:, at], 0, 0)
            own = par_ref[0] == hd // half

            @pl.when(own)
            def _():
                keep_ref[kind, hd % half] = s

            @pl.when(own & (par_ref[0] != kind))
            def _():
                send_ref[2, hd % half] = s.astype(BF16)

            @pl.when(jnp.logical_not(own))
            def _():
                send_ref[kind, hd % half] = s.astype(BF16)


def states(par, *arrays):
    n, cols = arrays[0].shape
    heads = cols // DH
    shape = (2, heads // 2, DH, DH)
    return call(
        states_kernel,
        vmem=60,
        in_specs=[SMEM] + [pl.BlockSpec(memory_space=pltpu.HBM)] * 4,
        out_specs=[VMEM] * 2,
        out_shape=[
            jax.ShapeDtypeStruct(shape, F32),
            jax.ShapeDtypeStruct((3, *shape[1:]), BF16),
        ],
        scratch_shapes=[pltpu.VMEM((n, cols), BF16)] * 4
        + [pltpu.SemaphoreType.DMA((4, heads))],
        name="states",
    )(par, *arrays)


def split_kernel(per, par_ref, x_ref, own_ref, theirs_ref, sems):
    width = own_ref.shape[2]
    for k in range(2):

        @pl.when(par_ref[0] == k)
        def _():
            copies = []
            for i in range(per):
                for j, out_ref in enumerate((own_ref, theirs_ref)):
                    at = (2 * i + (k ^ j)) * width
                    if width % 128:
                        out_ref[i] = x_ref[:, at : at + width]
                    else:
                        src = x_ref.at[:, pl.ds(at, width)]
                        copies.append(
                            pltpu.make_async_copy(src, out_ref.at[i], sems.at[j, i])
                        )
            for c in copies:
                c.start()
            for c in copies:
                c.wait()


def split(par, x, per):
    width = x.shape[1] // (2 * per)
    out = jax.ShapeDtypeStruct((per, x.shape[0], width), x.dtype)
    place = VMEM if width % 128 else pl.BlockSpec(memory_space=pltpu.HBM)
    return call(
        functools.partial(split_kernel, per),
        in_specs=[SMEM, place],
        out_specs=[VMEM] * 2,
        out_shape=[out, out],
        scratch_shapes=[pltpu.SemaphoreType.DMA((2, per))],
        name="split",
    )(par, x)


def inside_kernel(*refs):
    arrays, (out_ref, k_ref), bufs, sems = refs[:3], refs[3:5], refs[5:8], refs[8]
    n, cols = out_ref.shape
    heads = cols // DH

    def copy(j, hd):
        at = pl.ds(hd * DH, DH)
        return pltpu.make_async_copy(
            arrays[j].at[:, at], bufs[j].at[:, at], sems.at[j, hd]
        )

    for hd in range(heads):
        for j in range(3):
            copy(j, hd).start()
    rows = lax.broadcasted_iota(jnp.int32, (n, n), 0)
    causal = rows >= lax.broadcasted_iota(jnp.int32, (n, n), 1)
    for hd in range(heads):
        at = slice(hd * DH, (hd + 1) * DH)
        for j in range(3):
            copy(j, hd).wait()
        q, k, g = (x[:, at] for x in bufs)
        scores = jnp.where(causal, dot(q, k, 1, 1), 0.0).astype(BF16)
        out_ref[:, at] = dot(scores, g, 0, 0)
        k_ref[:, at] = k


def inside(*arrays):
    n, cols = arrays[0].shape
    return call(
        inside_kernel,
        in_specs=[pl.BlockSpec(memory_space=pltpu.HBM)] * 3,
        out_specs=[VMEM] * 2,
        out_shape=[jax.ShapeDtypeStruct((n, cols), d) for d in (F32, BF16)],
        scratch_shapes=[pltpu.VMEM((n, cols), BF16)] * 3
        + [pltpu.SemaphoreType.DMA((3, cols // DH))],
        name="inside",
    )(*arrays)


def offer_kernel(pair_ref, keep_ref, got_ref, out_ref):
    sums = [(keep_ref[k] + got_ref[k].astype(F32)).astype(BF16) for k in range(2)]
    for p in range(out_ref.shape[0]):
        out_ref[p] = jnp.where(p < pair_ref[0], sums[0], sums[1])


def offer(pair, keep, got, pairs):
    return call(
        offer_kernel,
        in_specs=[SMEM, VMEM, VMEM],
        out_specs=VMEM,
        out_shape=jax.ShapeDtypeStruct((pairs, *keep.shape[1:]), BF16),
        name="offer",
    )(pair, keep, got)


def far_kernel(pair_ref, every_ref, out_ref, send_ref):
    for kind in range(2):
        total = jnp.zeros(out_ref.shape[1:], F32)
        for p in range(every_ref.shape[0]):
            reached = p > pair_ref[0] if kind == 0 else p < pair_ref[0]
            total = total + jnp.where(reached, every_ref[p].astype(F32), 0.0)
        out_ref[kind] = total
        send_ref[kind] = total.astype(BF16)


def far_states(pair, every):
    shape = (2, *every.shape[1:])
    return call(
        far_kernel,
        in_specs=[SMEM, VMEM],
        out_specs=[VMEM] * 2,
        out_shape=[jax.ShapeDtypeStruct(shape, d) for d in (F32, BF16)],
        name="far",
    )(pair, every)


def entering(par, kind, hd, half, far, got, near):
    mine = par == hd // half
    i = hd % half
    outer = jnp.where(mine, far[kind, i], got[kind, i].astype(F32))
    close = jnp.where(mine, near[kind, i], near[2, i]).astype(F32)
    total = outer + jnp.where(par == kind, close, 0.0)
    hi = total.astype(BF16)
    return hi, (total - hi.astype(F32)).astype(BF16)


def value_kernel(factor, half, par_ref, k_ref, vi_ref, *refs):
    ends, out_ref = refs[:-1], refs[-1]
    for hd in range(2 * half):
        at = slice(hd * DH, (hd + 1) * DH)
        hi, lo = entering(par_ref[0], 0, hd, half, *ends)
        k = k_ref[:, at]
        total = vi_ref[:, at] + (dot(k, hi, 1, 0) + dot(k, lo, 1, 0))
        out_ref[:, at] = (factor * total).astype(BF16)


def finish_value(factor, par, k, vi, ends):
    return call(
        functools.partial(value_kernel, factor, k.shape[1] // DH // 2),
        in_specs=[SMEM] + [VMEM] * (2 + len(ends)),
        out_specs=VMEM,
        out_shape=jax.ShapeDtypeStruct(k.shape, BF16),
        name="finish_value",
    )(par, k, vi, *ends)


def others_kernel(factor, half, par_ref, q_ref, k_ref, v_ref, g_ref, *refs):
    ends, (qo_ref, ko_ref) = refs[:-2], refs[-2:]
    hd = pl.program_id(0)
    q, k, v, g = q_ref[...], k_ref[...], v_ref[...], g_ref[...]
    n = q.shape[0]
    rows = lax.broadcasted_iota(jnp.int32, (n, n), 0)
    cols = lax.broadcasted_iota(jnp.int32, (n, n), 1)
    scores = jnp.where(rows >= cols, dot(g, v, 1, 1), 0.0).astype(BF16)
    hi, lo = entering(par_ref[0], 1, hd, half, *ends)
    total = dot(scores, k, 1, 0) + (dot(g, hi, 1, 1) + dot(g, lo, 1, 1))
    qo_ref[...] = (factor * total).astype(BF16)
    hi, lo = entering(par_ref[0], 0, hd, half, *ends)
    total = dot(scores, q, 0, 0) + (dot(v, hi, 1, 1) + dot(v, lo, 1, 1))
    ko_ref[...] = (factor * total).astype(BF16)


def others(factor, par, q, k, v, g, ends):
    n, cols = q.shape
    spec = pl.BlockSpec((n, DH), lambda h: (0, h))
    held = [pl.BlockSpec(x.shape, lambda h, d=x.ndim: (0,) * d) for x in ends]
    out = jax.ShapeDtypeStruct(q.shape, BF16)
    return call(
        functools.partial(others_kernel, factor, cols // DH // 2),
        grid=(cols // DH,),
        in_specs=[SMEM] + [spec] * 4 + held,
        out_specs=[spec] * 2,
        out_shape=[out] * 2,
        name="others",
    )(par, q, k, v, g, *ends)


def line_at(order, place):
    place = lax.rem(place + 2 * len(order), len(order))
    line = jnp.int32(order[0])
    for i, p in enumerate(order[1:], 1):
        line = jnp.where(place == i, p, line)
    return line


def piece_kernel(order, per, step, count, spot_ref, head_ref, a_ref, b_ref, *refs):
    own, theirs = refs[:count], refs[count : 2 * count]
    outs, (x, y, at, bt, sems) = refs[2 * count : -5], refs[-5:]
    line = line_at(order, spot_ref[0] - 1 - step)
    off, sub = lax.div(line, per) ^ head_ref[0], lax.rem(line, per)

    for i in range(count):

        @pl.when(off == i)
        def _():
            for j, (src, dst) in enumerate(((own, x), (theirs, y))):
                pltpu.make_async_copy(src[i].at[sub], dst, sems.at[j]).start()

    at[...] = a_ref[...].T
    bt[...] = b_ref[...].T
    for j, (src, dst) in enumerate(((own, x), (theirs, y))):
        pltpu.make_async_copy(src[0].at[0], dst, sems.at[j]).wait()
    total = dot(at[...], x[...], 1, 0) + dot(bt[...], y[...], 1, 0)
    span = outs[0].shape[0]
    for i, out_ref in enumerate(outs):
        out_ref[...] = total[i * span : (i + 1) * span].astype(out_ref.dtype)


def pieces(dtype, chains, flops, order, per, step, spot, head, a, b, own, theirs):
    count = len(own)
    _, n, width = own[0].shape
    cols = a.shape[1]
    return call(
        functools.partial(piece_kernel, order, per, step, count),
        flops=flops,
        in_specs=[SMEM] * 2 + [VMEM] * 2 + [ANY] * (2 * count),
        out_specs=[VMEM] * chains,
        out_shape=[jax.ShapeDtypeStruct((cols // chains, width), dtype)] * chains,
        scratch_shapes=[pltpu.VMEM((n, width), BF16)] * 2
        + [pltpu.VMEM((cols, n), BF16)] * 2
        + [pltpu.SemaphoreType.DMA((2,))],
        name="pieces",
    )(spot, head, a, b, *own, *theirs)


def weight_kernel(scale, *refs):
    count, out_ref = len(refs) // 2, refs[-1]
    span = refs[0].shape[0]
    for i in range(count):
        total = refs[i][...].astype(F32) + refs[count + i][...]
        out_ref[:, i * span : (i + 1) * span] = total.T * scale


def finish_weight(scale, moved, own):
    span, width = moved[0].shape
    count = len(moved)
    return call(
        functools.partial(weight_kernel, scale),
        in_specs=[VMEM] * (2 * count),
        out_specs=VMEM,
        out_shape=jax.ShapeDtypeStruct((width, span * count), F32),
        name="finish_weight",
    )(*moved, *own)


def add_kernel(moved_ref, own_ref, out_ref):
    out_ref[...] = (moved_ref[...].astype(F32) + own_ref[...]).astype(BF16)


def add_own(moved, own):
    return call(
        add_kernel,
        in_specs=[VMEM] * 2,
        out_specs=VMEM,
        out_shape=jax.ShapeDtypeStruct(moved.shape, BF16),
        name="add_own",
    )(moved, own)


def arrange_kernel(order, per, head_ref, spot_ref, *refs):
    count = len(order)
    outs, sems = refs[-3:-1], refs[-1]
    rows = refs[0].shape[0]

    def copies(s):
        p = line_at(order, spot_ref[0] - s)
        head, sub = lax.div(p, per), lax.rem(p, per)
        at = (lax.div(head, 2), pl.ds(sub * rows, rows))
        pair = [
            pltpu.make_async_copy(refs[j * count + s], outs[j].at[at], sems.at[j, s])
            for j in range(2)
        ]
        return pair, lax.rem(head, 2) == lax.rem(head_ref[0], 2)

    for act in ("start", "wait"):
        for s in range(count):
            pair, needed = copies(s)

            @pl.when(needed)
            def _():
                for c in pair:
                    getattr(c, act)()


def arrange(order, per, n_head, head, spot, blocks, lent):
    rows, cols = blocks[0].shape
    count = len(blocks)
    out = jax.ShapeDtypeStruct((n_head // 2, per * rows, cols), BF16)
    return call(
        functools.partial(arrange_kernel, order, per),
        in_specs=[SMEM] * 2 + [ANY] * (2 * count),
        out_specs=[VMEM] * 2,
        out_shape=[out] * 2,
        scratch_shapes=[pltpu.SemaphoreType.DMA((2, count))],
        name="arrange",
    )(head, spot, *blocks, *lent)


def block_product(at_ref, x_ref, y_ref, w_ref, wy_ref):
    at = at_ref[0] // 2
    return dot(x_ref[...], w_ref[at], 1, 1) + dot(y_ref[...], wy_ref[at], 1, 1)


def part_kernel(at_ref, x_ref, y_ref, w_ref, wy_ref, *refs):
    total = block_product(at_ref, x_ref, y_ref, w_ref, wy_ref)
    for got in refs[:-1]:
        total = total + got[...].astype(F32)
    refs[-1][...] = total.astype(BF16)


def head_part(at, x, y, w, wy, got=()):
    return call(
        part_kernel,
        in_specs=[SMEM] + [VMEM] * (4 + len(got)),
        out_specs=VMEM,
        out_shape=jax.ShapeDtypeStruct((x.shape[0], w.shape[1]), BF16),
        name="head_part",
    )(at, x, y, w, wy, *got)


def join_kernel(per, par_ref, at_ref, x_ref, y_ref, w_ref, wy_ref, *refs):
    total = block_product(at_ref, x_ref, y_ref, w_ref, wy_ref)
    for got in refs[:-2]:
        total = total + got[...].astype(F32)
    other_ref, out_ref = refs[-2:]
    rows = other_ref.shape[1] // per
    both = (total.astype(BF16), other_ref[...])
    for k in range(2):

        @pl.when(par_ref[0] == k)
        def _():
            for i in range(per):
                at = slice(i * rows, (i + 1) * rows)
                for j in range(2):
                    to = (2 * i + j) * rows
                    out_ref[:, to : to + rows] = both[j ^ k][:, at]


def join(par, at, per, x, y, w, wy, got, other):
    return call(
        functools.partial(join_kernel, per),
        in_specs=[SMEM] * 2 + [VMEM] * (5 + len(got)),
        out_specs=VMEM,
        out_shape=jax.ShapeDtypeStruct((x.shape[0], 2 * other.shape[1]), BF16),
        name="join",
    )(par, at, x, y, w, wy, *got, other)


def after(x, *earlier):
    return lax.optimization_barrier((x, *earlier))[0]


def local(queries, keys, values, out_grad, inputs, value_weight):
    length, cols = queries.shape
    n_ctx, n_head = lax.axis_size("ctx"), lax.axis_size("head")
    pairs = n_ctx // 2
    ctx, head = lax.axis_index("ctx"), lax.axis_index("head")
    parity, pair = ctx % 2, ctx // 2
    par = parity.astype(jnp.int32).reshape(1)
    factor = 1.0 / math.sqrt(DH * length * n_ctx)
    lines = [[2 * i + k for i in range(pairs)] for k in range(2)]
    def partner(x):
        return lax.ppermute(x, "ctx", [(i, i ^ 1) for i in range(n_ctx)])

    def across(x, bit):
        return lax.ppermute(x, "head", [(i, i ^ bit) for i in range(n_head)])

    order = list(range(0, pairs, 2)) + list(range(1, pairs, 2))[::-1]
    place = [order.index(i) for i in range(pairs)]
    moves = [
        (2 * order[i] + k, 2 * order[(i + 1) % pairs] + k)
        for i in range(pairs)
        for k in range(2)
    ]
    here = head.astype(jnp.int32).reshape(1)
    spot = line_at(place, pair.astype(jnp.int32)).reshape(1)

    def ring(x):
        return lax.ppermute(x, "ctx", moves)

    def back(x):
        return lax.ppermute(x, "ctx", [(b, a) for a, b in moves])

    keep, send = states(par, queries, keys, values, out_grad)
    near = partner(send)
    line = pair.astype(jnp.int32).reshape(1)

    per = n_ctx // n_head // 2
    width = value_weight.shape[0]
    own, theirs = split(after(par, send), inputs, per)
    blocks = [value_weight, ring(after(value_weight, send))]
    own, theirs = [own], [partner(after(theirs, near))]

    offered = offer(line, keep, near, pairs)
    every = lax.all_to_all(
        offered, "ctx", split_axis=0, concat_axis=0, axis_index_groups=lines
    )
    far, send_far = far_states(line, after(every, blocks[1]))
    ends = (far, partner(send_far), near)
    vi, keys_too = inside(after(queries, send_far), keys, out_grad)
    theirs = [after(theirs[0], send_far)]
    mine = finish_value(factor, par, keys_too, vi, ends)
    other = partner(mine)
    query_grad, key_grad = others(
        factor, par, queries, keys, after(values, mine), out_grad, ends
    )
    token = send_far
    for _ in range(2, pairs // 2 + 1):
        blocks.append(ring(after(blocks[-1], token)))
        token = mine
    ahead = [value_weight]
    for _ in range(pairs // 2 + 1, pairs):
        ahead.append(back(after(ahead[-1], mine)))
    blocks = blocks + ahead[:0:-1]
    early = pairs // 2
    lent = [across(after(x, mine), 1) for x in blocks[:early]]
    mine_too = across(mine, 1)

    offsets = [0]
    bit = n_head // 2
    while bit:
        own = own + [across(after(r, mine) if len(own) > 1 else r, bit) for r in own]
        last = len(theirs) > 1
        theirs = theirs + [
            across(after(r, blocks[2]) if last and i else r, bit)
            for i, r in enumerate(theirs)
        ]
        offsets = offsets + [o ^ bit for o in offsets]
        bit //= 2
    own = [own[offsets.index(i)] for i in range(n_head)]
    theirs = [theirs[offsets.index(i)] for i in range(n_head)]


    chains = 2

    def piece(dtype, step, token, flops=1):
        vals = (spot, here, after(mine, token), other, own, theirs)
        return pieces(dtype, chains, flops, order, per, step, *vals)

    token = after(query_grad, blocks[-1])
    total = piece(BF16, 0, token, 4 * length * cols * width)
    moved = [ring(x) for x in total]
    other_too = across(other, 1)
    lent = lent + [across(after(x, total[0]), 1) for x in blocks[early:]]
    local_part = piece(F32, 1, total[0])


    def summed_parts(x, y):
        sent = [
            head_part(here ^ off, x, y, weight, borrowed)
            for off in range(2, n_head, 2)
        ]
        return sent[-1], [across(x, 2 * i + 2) for i, x in enumerate(sent)]

    held = [after(blocks[0], local_part[0])] + blocks[1:]
    weight, borrowed = arrange(order, per, n_head, here, spot, held, lent)
    token, got_other = summed_parts(other, other_too)
    token, got_mine = summed_parts(after(mine, token), mine_too)
    part = None
    for step in range(1, pairs - 1):
        if step == pairs - 2:
            last = piece(F32, pairs - 1, token)
            token = last[0]
        for i in range(chains):
            if step == pairs - 2 and i == chains - 1:
                lead = (here, after(other, token), other_too, weight, borrowed)
                token = part = head_part(*lead, got_other)
            token = add_own(moved[i], after(local_part[i], token))
            moved[i] = ring(token)
        if step < pairs - 2:
            local_part = piece(F32, step + 1, token)
            token = local_part[0]
    swapped = partner(part)
    input_grad = join(
        par, here, per, mine, mine_too, weight, borrowed, got_mine, swapped
    )
    last = [after(last[0], input_grad), *last[1:]]
    weight_grad = finish_weight(1.0 / math.sqrt(length * n_ctx), moved, last)
    return (query_grad, key_grad, input_grad, weight_grad)


def solution(mesh):
    spec = P("ctx", "head")
    return jax.shard_map(
        local, mesh=mesh, in_specs=(spec,) * 6, out_specs=(spec,) * 4, check_vma=False
    )
```

```python
import functools
import math

import jax
import jax.numpy as jnp
from jax import lax
from jax.experimental import pallas as pl
from jax.experimental.pallas import tpu as pltpu
from jax.sharding import PartitionSpec as P

DH = 128
F32, BF16 = jnp.float32, jnp.bfloat16
VMEM = pl.BlockSpec(memory_space=pltpu.VMEM)
SMEM = pl.BlockSpec(memory_space=pltpu.SMEM)
ANY = pl.BlockSpec(memory_space=pl.ANY)


def dot(a, b, ca, cb):
    return lax.dot_general(a, b, (((ca,), (cb,)), ((), ())), preferred_element_type=F32)


def call(kernel, vmem=16, flops=1, **kw):
    hint = pl.CostEstimate(flops=flops, bytes_accessed=1, transcendentals=0)
    params = pltpu.CompilerParams(vmem_limit_bytes=vmem * 2**20)
    return pl.pallas_call(kernel, cost_estimate=hint, compiler_params=params, **kw)


def states_kernel(par_ref, *refs):
    arrays, (keep_ref, send_ref), bufs, sems = refs[:4], refs[4:6], refs[6:10], refs[10]
    heads = arrays[0].shape[1] // DH
    half = heads // 2

    def copy(j, hd):
        at = pl.ds(hd * DH, DH)
        return pltpu.make_async_copy(
            arrays[j].at[:, at], bufs[j].at[:, at], sems.at[j, hd]
        )

    for hd in range(heads):
        for j in range(4):
            copy(j, hd).start()
    for hd in range(heads):
        at = slice(hd * DH, (hd + 1) * DH)
        for j in range(4):
            copy(j, hd).wait()
        for kind, (a, b) in enumerate(((0, 3), (1, 2))):
            s = dot(bufs[a][:, at], bufs[b][:, at], 0, 0)
            own = par_ref[0] == hd // half

            @pl.when(own)
            def _():
                keep_ref[kind, hd % half] = s

            @pl.when(own & (par_ref[0] != kind))
            def _():
                send_ref[2, hd % half] = s.astype(BF16)

            @pl.when(jnp.logical_not(own))
            def _():
                send_ref[kind, hd % half] = s.astype(BF16)


def states(par, *arrays):
    n, cols = arrays[0].shape
    heads = cols // DH
    shape = (2, heads // 2, DH, DH)
    return call(
        states_kernel,
        vmem=60,
        in_specs=[SMEM] + [pl.BlockSpec(memory_space=pltpu.HBM)] * 4,
        out_specs=[VMEM] * 2,
        out_shape=[
            jax.ShapeDtypeStruct(shape, F32),
            jax.ShapeDtypeStruct((3, *shape[1:]), BF16),
        ],
        scratch_shapes=[pltpu.VMEM((n, cols), BF16)] * 4
        + [pltpu.SemaphoreType.DMA((4, heads))],
        name="states",
    )(par, *arrays)


def split_kernel(per, par_ref, x_ref, own_ref, theirs_ref, sems):
    width = own_ref.shape[2]
    for k in range(2):

        @pl.when(par_ref[0] == k)
        def _():
            copies = []
            for i in range(per):
                for j, out_ref in enumerate((own_ref, theirs_ref)):
                    at = (2 * i + (k ^ j)) * width
                    if width % 128:
                        out_ref[i] = x_ref[:, at : at + width]
                    else:
                        src = x_ref.at[:, pl.ds(at, width)]
                        copies.append(
                            pltpu.make_async_copy(src, out_ref.at[i], sems.at[j, i])
                        )
            for c in copies:
                c.start()
            for c in copies:
                c.wait()


def split(par, x, per):
    width = x.shape[1] // (2 * per)
    out = jax.ShapeDtypeStruct((per, x.shape[0], width), x.dtype)
    place = VMEM if width % 128 else pl.BlockSpec(memory_space=pltpu.HBM)
    return call(
        functools.partial(split_kernel, per),
        in_specs=[SMEM, place],
        out_specs=[VMEM] * 2,
        out_shape=[out, out],
        scratch_shapes=[pltpu.SemaphoreType.DMA((2, per))],
        name="split",
    )(par, x)


def inside_kernel(*refs):
    arrays, (out_ref, k_ref), bufs, sems = refs[:3], refs[3:5], refs[5:8], refs[8]
    n, cols = out_ref.shape
    heads = cols // DH

    def copy(j, hd):
        at = pl.ds(hd * DH, DH)
        return pltpu.make_async_copy(
            arrays[j].at[:, at], bufs[j].at[:, at], sems.at[j, hd]
        )

    for hd in range(heads):
        for j in range(3):
            copy(j, hd).start()
    rows = lax.broadcasted_iota(jnp.int32, (n, n), 0)
    causal = rows >= lax.broadcasted_iota(jnp.int32, (n, n), 1)
    for hd in range(heads):
        at = slice(hd * DH, (hd + 1) * DH)
        for j in range(3):
            copy(j, hd).wait()
        q, k, g = (x[:, at] for x in bufs)
        scores = jnp.where(causal, dot(q, k, 1, 1), 0.0).astype(BF16)
        out_ref[:, at] = dot(scores, g, 0, 0)
        k_ref[:, at] = k


def inside(*arrays):
    n, cols = arrays[0].shape
    return call(
        inside_kernel,
        in_specs=[pl.BlockSpec(memory_space=pltpu.HBM)] * 3,
        out_specs=[VMEM] * 2,
        out_shape=[jax.ShapeDtypeStruct((n, cols), d) for d in (F32, BF16)],
        scratch_shapes=[pltpu.VMEM((n, cols), BF16)] * 3
        + [pltpu.SemaphoreType.DMA((3, cols // DH))],
        name="inside",
    )(*arrays)


def offer_kernel(pair_ref, keep_ref, got_ref, out_ref):
    sums = [(keep_ref[k] + got_ref[k].astype(F32)).astype(BF16) for k in range(2)]
    for p in range(out_ref.shape[0]):
        out_ref[p] = jnp.where(p < pair_ref[0], sums[0], sums[1])


def offer(pair, keep, got, pairs):
    return call(
        offer_kernel,
        in_specs=[SMEM, VMEM, VMEM],
        out_specs=VMEM,
        out_shape=jax.ShapeDtypeStruct((pairs, *keep.shape[1:]), BF16),
        name="offer",
    )(pair, keep, got)


def far_kernel(pair_ref, every_ref, out_ref, send_ref):
    for kind in range(2):
        total = jnp.zeros(out_ref.shape[1:], F32)
        for p in range(every_ref.shape[0]):
            reached = p > pair_ref[0] if kind == 0 else p < pair_ref[0]
            total = total + jnp.where(reached, every_ref[p].astype(F32), 0.0)
        out_ref[kind] = total
        send_ref[kind] = total.astype(BF16)


def far_states(pair, every):
    shape = (2, *every.shape[1:])
    return call(
        far_kernel,
        in_specs=[SMEM, VMEM],
        out_specs=[VMEM] * 2,
        out_shape=[jax.ShapeDtypeStruct(shape, d) for d in (F32, BF16)],
        name="far",
    )(pair, every)


def entering(par, kind, hd, half, far, got, near):
    mine = par == hd // half
    i = hd % half
    outer = jnp.where(mine, far[kind, i], got[kind, i].astype(F32))
    close = jnp.where(mine, near[kind, i], near[2, i]).astype(F32)
    total = outer + jnp.where(par == kind, close, 0.0)
    hi = total.astype(BF16)
    return hi, (total - hi.astype(F32)).astype(BF16)


def value_kernel(factor, half, par_ref, k_ref, vi_ref, *refs):
    ends, out_ref = refs[:-1], refs[-1]
    for hd in range(2 * half):
        at = slice(hd * DH, (hd + 1) * DH)
        hi, lo = entering(par_ref[0], 0, hd, half, *ends)
        k = k_ref[:, at]
        total = vi_ref[:, at] + (dot(k, hi, 1, 0) + dot(k, lo, 1, 0))
        out_ref[:, at] = (factor * total).astype(BF16)


def finish_value(factor, par, k, vi, ends):
    return call(
        functools.partial(value_kernel, factor, k.shape[1] // DH // 2),
        in_specs=[SMEM] + [VMEM] * (2 + len(ends)),
        out_specs=VMEM,
        out_shape=jax.ShapeDtypeStruct(k.shape, BF16),
        name="finish_value",
    )(par, k, vi, *ends)


def others_kernel(factor, half, par_ref, q_ref, k_ref, v_ref, g_ref, *refs):
    ends, (qo_ref, ko_ref) = refs[:-2], refs[-2:]
    hd = pl.program_id(0)
    q, k, v, g = q_ref[...], k_ref[...], v_ref[...], g_ref[...]
    n = q.shape[0]
    rows = lax.broadcasted_iota(jnp.int32, (n, n), 0)
    cols = lax.broadcasted_iota(jnp.int32, (n, n), 1)
    scores = jnp.where(rows >= cols, dot(g, v, 1, 1), 0.0).astype(BF16)
    hi, lo = entering(par_ref[0], 1, hd, half, *ends)
    total = dot(scores, k, 1, 0) + (dot(g, hi, 1, 1) + dot(g, lo, 1, 1))
    qo_ref[...] = (factor * total).astype(BF16)
    hi, lo = entering(par_ref[0], 0, hd, half, *ends)
    total = dot(scores, q, 0, 0) + (dot(v, hi, 1, 1) + dot(v, lo, 1, 1))
    ko_ref[...] = (factor * total).astype(BF16)


def others(factor, par, q, k, v, g, ends):
    n, cols = q.shape
    spec = pl.BlockSpec((n, DH), lambda h: (0, h))
    held = [pl.BlockSpec(x.shape, lambda h, d=x.ndim: (0,) * d) for x in ends]
    out = jax.ShapeDtypeStruct(q.shape, BF16)
    return call(
        functools.partial(others_kernel, factor, cols // DH // 2),
        grid=(cols // DH,),
        in_specs=[SMEM] + [spec] * 4 + held,
        out_specs=[spec] * 2,
        out_shape=[out] * 2,
        name="others",
    )(par, q, k, v, g, *ends)


def line_at(order, place):
    place = lax.rem(place + 2 * len(order), len(order))
    line = jnp.int32(order[0])
    for i, p in enumerate(order[1:], 1):
        line = jnp.where(place == i, p, line)
    return line


def piece_kernel(order, per, step, count, spot_ref, head_ref, a_ref, b_ref, *refs):
    own, theirs = refs[:count], refs[count : 2 * count]
    outs, (x, y, at, bt, sems) = refs[2 * count : -5], refs[-5:]
    line = line_at(order, spot_ref[0] - 1 - step)
    off, sub = lax.div(line, per) ^ head_ref[0], lax.rem(line, per)

    for i in range(count):

        @pl.when(off == i)
        def _():
            for j, (src, dst) in enumerate(((own, x), (theirs, y))):
                pltpu.make_async_copy(src[i].at[sub], dst, sems.at[j]).start()

    at[...] = a_ref[...].T
    bt[...] = b_ref[...].T
    for j, (src, dst) in enumerate(((own, x), (theirs, y))):
        pltpu.make_async_copy(src[0].at[0], dst, sems.at[j]).wait()
    total = dot(at[...], x[...], 1, 0) + dot(bt[...], y[...], 1, 0)
    span = outs[0].shape[0]
    for i, out_ref in enumerate(outs):
        out_ref[...] = total[i * span : (i + 1) * span].astype(out_ref.dtype)


def pieces(dtype, chains, flops, order, per, step, spot, head, a, b, own, theirs):
    count = len(own)
    _, n, width = own[0].shape
    cols = a.shape[1]
    return call(
        functools.partial(piece_kernel, order, per, step, count),
        flops=flops,
        in_specs=[SMEM] * 2 + [VMEM] * 2 + [ANY] * (2 * count),
        out_specs=[VMEM] * chains,
        out_shape=[jax.ShapeDtypeStruct((cols // chains, width), dtype)] * chains,
        scratch_shapes=[pltpu.VMEM((n, width), BF16)] * 2
        + [pltpu.VMEM((cols, n), BF16)] * 2
        + [pltpu.SemaphoreType.DMA((2,))],
        name="pieces",
    )(spot, head, a, b, *own, *theirs)


def weight_kernel(scale, *refs):
    count, out_ref = len(refs) // 2, refs[-1]
    span = refs[0].shape[0]
    for i in range(count):
        total = refs[i][...].astype(F32) + refs[count + i][...]
        out_ref[:, i * span : (i + 1) * span] = total.T * scale


def finish_weight(scale, moved, own):
    span, width = moved[0].shape
    count = len(moved)
    return call(
        functools.partial(weight_kernel, scale),
        in_specs=[VMEM] * (2 * count),
        out_specs=VMEM,
        out_shape=jax.ShapeDtypeStruct((width, span * count), F32),
        name="finish_weight",
    )(*moved, *own)


def add_kernel(moved_ref, own_ref, out_ref):
    out_ref[...] = (moved_ref[...].astype(F32) + own_ref[...]).astype(BF16)


def add_own(moved, own):
    return call(
        add_kernel,
        in_specs=[VMEM] * 2,
        out_specs=VMEM,
        out_shape=jax.ShapeDtypeStruct(moved.shape, BF16),
        name="add_own",
    )(moved, own)


def arrange_kernel(order, per, head_ref, spot_ref, *refs):
    count = len(order)
    outs, sems = refs[-3:-1], refs[-1]
    rows = refs[0].shape[0]

    def copies(s):
        p = line_at(order, spot_ref[0] - s)
        head, sub = lax.div(p, per), lax.rem(p, per)
        at = (lax.div(head, 2), pl.ds(sub * rows, rows))
        pair = [
            pltpu.make_async_copy(refs[j * count + s], outs[j].at[at], sems.at[j, s])
            for j in range(2)
        ]
        return pair, lax.rem(head, 2) == lax.rem(head_ref[0], 2)

    for act in ("start", "wait"):
        for s in range(count):
            pair, needed = copies(s)

            @pl.when(needed)
            def _():
                for c in pair:
                    getattr(c, act)()


def arrange(order, per, n_head, head, spot, blocks, lent):
    rows, cols = blocks[0].shape
    count = len(blocks)
    out = jax.ShapeDtypeStruct((n_head // 2, per * rows, cols), BF16)
    return call(
        functools.partial(arrange_kernel, order, per),
        in_specs=[SMEM] * 2 + [ANY] * (2 * count),
        out_specs=[VMEM] * 2,
        out_shape=[out] * 2,
        scratch_shapes=[pltpu.SemaphoreType.DMA((2, count))],
        name="arrange",
    )(head, spot, *blocks, *lent)


def block_product(at_ref, x_ref, y_ref, w_ref, wy_ref):
    at = at_ref[0] // 2
    return dot(x_ref[...], w_ref[at], 1, 1) + dot(y_ref[...], wy_ref[at], 1, 1)


def part_kernel(at_ref, x_ref, y_ref, w_ref, wy_ref, *refs):
    total = block_product(at_ref, x_ref, y_ref, w_ref, wy_ref)
    for got in refs[:-1]:
        total = total + got[...].astype(F32)
    refs[-1][...] = total.astype(BF16)


def head_part(at, x, y, w, wy, got=()):
    return call(
        part_kernel,
        in_specs=[SMEM] + [VMEM] * (4 + len(got)),
        out_specs=VMEM,
        out_shape=jax.ShapeDtypeStruct((x.shape[0], w.shape[1]), BF16),
        name="head_part",
    )(at, x, y, w, wy, *got)


def join_kernel(per, par_ref, at_ref, x_ref, y_ref, w_ref, wy_ref, *refs):
    total = block_product(at_ref, x_ref, y_ref, w_ref, wy_ref)
    for got in refs[:-2]:
        total = total + got[...].astype(F32)
    other_ref, out_ref = refs[-2:]
    rows = other_ref.shape[1] // per
    both = (total.astype(BF16), other_ref[...])
    for k in range(2):

        @pl.when(par_ref[0] == k)
        def _():
            for i in range(per):
                at = slice(i * rows, (i + 1) * rows)
                for j in range(2):
                    to = (2 * i + j) * rows
                    out_ref[:, to : to + rows] = both[j ^ k][:, at]


def join(par, at, per, x, y, w, wy, got, other):
    return call(
        functools.partial(join_kernel, per),
        in_specs=[SMEM] * 2 + [VMEM] * (5 + len(got)),
        out_specs=VMEM,
        out_shape=jax.ShapeDtypeStruct((x.shape[0], 2 * other.shape[1]), BF16),
        name="join",
    )(par, at, x, y, w, wy, *got, other)


def after(x, *earlier):
    return lax.optimization_barrier((x, *earlier))[0]


def local(queries, keys, values, out_grad, inputs, value_weight):
    length, cols = queries.shape
    n_ctx, n_head = lax.axis_size("ctx"), lax.axis_size("head")
    pairs = n_ctx // 2
    ctx, head = lax.axis_index("ctx"), lax.axis_index("head")
    parity, pair = ctx % 2, ctx // 2
    par = parity.astype(jnp.int32).reshape(1)
    factor = 1.0 / math.sqrt(DH * length * n_ctx)
    lines = [[2 * i + k for i in range(pairs)] for k in range(2)]
    def partner(x):
        return lax.ppermute(x, "ctx", [(i, i ^ 1) for i in range(n_ctx)])

    def across(x, bit):
        return lax.ppermute(x, "head", [(i, i ^ bit) for i in range(n_head)])

    order = list(range(0, pairs, 2)) + list(range(1, pairs, 2))[::-1]
    place = [order.index(i) for i in range(pairs)]
    moves = [
        (2 * order[i] + k, 2 * order[(i + 1) % pairs] + k)
        for i in range(pairs)
        for k in range(2)
    ]
    here = head.astype(jnp.int32).reshape(1)
    spot = line_at(place, pair.astype(jnp.int32)).reshape(1)

    def ring(x):
        return lax.ppermute(x, "ctx", moves)

    def back(x):
        return lax.ppermute(x, "ctx", [(b, a) for a, b in moves])

    keep, send = states(par, queries, keys, values, out_grad)
    near = partner(send)
    line = pair.astype(jnp.int32).reshape(1)

    per = n_ctx // n_head // 2
    width = value_weight.shape[0]
    own, theirs = split(after(par, send), inputs, per)
    blocks = [value_weight, ring(after(value_weight, send))]
    own, theirs = [own], [partner(after(theirs, near))]

    offered = offer(line, keep, near, pairs)
    every = lax.all_to_all(
        offered, "ctx", split_axis=0, concat_axis=0, axis_index_groups=lines
    )
    far, send_far = far_states(line, after(every, blocks[1]))
    ends = (far, partner(send_far), near)
    vi, keys_too = inside(after(queries, send_far), keys, out_grad)
    theirs = [after(theirs[0], send_far)]
    mine = finish_value(factor, par, keys_too, vi, ends)
    other = partner(mine)
    query_grad, key_grad = others(
        factor, par, queries, keys, after(values, mine), out_grad, ends
    )
    token = send_far
    for _ in range(2, pairs // 2 + 1):
        blocks.append(ring(after(blocks[-1], token)))
        token = mine
    ahead = [value_weight]
    for _ in range(pairs // 2 + 1, pairs):
        ahead.append(back(after(ahead[-1], mine)))
    blocks = blocks + ahead[:0:-1]
    early = pairs // 2
    lent = [across(after(x, mine), 1) for x in blocks[:early]]
    mine_too = across(mine, 1)

    offsets = [0]
    bit = n_head // 2
    while bit:
        own = own + [across(after(r, mine) if len(own) > 1 else r, bit) for r in own]
        last = len(theirs) > 1
        theirs = theirs + [
            across(after(r, blocks[2]) if last and i else r, bit)
            for i, r in enumerate(theirs)
        ]
        offsets = offsets + [o ^ bit for o in offsets]
        bit //= 2
    own = [own[offsets.index(i)] for i in range(n_head)]
    theirs = [theirs[offsets.index(i)] for i in range(n_head)]


    chains = 2

    def piece(dtype, step, token, flops=1):
        vals = (spot, here, after(mine, token), other, own, theirs)
        return pieces(dtype, chains, flops, order, per, step, *vals)

    token = after(query_grad, blocks[-1])
    total = piece(BF16, 0, token, 4 * length * cols * width)
    moved = [ring(x) for x in total]
    other_too = across(other, 1)
    lent = lent + [across(after(x, total[0]), 1) for x in blocks[early:]]
    local_part = piece(F32, 1, lent[-1])


    def summed_parts(x, y):
        sent = [
            head_part(here ^ off, x, y, weight, borrowed)
            for off in range(2, n_head, 2)
        ]
        return sent[-1], [across(x, 2 * i + 2) for i, x in enumerate(sent)]

    held = [after(blocks[0], local_part[0])] + blocks[1:]
    weight, borrowed = arrange(order, per, n_head, here, spot, held, lent)
    token, got_other = summed_parts(other, other_too)
    token, got_mine = summed_parts(after(mine, token), mine_too)
    part = None
    for step in range(1, pairs - 1):
        if step == pairs - 2:
            last = piece(F32, pairs - 1, token)
            token = last[0]
        for i in range(chains):
            if step == pairs - 2 and i == chains - 1:
                lead = (here, after(other, token), other_too, weight, borrowed)
                token = part = head_part(*lead, got_other)
            token = add_own(moved[i], after(local_part[i], token))
            moved[i] = ring(token)
        if step < pairs - 2:
            local_part = piece(F32, step + 1, token)
            token = local_part[0]
    swapped = partner(part)
    weight_grad = finish_weight(1.0 / math.sqrt(length * n_ctx), moved, last)
    mine = after(mine, weight_grad)
    input_grad = join(
        par, here, per, mine, mine_too, weight, borrowed, got_mine, swapped
    )
    return (query_grad, key_grad, input_grad, weight_grad)


def solution(mesh):
    spec = P("ctx", "head")
    return jax.shard_map(
        local, mesh=mesh, in_specs=(spec,) * 6, out_specs=(spec,) * 4, check_vma=False
    )
```
